768 devices in a mesh: dp: 24 (over z, core), group: 32 (over x, y).
Axes of the slice: x: 4, y: 8, z: 12, core: 2. Of those that a mesh axis runs over, the one named last changes fastest.
Arguments:
- query_layer_input: bfloat16 [49152, 4096], P(('dp', 'group')), may hold values from -6 to 6
- query_frozen_base: bfloat16 [49152, 4096], P(('dp', 'group')), may hold values from -6 to 6
- passage_layer_input: bfloat16 [49152, 4096], P(('dp', 'group')), may hold values from -6 to 6
- passage_frozen_base: bfloat16 [49152, 4096], P(('dp', 'group')), may hold values from -6 to 6
- adapter_down_weight: bfloat16 [4096, 64], replicated, may hold values from -0.09375 to 0.09375
- adapter_up_weight: bfloat16 [64, 4096], replicated, may hold values from -0.75 to 0.75
- positive_passage_index: int32 [49152], P(('dp', 'group')), may hold values from 0 to 63
- hard_negative_slots: int32 [49152, 32], P(('dp', 'group')), may hold values from 0 to 255
- group_peer_rows: int32 [18432, 8], P(('dp', 'group')), may hold values from 0 to 63
- remote_group_rows: int32 [24576, 2], P(('dp', 'group')), may hold values from 0 to 63
Outputs:
- lora_down_grad: float32 [4096, 64], replicated
- lora_up_grad: float32 [64, 4096], replicated
- loss: float32 [], replicated
The draws below stay inside these ranges and needn't reach their ends.
All inputs are finite; a program needn't handle non-finite values.
Results may differ from the reference program's by a relative error of at most 0.008.
Values may be sent and summed in bfloat16 or wider, within the bound.
No kernel may reach another device: no remote copies, remote signals or barrier semaphores. Data moves between devices by JAX's collectives and lax.ppermute only.
A program may use at most 32 MiB of HBM per device.

```python
import math
import jax
import jax.numpy as jnp
import numpy as np
from jax import lax

MODEL_WIDTH = 4096
ADAPTER_RANK = 64
Q_DEV = 64
DEVICE_PASSAGES = 64
HARD = 32
C_NEAR = 8
C_FAR = 2
SLOTS = 256
QUERIES = 49152
PASSAGES = 49152
N_DP = 24
N_GROUP = 32


def plant(entries, own_key, smallest, top_value):
    place = [jax.random.randint(jax.random.fold_in(own_key, axis), (), 0, length) for axis, length in enumerate(entries.shape)]
    widest = entries.shape.index(max(entries.shape))
    next_to = place[:widest] + [(place[widest] + 1) % entries.shape[widest]] + place[widest + 1:]
    return entries.at[tuple(place)].set(smallest).at[tuple(next_to)].set(top_value)


def block_scale(own_key, shape, split, smallest, top_value):
    factor_of, own = 1.0, jax.random.fold_in(own_key, 6)
    for dim, blocks in split:
        steps = jnp.exp(jax.random.uniform(jax.random.fold_in(own, dim), (blocks,), jnp.float32, smallest / len(split), top_value / len(split)))
        factor_of = factor_of * jnp.repeat(steps, shape[dim] // blocks).reshape([-1 if axis == dim else 1 for axis in range(len(shape))])
    return factor_of


def rank_bounds(amount, skew):
    weights = [(1 << 20) // math.isqrt(standing ** skew) + 1 for standing in range(1, amount + 1)]
    deviation = 1 + sum(weights) // (1 << 30)
    return np.cumsum(np.array([max(1, weight // deviation) for weight in weights]))


def ranked_ids(own_key, shape, number_of, slope):
    grid = rank_bounds(number_of, slope)
    pick = jax.random.randint(jax.random.fold_in(own_key, 1), shape, 0, int(grid[number_of - 1]))
    standing = jnp.searchsorted(jnp.asarray(grid, jnp.int32), pick, side="right")
    return jax.random.permutation(jax.random.fold_in(own_key, 2), number_of)[standing].astype(jnp.int32)


def normal_values(key, shape, deviation, most, pieces=(), kind=jnp.bfloat16):
    factor_of = block_scale(key, shape, pieces, -0.22, 0.18) if pieces else 1.0
    drawn = jax.random.normal(key, shape, jnp.float32) * deviation * factor_of
    return jnp.minimum(jnp.maximum(drawn, -most), most).astype(kind)


def setup_inputs(seed: int = 0) -> dict:
    seeds = jax.random.split(jax.random.key(seed), 11)
    return {
        "query_layer_input": normal_values(seeds[0], (QUERIES, MODEL_WIDTH), 1.0, 6.0, ((0, 768),)),
        "query_frozen_base": normal_values(seeds[1], (QUERIES, MODEL_WIDTH), 1.0, 6.0, ((0, 768),)),
        "passage_layer_input": normal_values(seeds[2], (PASSAGES, MODEL_WIDTH), 1.0, 6.0, ((0, 768),)),
        "passage_frozen_base": normal_values(seeds[3], (PASSAGES, MODEL_WIDTH), 1.0, 6.0, ((0, 768),)),
        "adapter_down_weight": normal_values(seeds[4], (MODEL_WIDTH, ADAPTER_RANK), MODEL_WIDTH ** -0.5, 0.09375),
        "adapter_up_weight": normal_values(seeds[5], (ADAPTER_RANK, MODEL_WIDTH), ADAPTER_RANK ** -0.5, 0.75),
        "positive_passage_index": plant(jax.random.randint(seeds[6], (QUERIES,), 0, DEVICE_PASSAGES), jax.random.fold_in(seeds[6], 1), 0, DEVICE_PASSAGES - 1).astype(jnp.int32),
        "hard_negative_slots": plant(ranked_ids(seeds[7], (QUERIES, HARD), SLOTS, 2), jax.random.fold_in(seeds[7], 3), 0, SLOTS - 1).astype(jnp.int32),
        "group_peer_rows": plant(jax.random.randint(seeds[8], (N_DP * N_GROUP * N_DP, C_NEAR), 0, DEVICE_PASSAGES), jax.random.fold_in(seeds[8], 1), 0, DEVICE_PASSAGES - 1).astype(jnp.int32),
        "remote_group_rows": plant(jax.random.randint(seeds[9], (N_DP * N_GROUP * N_GROUP, C_FAR), 0, DEVICE_PASSAGES), jax.random.fold_in(seeds[9], 1), 0, DEVICE_PASSAGES - 1).astype(jnp.int32),
    }


adapter_scale = 2.0
logit_divisor = 0.05
epsilon = 1e-06

def embedding_rows(hidden_state, frozen_output, adapter_down_weight, adapter_up_weight):
    adapter_latent = jnp.dot(hidden_state, adapter_down_weight, preferred_element_type=jnp.float32).astype(jnp.bfloat16)
    unnormalized_rows = frozen_output.astype(jnp.float32) + adapter_scale * jnp.dot(adapter_latent, adapter_up_weight, preferred_element_type=jnp.float32)
    inverse = lax.rsqrt(lax.optimization_barrier(jnp.sum(unnormalized_rows * unnormalized_rows, axis=-1, keepdims=True)) + epsilon)
    unit_rows = (unnormalized_rows * inverse).astype(jnp.bfloat16)
    scaled = (adapter_latent.astype(jnp.float32) * inverse).astype(jnp.bfloat16)
    return (unit_rows, scaled, inverse)

def tangent_of(grad_rows, unit_rows):
    unit_f = unit_rows.astype(jnp.float32)
    radial = lax.optimization_barrier(jnp.sum(unit_f * grad_rows, axis=-1, keepdims=True))
    return (grad_rows - unit_f * radial).astype(jnp.bfloat16)

def backward_projection(tangent_row_block, adapter_up_weight):
    return jnp.dot(tangent_row_block, adapter_up_weight.T, preferred_element_type=jnp.float32).astype(jnp.bfloat16)

def up_weight_term(scaled, tangent_row_block):
    return jnp.dot(scaled.T, tangent_row_block, preferred_element_type=jnp.float32)

def score_rows(request_normalized_directions, match_entries, collected_entries, slots, loss_slope_coefficient):
    slot_count = collected_entries.shape[0]
    match_similarities = jnp.dot(request_normalized_directions, match_entries.T, preferred_element_type=jnp.float32) / logit_divisor
    similarity_table = jnp.dot(request_normalized_directions, collected_entries.T, preferred_element_type=jnp.float32) / logit_divisor
    hard_scores = jnp.take_along_axis(similarity_table, slots, axis=1)
    maximal_logit_offset = 1.0 / logit_divisor
    match_exponential = jnp.exp(match_similarities - maximal_logit_offset)
    distractor_exponential = jnp.exp(hard_scores - maximal_logit_offset)
    partition_function = lax.optimization_barrier(jnp.sum(match_exponential, axis=1, keepdims=True)) + lax.optimization_barrier(jnp.sum(distractor_exponential, axis=1, keepdims=True))
    loss_sum = jnp.sum(jnp.log(partition_function[:, 0]) + maximal_logit_offset - jnp.diagonal(match_similarities))
    match_indicator = jnp.eye(match_similarities.shape[0], dtype=jnp.float32)
    match_slope = ((match_exponential / partition_function - match_indicator) * (loss_slope_coefficient / logit_divisor)).astype(jnp.bfloat16)
    distractor_probability = distractor_exponential / partition_function * (loss_slope_coefficient / logit_divisor)
    row_match = (slots[:, :, None] == jnp.arange(slot_count, dtype=jnp.int32)[None, None, :]).astype(jnp.float32)
    hard_grad = lax.optimization_barrier(jnp.sum(row_match * distractor_probability[:, :, None], axis=1)).astype(jnp.bfloat16)
    return (loss_sum, match_slope, hard_grad)

def reference(query_layer_input, query_frozen_base, passage_layer_input, passage_frozen_base, adapter_down_weight, adapter_up_weight, positive_passage_index, hard_negative_slots, group_peer_rows, remote_group_rows):
    device_list = N_DP * N_GROUP
    queries = Q_DEV * device_list
    loss_slope_coefficient = 16.0 / math.sqrt(queries)
    passage_hidden_state = passage_layer_input.reshape(device_list, DEVICE_PASSAGES, MODEL_WIDTH)
    passage_frozen_output = passage_frozen_base.reshape(device_list, DEVICE_PASSAGES, MODEL_WIDTH)
    passage_unit_rows, passage_scaled_rows, passage_inverse_norm = lax.map(lambda hidden_state_pair: embedding_rows(hidden_state_pair[0], hidden_state_pair[1], adapter_down_weight, adapter_up_weight), (passage_hidden_state, passage_frozen_output))
    unit_grid = passage_unit_rows.reshape(N_DP, N_GROUP, DEVICE_PASSAGES, MODEL_WIDTH)
    scaled_grid = passage_scaled_rows.reshape(N_DP, N_GROUP, DEVICE_PASSAGES, ADAPTER_RANK)
    near_grid = group_peer_rows.reshape(N_DP, N_GROUP, N_DP, C_NEAR)
    far_grid = remote_group_rows.reshape(N_DP, N_GROUP, N_GROUP, C_FAR)
    pick_rows = jax.vmap(lambda source, picks: source[picks])

    def device_step(carry, inputs):
        loss_acc, down_acc, up_acc = carry
        device_index, query_hidden_state, query_frozen_output, positives, slots = inputs
        dp_index = device_index // N_GROUP
        group_index = device_index % N_GROUP
        near_ids = near_grid[:, group_index, dp_index]
        far_ids = far_grid[dp_index, :, group_index]
        collected_entries = jnp.concatenate([pick_rows(unit_grid[:, group_index], near_ids).reshape(-1, MODEL_WIDTH), pick_rows(unit_grid[dp_index], far_ids).reshape(-1, MODEL_WIDTH)], axis=0)
        gathered_latent_rows = jnp.concatenate([pick_rows(scaled_grid[:, group_index], near_ids).reshape(-1, ADAPTER_RANK), pick_rows(scaled_grid[dp_index], far_ids).reshape(-1, ADAPTER_RANK)], axis=0)
        local_unit = unit_grid[dp_index, group_index]
        local_scaled = scaled_grid[dp_index, group_index]
        match_entries = local_unit[positives]
        positive_latent = local_scaled[positives]
        query_unit_rows, query_scaled_rows, query_inverse_norm = embedding_rows(query_hidden_state, query_frozen_output, adapter_down_weight, adapter_up_weight)
        loss_sum, match_slope, hard_grad = score_rows(query_unit_rows, match_entries, collected_entries, slots, loss_slope_coefficient)
        query_grad = jnp.dot(match_slope, match_entries, preferred_element_type=jnp.float32) + jnp.dot(hard_grad, collected_entries, preferred_element_type=jnp.float32)
        pos_slot_grad = jnp.dot(match_slope.T, query_unit_rows, preferred_element_type=jnp.float32)
        fetched_grad = jnp.dot(hard_grad.T, query_unit_rows, preferred_element_type=jnp.float32)
        query_tangent_rows = tangent_of(query_grad, query_unit_rows)
        positive_tangent = tangent_of(pos_slot_grad, match_entries)
        gathered_tangent_rows = tangent_of(fetched_grad, collected_entries)
        up_weight_partial = adapter_scale * (up_weight_term(query_scaled_rows, query_tangent_rows) + up_weight_term(positive_latent, positive_tangent) + up_weight_term(gathered_latent_rows, gathered_tangent_rows))
        query_back_rows = backward_projection(query_tangent_rows, adapter_up_weight)
        query_output_gradient = (adapter_scale * query_inverse_norm * query_back_rows.astype(jnp.float32)).astype(jnp.bfloat16)
        down_part = jnp.dot(query_hidden_state.T, query_output_gradient, preferred_element_type=jnp.float32)
        positive_back_rows = backward_projection(positive_tangent, adapter_up_weight)
        gathered_back_rows = backward_projection(gathered_tangent_rows, adapter_up_weight)
        return ((loss_acc + loss_sum, down_acc + down_part, up_acc + up_weight_partial), (positive_back_rows, gathered_back_rows))
    inputs = (jnp.arange(device_list, dtype=jnp.int32), query_layer_input.reshape(device_list, Q_DEV, MODEL_WIDTH), query_frozen_base.reshape(device_list, Q_DEV, MODEL_WIDTH), positive_passage_index.reshape(device_list, Q_DEV), hard_negative_slots.reshape(device_list, Q_DEV, HARD))
    init = (jnp.zeros((), jnp.float32), jnp.zeros((MODEL_WIDTH, ADAPTER_RANK), jnp.float32), jnp.zeros((ADAPTER_RANK, MODEL_WIDTH), jnp.float32))
    (loss_total, down_total, up_total), (positive_back_rows, gathered_back_rows) = lax.scan(device_step, init, inputs)
    dp_axis = jnp.arange(N_DP, dtype=jnp.int32)
    group_axis = jnp.arange(N_GROUP, dtype=jnp.int32)
    row_total_sum = jnp.zeros((N_DP, N_GROUP, DEVICE_PASSAGES, ADAPTER_RANK), jnp.float32)
    row_total_sum = row_total_sum.at[dp_axis[:, None, None], group_axis[None, :, None], positive_passage_index.reshape(N_DP, N_GROUP, Q_DEV)].add(positive_back_rows.reshape(N_DP, N_GROUP, Q_DEV, ADAPTER_RANK).astype(jnp.float32))
    near_part = gathered_back_rows[:, :N_DP * C_NEAR].reshape(N_DP, N_GROUP, N_DP, C_NEAR, ADAPTER_RANK)
    row_total_sum = row_total_sum.at[dp_axis[None, None, :, None], group_axis[None, :, None, None], near_grid.transpose(2, 1, 0, 3)].add(near_part.astype(jnp.float32))
    far_part = gathered_back_rows[:, N_DP * C_NEAR:].reshape(N_DP, N_GROUP, N_GROUP, C_FAR, ADAPTER_RANK)
    row_total_sum = row_total_sum.at[dp_axis[:, None, None, None], group_axis[None, None, :, None], far_grid.transpose(0, 2, 1, 3)].add(far_part.astype(jnp.float32))
    passage_output_gradient = (adapter_scale * passage_inverse_norm * row_total_sum.reshape(device_list, DEVICE_PASSAGES, ADAPTER_RANK)).astype(jnp.bfloat16)

    def passage_step(carry, inputs):
        hidden_state, grad_latent = inputs
        return (carry + jnp.dot(hidden_state.T, grad_latent, preferred_element_type=jnp.float32), None)
    down_passage, _ = lax.scan(passage_step, jnp.zeros((MODEL_WIDTH, ADAPTER_RANK), jnp.float32), (passage_hidden_state, passage_output_gradient))
    return (down_total + down_passage, up_total, loss_total / queries)
```

```python
import math

import jax
import jax.numpy as jnp
from jax import lax
from jax.experimental import pallas as pl
from jax.experimental.pallas import tpu as pltpu
from jax.sharding import PartitionSpec as P

f32 = jnp.float32
bf16 = jnp.bfloat16
adapter_scale = 2.0
logit_divisor = 0.05
epsilon = 1e-06
offset = 1.0 / logit_divisor
tile = 512
lanes = 128


def dot(a, b, ca=1, cb=0):
    return lax.dot_general(a, b, (((ca,), (cb,)), ((), ())), preferred_element_type=f32)


def iota(shape, dim):
    return lax.broadcasted_iota(jnp.int32, shape, dim)


def eye(n, m):
    return (iota((n, m), 0) == iota((n, m), 1)).astype(bf16)


def flip(a):
    return dot(eye(a.shape[1], a.shape[1]), a, 1, 1).astype(bf16)


def column_tiles(width):
    step = min(tile, width)
    return [slice(c, c + step) for c in range(0, width, step)]


def embed(x_ref, base_ref, down_ref, up_ref, unit_ref, ext_ref, inv_ref, raw_ref):
    rows, width = x_ref.shape
    rank = up_ref.shape[0]
    latent = dot(x_ref[...], down_ref[...], 1, 1).astype(bf16)
    squares = jnp.zeros((rows, 1), f32)
    for cols in column_tiles(width):
        raw = base_ref[:, cols].astype(f32) + adapter_scale * dot(latent, up_ref[:, cols])
        raw_ref[:, cols] = raw
        squares = squares + jnp.sum(raw * raw, axis=1, keepdims=True)
    inverse = lax.rsqrt(squares + epsilon)
    for cols in column_tiles(width):
        unit_ref[:, cols] = (raw_ref[:, cols] * inverse).astype(bf16)
    scaled = (latent.astype(f32) * inverse).astype(bf16)
    high = inverse.astype(bf16).astype(f32)
    lane = iota((rows, lanes), 1)
    ext = dot(scaled, eye(rank, lanes))
    ext = jnp.where(lane == rank, high, ext)
    ext = jnp.where(lane == rank + 1, inverse - high, ext)
    ext_ref[...] = ext.astype(bf16)
    inv_ref[...] = jnp.broadcast_to(inverse, inv_ref.shape)


def passage_kernel(
    grid_x, grid_y, place_ref, x_ref, base_ref, down_ref, up_ref, near_ids_ref, far_ids_ref,
    near_ref, far_ref, unit_ref, ext_ref, inv_ref, pick_ref, raw_ref,
):
    embed(x_ref, base_ref, down_ref, up_ref, unit_ref, ext_ref, inv_ref, raw_ref)
    rows, width = x_ref.shape
    half = width // 2
    per_near, n_near = near_ids_ref.shape
    count = per_near * n_near
    ids = near_ids_ref[...].astype(f32).astype(bf16)
    spread = (iota((count, n_near), 0) // per_near == iota((count, n_near), 1)).astype(bf16)
    table = dot(spread, ids, 1, 1)
    mine = iota((count, per_near), 0) % per_near == iota((count, per_near), 1)
    wanted = jnp.sum(jnp.where(mine, table, 0.0), axis=1, keepdims=True).astype(jnp.int32)
    pick = (iota((count, rows), 1) == wanted).astype(bf16)
    pick_ref[...] = pick
    for cols in column_tiles(width):
        near_ref[:, cols] = dot(pick, unit_ref[:, cols]).astype(bf16)
    near_ref[:, width:] = dot(pick, ext_ref[...]).astype(bf16)
    n_far = far_ids_ref.shape[1]
    total = n_far * 8
    where_x, where_y = place_ref[0], place_ref[1]
    ids = far_ids_ref[...].astype(f32).astype(bf16)
    block = iota((total, n_far), 0) // 8
    to_x = (where_x + block // grid_y) % grid_x
    to_y = (where_y + block % grid_y) % grid_y
    spread = (to_x * grid_y + to_y == iota((total, n_far), 1)).astype(bf16)
    table = dot(spread, ids, 1, 1)
    mine = iota((total, 2), 0) % 2 == iota((total, 2), 1)
    wanted = jnp.sum(jnp.where(mine, table, 0.0), axis=1, keepdims=True).astype(jnp.int32)
    kind = (iota((total, 4 * rows), 0) // 2) % 4
    source = iota((total, 4 * rows), 1)
    choose = ((source // rows == kind) & (source % rows == wanted)).astype(bf16)
    for cols in column_tiles(half):
        later = slice(half + cols.start, half + cols.stop)
        stack = jnp.concatenate(
            [unit_ref[:, cols], unit_ref[:, later], x_ref[:, cols], x_ref[:, later]], axis=0
        )
        far_ref[:, cols] = dot(choose, stack).astype(bf16)
    first = jnp.where(iota((total, rows), 0) // 2 % 4 == 0, wanted, -1)
    far_ref[:, half:] = dot((iota((total, rows), 1) == first).astype(bf16), ext_ref[...]).astype(
        bf16
    )


def query_kernel(
    grid_x, grid_y, place_ref, x_ref, base_ref, down_ref, up_ref, slots_ref,
    unit_ref, ext_ref, inv_ref, near_count_ref, other_count_ref, raw_ref,
):
    embed(x_ref, base_ref, down_ref, up_ref, unit_ref, ext_ref, inv_ref, raw_ref)
    hard, rows = slots_ref.shape
    n_near = near_count_ref.shape[1]
    n_other = other_count_ref.shape[1]
    n_far = n_other - rows
    where_x, where_y = place_ref[0], place_ref[1]
    near_slot = iota((n_near, rows), 0)
    spot = iota((n_other, rows), 0)
    block = spot // 2
    from_x = (where_x + grid_x - block % grid_x) % grid_x
    from_y = (where_y + grid_y - (block // grid_x) % grid_y) % grid_y
    far_slot = n_near + (from_x * grid_y + from_y) * 2 + spot % 2
    far_slot = jnp.where(spot < n_far, far_slot, -1)
    near_count = jnp.zeros((n_near, rows), f32)
    other_count = jnp.zeros((n_other, rows), f32)
    for k in range(hard):
        slot = slots_ref[k : k + 1, :]
        near_count = near_count + (near_slot == slot).astype(f32)
        other_count = other_count + (far_slot == slot).astype(f32)
    other_count = jnp.where(spot < n_far, other_count, 1.0)
    unit = eye(rows, rows)
    near_count_ref[...] = dot(unit, near_count.astype(bf16), 1, 1)
    other_count_ref[...] = dot(unit, other_count.astype(bf16), 1, 1)


def store_blocks(ref, cols, value):
    size = ref.shape[2]
    step = min(size, cols.stop - cols.start)
    for c in range(cols.start, cols.stop, step):
        at = c % size
        ref[c // size, :, at : at + step] = value[:, c - cols.start : c - cols.start + step]


def load_blocks(ref, cols):
    size = ref.shape[2]
    step = min(size, cols.stop - cols.start)
    parts = []
    for c in range(cols.start, cols.stop, step):
        parts.append(ref[c // size, :, c % size : c % size + step])
    return parts[0] if len(parts) == 1 else jnp.concatenate(parts, axis=1)


def score_kernel(
    slope, near_ref, far_ref, q_ref, q_ext_ref, q_inv_ref, unit_ref, p_ext_ref, positive_ref,
    near_count_ref, other_count_ref, up_ref,
    ret_ref, up_out_ref, row_ref, dz_q_ref, dz_f_ref, x_far_ref, o_ref,
):
    rows, width = q_ref.shape
    rank = up_ref.shape[0]
    half = width // 2
    total = far_ref.shape[0]
    n_far = total // 4
    n_near = near_ref.shape[0]
    out_row = iota((total, total), 0)
    in_row = iota((total, total), 1)
    spot = out_row % n_far
    undo = (
        (in_row // 8 == spot // 2)
        & (in_row % 2 == spot % 2)
        & ((in_row // 2) % 4 == out_row // n_far)
    ).astype(bf16)
    for cols in column_tiles(half):
        later = slice(half + cols.start, half + cols.stop)
        got = dot(undo, far_ref[:, cols]).astype(bf16)
        o_ref[0:n_far, cols] = got[0:n_far]
        o_ref[0:n_far, later] = got[n_far : 2 * n_far]
        x_far_ref[:, cols] = got[2 * n_far : 3 * n_far]
        x_far_ref[:, later] = got[3 * n_far :]
    far_ext = dot(undo[0:n_far], far_ref[:, half:])
    own = (iota((rows, rows), 0) == positive_ref[...]).astype(bf16)
    own_t = flip(own)
    for cols in column_tiles(width):
        o_ref[n_far:, cols] = dot(own_t, unit_ref[:, cols]).astype(bf16)
    pos_ext = dot(own_t, p_ext_ref[...])

    q_all = q_ref[...]
    near_raw = dot(q_all, near_ref[:, :width], 1, 1)
    other_raw = dot(q_all, o_ref[...], 1, 1)
    near_raw_t = dot(near_ref[:, :width], q_all, 1, 1)
    other_raw_t = dot(o_ref[...], q_all, 1, 1)
    near_exp = jnp.exp(near_raw / logit_divisor - offset) * near_count_ref[...]
    other_exp = jnp.exp(other_raw / logit_divisor - offset) * other_count_ref[...]
    partition = jnp.sum(near_exp, axis=1, keepdims=True) + jnp.sum(
        other_exp, axis=1, keepdims=True
    )
    same = iota(other_raw.shape, 1) == iota(other_raw.shape, 0) + n_far
    matched = jnp.sum(jnp.where(same, other_raw, 0.0), axis=1, keepdims=True) / logit_divisor
    loss = jnp.sum(jnp.log(partition) + offset - matched, axis=0, keepdims=True)
    near_g = (near_exp / partition * slope).astype(bf16)
    other_g = ((other_exp / partition - same.astype(f32)) * slope).astype(bf16)
    near_gt = flip(near_g)
    other_gt = flip(other_g)
    q_radial = jnp.sum(near_g.astype(f32) * near_raw, axis=1, keepdims=True) + jnp.sum(
        other_g.astype(f32) * other_raw, axis=1, keepdims=True
    )
    near_radial = jnp.sum(near_gt.astype(f32) * near_raw_t, axis=1, keepdims=True)
    other_radial = jnp.sum(other_gt.astype(f32) * other_raw_t, axis=1, keepdims=True)
    q_lat = flip(q_ext_ref[...])[0:rank]
    near_lat = flip(near_ref[:, width:])[0:rank]
    other_lat = flip(jnp.concatenate([far_ext, pos_ext], axis=0).astype(bf16))[0:rank]
    q_back = jnp.zeros((rows, rank), f32)
    near_back = jnp.zeros((n_near, rank), f32)
    other_back = jnp.zeros((n_far + rows, rank), f32)
    for cols in column_tiles(width):
        q = q_ref[:, cols]
        near = near_ref[:, cols]
        other = o_ref[:, cols]
        up = up_ref[:, cols]
        q_t = dot(near_g, near) + dot(other_g, other) - q.astype(f32) * q_radial
        near_t = dot(near_gt, q) - near.astype(f32) * near_radial
        other_t = dot(other_gt, q) - other.astype(f32) * other_radial
        q_t, near_t, other_t = q_t.astype(bf16), near_t.astype(bf16), other_t.astype(bf16)
        q_back = q_back + dot(q_t, up, 1, 1)
        near_back = near_back + dot(near_t, up, 1, 1)
        other_back = other_back + dot(other_t, up, 1, 1)
        grad = dot(q_lat, q_t) + dot(near_lat, near_t) + dot(other_lat, other_t)
        store_blocks(up_out_ref, cols, adapter_scale * grad)
    back = dot(near_back.astype(bf16), eye(rank, lanes))
    lane = iota((n_near, lanes), 1)
    high = loss.astype(bf16).astype(f32)
    back = jnp.where(lane == rank, high, back)
    back = jnp.where(lane == rank + 1, loss - high, back)
    ret_ref[...] = back.astype(bf16)
    other_back = other_back.astype(bf16)
    row_ref[...] = dot(own, other_back[n_far:])
    dz_q_ref[...] = (adapter_scale * q_inv_ref[:, 0:1] * q_back.astype(bf16).astype(f32)).astype(
        bf16
    )
    far_inv = far_ext[:, rank : rank + 1] + far_ext[:, rank + 1 : rank + 2]
    dz_f_ref[...] = (adapter_scale * far_inv * other_back[0:n_far].astype(f32)).astype(bf16)


def down_kernel(
    per_near, place_ref, ret_ref, pick_ref, row_ref, p_inv_ref, dz_q_ref, dz_f_ref, x_q_ref, x_p_ref,
    x_far_ref, up_part_ref, keep_ref, send_ref, loss_ref,
):
    rank = row_ref.shape[1]
    ret = ret_ref[...]
    row_sum = dot(flip(pick_ref[...]), ret)[:, 0:rank] + row_ref[...]
    dz_p = (adapter_scale * p_inv_ref[:, 0:1] * row_sum).astype(bf16)
    dz_pt, dz_qt, dz_ft = flip(dz_p), flip(dz_q_ref[...]), flip(dz_f_ref[...])
    even = place_ref[2] == 0
    for cols in column_tiles(x_q_ref.shape[1]):
        grad = (
            dot(dz_qt, x_q_ref[:, cols])
            + dot(dz_pt, x_p_ref[:, cols])
            + dot(dz_ft, x_far_ref[:, cols])
        )
        other = load_blocks(up_part_ref, cols)
        store_blocks(keep_ref, cols, jnp.where(even, grad, other))
        store_blocks(send_ref, cols, jnp.where(even, other, grad).astype(bf16))
    first = iota(ret.shape, 0) % per_near == 0
    lane = iota(ret.shape, 1)
    chosen = first & ((lane == rank) | (lane == rank + 1))
    part = jnp.sum(jnp.where(chosen, ret.astype(f32), 0.0), axis=1, keepdims=True)
    loss_ref[...] = jnp.broadcast_to(jnp.sum(part, axis=0, keepdims=True), loss_ref.shape)


def add_kernel(keep_ref, got_ref, out_ref):
    for i in range(keep_ref.shape[0]):
        out_ref[i] = (keep_ref[i] + got_ref[i].astype(f32)).astype(bf16)


def sum_blocks(ref):
    acc = ref[0].astype(f32)
    for i in range(1, ref.shape[0]):
        acc = acc + ref[i].astype(f32)
    return acc


def spread_kernel(in_ref, out_ref):
    value = sum_blocks(in_ref).astype(bf16)
    for i in range(out_ref.shape[0]):
        out_ref[i] = value


def finish_kernel(in_ref, loss_ref, out_ref):
    loss = loss_ref[...]
    high = loss.astype(bf16).astype(f32)
    row = iota(loss.shape, 0)
    tail = jnp.where(row == 0, high, jnp.where(row == 1, loss - high, 0.0))
    if out_ref.shape[2] > lanes:
        tail = jnp.concatenate([tail] * (out_ref.shape[2] // lanes), axis=1)
    value = jnp.concatenate([sum_blocks(in_ref), tail], axis=0).astype(bf16)
    for i in range(out_ref.shape[0]):
        out_ref[i] = value


def output_kernel(place_ref, mine_ref, other_ref, down_ref, up_ref, loss_ref):
    rank = down_ref.shape[0]
    size = mine_ref.shape[2]
    even = place_ref[2] == 0
    loss = jnp.zeros((8, lanes), f32)
    for i in range(mine_ref.shape[0]):
        mine, other = mine_ref[i].astype(f32), other_ref[i].astype(f32)
        cols = slice(i * size, (i + 1) * size)
        down_ref[:, cols] = jnp.where(even, mine[0:rank], other[0:rank])
        up_ref[:, cols] = jnp.where(even, other[0:rank], mine[0:rank])
        loss = loss + mine[rank:, 0:lanes]
    loss_ref[...] = jnp.broadcast_to(jnp.sum(loss, axis=0, keepdims=True), loss.shape)


def call(kernel, outs, args, scratch=(), flops=0, moved=0):
    specs = []
    for a in args:
        space = pltpu.SMEM if a.dtype == jnp.int32 and a.ndim == 1 else pltpu.VMEM
        specs.append(pl.BlockSpec(memory_space=space))
    shapes = [jax.ShapeDtypeStruct(s, d) for s, d in outs]
    return pl.pallas_call(
        kernel,
        out_shape=shapes,
        in_specs=specs,
        out_specs=[pl.BlockSpec(memory_space=pltpu.VMEM) for _ in shapes],
        scratch_shapes=[pltpu.VMEM(s, d) for s, d in scratch],
        compiler_params=pltpu.CompilerParams(vmem_limit_bytes=40 * 1024 * 1024),
        cost_estimate=pl.CostEstimate(flops=flops, bytes_accessed=moved, transcendentals=0),
    )(*args)


def exchange(x, axis, groups=None):
    return lax.all_to_all(
        x, axis, split_axis=0, concat_axis=0, tiled=True, axis_index_groups=groups
    )


def far_exchange(blocks, grid_x, grid_y):
    rows, width = blocks.shape
    group = [(x, y) for x in range(grid_x) for y in range(grid_y)]
    line = blocks.reshape(grid_x, grid_y, 8, width)
    got = [line[0]]
    for dx in range(1, grid_x):
        pairs = [(x * grid_y + y, (x + dx) % grid_x * grid_y + y) for x, y in group]
        got.append(lax.ppermute(line[dx], "group", pairs))
    ended = []
    for dy in range(grid_y):
        piece = jnp.concatenate([g[dy] for g in got], axis=0)
        if dy:
            pairs = [(x * grid_y + y, x * grid_y + (y + dy) % grid_y) for x, y in group]
            piece = lax.ppermute(piece, "group", pairs)
        ended.append(piece)
    return jnp.concatenate(ended, axis=0)


def make_body(grid_x, grid_y):
    def body(
        query_layer_input,
        query_frozen_base,
        passage_layer_input,
        passage_frozen_base,
        adapter_down_weight,
        adapter_up_weight,
        positive_passage_index,
        hard_negative_slots,
        group_peer_rows,
        remote_group_rows,
    ):
        n_dp = lax.axis_size("dp")
        n_group = lax.axis_size("group")
        rows, width = query_layer_input.shape
        rank = adapter_up_weight.shape[0]
        queries = rows * n_dp * n_group
        slope = 16.0 / math.sqrt(queries) / logit_divisor
        g = lax.axis_index("group")
        place = jnp.stack([g // grid_y, g % grid_y, lax.axis_index("dp") % 2]).astype(jnp.int32)
        down_t = adapter_down_weight.T
        per_near = group_peer_rows.shape[1]
        n_near = n_dp * per_near
        n_far = n_group * 2
        half = width // 2
        block = width // n_group
        near, far, p_unit, p_ext, p_inv, pick = call(
            lambda *refs: passage_kernel(grid_x, grid_y, *refs),
            [
                ((n_near, width + lanes), bf16),
                ((n_far * 4, half + lanes), bf16),
                ((rows, width), bf16),
                ((rows, lanes), bf16),
                ((rows, lanes), f32),
                ((n_near, rows), bf16),
            ],
            (
                place, passage_layer_input, passage_frozen_base, down_t, adapter_up_weight,
                group_peer_rows.T, remote_group_rows.T,
            ),
            [((rows, width), f32)], flops=400_000_000, moved=6_000_000,
        )
        near = exchange(near.reshape(n_dp, per_near, width + lanes), "dp")
        near = near.reshape(n_near, width + lanes)
        far = far_exchange(far, grid_x, grid_y)
        q_unit, q_ext, q_inv, near_count, other_count = call(
            lambda *refs: query_kernel(grid_x, grid_y, *refs),
            [
                ((rows, width), bf16),
                ((rows, lanes), bf16),
                ((rows, lanes), f32),
                ((rows, n_near), f32),
                ((rows, n_far + rows), f32),
            ],
            (
                place, query_layer_input, query_frozen_base, down_t, adapter_up_weight,
                hard_negative_slots.T,
            ),
            [((rows, width), f32)], flops=100_000_000, moved=3_000_000,
        )
        ret, up_part, row_part, dz_q, dz_f, x_far = call(
            lambda *refs: score_kernel(slope, *refs),
            [
                ((n_near, lanes), bf16),
                ((n_group, rank, block), f32),
                ((rows, rank), f32),
                ((rows, rank), bf16),
                ((n_far, rank), bf16),
                ((n_far, width), bf16),
            ],
            (
                near, far, q_unit, q_ext, q_inv, p_unit, p_ext,
                positive_passage_index.reshape(1, rows), near_count, other_count,
                adapter_up_weight,
            ),
            [((n_far + rows, width), bf16)], flops=1_500_000_000, moved=8_000_000,
        )
        ret = exchange(ret.reshape(n_dp, per_near, lanes), "dp").reshape(n_near, lanes)
        keep, send, loss = call(
            lambda *refs: down_kernel(per_near, *refs),
            [
                ((n_group, rank, block), f32),
                ((n_group, rank, block), bf16),
                ((8, lanes), f32),
            ],
            (
                place, ret, pick, row_part, p_inv, dz_q, dz_f, query_layer_input,
                passage_layer_input, x_far, up_part,
            ),
            flops=200_000_000, moved=5_000_000,
        )
        swap = [(i, i ^ 1) for i in range(n_dp)]
        got = lax.ppermute(send, "dp", swap)
        (part,) = call(add_kernel, [((n_group, rank, block), bf16)], (keep, got), moved=2_500_000)
        part = exchange(part, "group")
        cores = [list(range(c, n_dp, 2)) for c in range(2)]
        (part,) = call(
            spread_kernel, [((n_dp // 2, rank, block), bf16)], (part,), moved=1_000_000
        )
        part = exchange(part, "dp", cores)
        (part,) = call(
            finish_kernel, [((n_group, rank + 8, block), bf16)], (part, loss), moved=1_000_000
        )
        part = exchange(part, "group")
        other = lax.ppermute(part, "dp", swap)
        down, up, loss = call(
            output_kernel,
            [((rank, width), f32), ((rank, width), f32), ((8, lanes), f32)],
            (place, part, other),
            moved=3_500_000,
        )
        return (down.T, up, loss[0, 0] / queries)

    return body


def solution(mesh):
    n_group = mesh.shape["group"]
    grid_x = {32: 4, 4: 2}[n_group]
    both = P(("dp", "group"), None)
    placed = (both, both, both, both, P(), P(), P(("dp", "group")), both, both, both)
    return jax.shard_map(
        make_body(grid_x, n_group // grid_x),
        mesh=mesh,
        in_specs=placed,
        out_specs=(P(), P(), P()),
        check_vma=False,
    )
```

```python
import math

import jax
import jax.numpy as jnp
from jax import lax
from jax.experimental import pallas as pl
from jax.experimental.pallas import tpu as pltpu
from jax.sharding import PartitionSpec as P

f32 = jnp.float32
bf16 = jnp.bfloat16
adapter_scale = 2.0
logit_divisor = 0.05
epsilon = 1e-06
offset = 1.0 / logit_divisor
tile = 512
lanes = 128


def dot(a, b, ca=1, cb=0):
    return lax.dot_general(a, b, (((ca,), (cb,)), ((), ())), preferred_element_type=f32)


def iota(shape, dim):
    return lax.broadcasted_iota(jnp.int32, shape, dim)


def eye(n, m):
    return (iota((n, m), 0) == iota((n, m), 1)).astype(bf16)


def flip(a):
    return dot(eye(a.shape[1], a.shape[1]), a, 1, 1).astype(bf16)


def column_tiles(width):
    step = min(tile, width)
    return [slice(c, c + step) for c in range(0, width, step)]


def embed(x_ref, base_ref, down_ref, up_ref, unit_ref, ext_ref, inv_ref, raw_ref, ready=None):
    rows, width = x_ref.shape
    rank = up_ref.shape[0]
    latent = dot(x_ref[...], down_ref[...], 1, 1).astype(bf16)
    if ready is not None:
        ready()
    squares = jnp.zeros((rows, 1), f32)
    for cols in column_tiles(width):
        raw = base_ref[:, cols].astype(f32) + adapter_scale * dot(latent, up_ref[:, cols])
        raw_ref[:, cols] = raw
        squares = squares + jnp.sum(raw * raw, axis=1, keepdims=True)
    inverse = lax.rsqrt(squares + epsilon)
    for cols in column_tiles(width):
        unit_ref[:, cols] = (raw_ref[:, cols] * inverse).astype(bf16)
    scaled = (latent.astype(f32) * inverse).astype(bf16)
    high = inverse.astype(bf16).astype(f32)
    lane = iota((rows, lanes), 1)
    ext = dot(scaled, eye(rank, lanes))
    ext = jnp.where(lane == rank, high, ext)
    ext = jnp.where(lane == rank + 1, inverse - high, ext)
    ext_ref[...] = ext.astype(bf16)
    inv_ref[...] = jnp.broadcast_to(inverse, inv_ref.shape)


def passage_kernel(
    grid_x, grid_y, place_ref, x_hbm, base_hbm, down_hbm, up_hbm, near_ids_hbm, far_ids_hbm, *refs
):
    near_ref, *far_refs = refs[: 1 + grid_y]
    unit_ref, ext_ref, inv_ref, pick_ref = refs[1 + grid_y : 5 + grid_y]
    (x_ref, base_ref, down_ref, up_ref, near_ids_ref, far_ids_ref, raw_ref, sems) = refs[5 + grid_y :]
    pairs = [
        (x_hbm, x_ref), (down_hbm, down_ref), (base_hbm, base_ref), (up_hbm, up_ref),
        (near_ids_hbm, near_ids_ref), (far_ids_hbm, far_ids_ref),
    ]
    copies = [pltpu.make_async_copy(a, b, sems.at[i]) for i, (a, b) in enumerate(pairs)]
    for c in copies:
        c.start()
    copies[0].wait()
    copies[1].wait()

    def ready():
        copies[2].wait()
        copies[3].wait()

    embed(x_ref, base_ref, down_ref, up_ref, unit_ref, ext_ref, inv_ref, raw_ref, ready)
    copies[4].wait()
    copies[5].wait()
    rows, width = x_ref.shape
    half = width // 2
    per_near, n_near = near_ids_ref.shape
    count = per_near * n_near
    ids = near_ids_ref[...].astype(f32).astype(bf16)
    spread = (iota((count, n_near), 0) // per_near == iota((count, n_near), 1)).astype(bf16)
    table = dot(spread, ids, 1, 1)
    mine = iota((count, per_near), 0) % per_near == iota((count, per_near), 1)
    wanted = jnp.sum(jnp.where(mine, table, 0.0), axis=1, keepdims=True).astype(jnp.int32)
    pick = (iota((count, rows), 1) == wanted).astype(bf16)
    pick_ref[...] = pick
    for cols in column_tiles(width):
        near_ref[:, cols] = dot(pick, unit_ref[:, cols]).astype(bf16)
    near_ref[:, width:] = dot(pick, ext_ref[...]).astype(bf16)
    n_far = far_ids_ref.shape[1]
    total = n_far * 8
    size = grid_x * 8
    where_x, where_y = place_ref[0], place_ref[1]
    ids = far_ids_ref[...].astype(f32).astype(bf16)
    block = iota((total, n_far), 0) // 8
    to_x = (where_x + block % grid_x) % grid_x
    to_y = (where_y + block // grid_x) % grid_y
    spread = (to_x * grid_y + to_y == iota((total, n_far), 1)).astype(bf16)
    table = dot(spread, ids, 1, 1)
    mine = iota((total, 2), 0) % 2 == iota((total, 2), 1)
    wanted = jnp.sum(jnp.where(mine, table, 0.0), axis=1, keepdims=True).astype(jnp.int32)
    kind = (iota((total, 4 * rows), 0) // 2) % 4
    source = iota((total, 4 * rows), 1)
    choose = ((source // rows == kind) & (source % rows == wanted)).astype(bf16)
    for cols in column_tiles(half):
        later = slice(half + cols.start, half + cols.stop)
        stack = jnp.concatenate(
            [unit_ref[:, cols], unit_ref[:, later], x_ref[:, cols], x_ref[:, later]], axis=0
        )
        got = dot(choose, stack).astype(bf16)
        for dy in range(grid_y):
            far_refs[dy][:, cols] = got[dy * size : (dy + 1) * size]
    first = jnp.where(iota((total, rows), 0) // 2 % 4 == 0, wanted, -1)
    got = dot((iota((total, rows), 1) == first).astype(bf16), ext_ref[...]).astype(bf16)
    for dy in range(grid_y):
        far_refs[dy][:, half:] = got[dy * size : (dy + 1) * size]


def query_kernel(
    grid_x, grid_y, place_ref, x_ref, base_ref, down_ref, up_ref, slots_ref,
    unit_ref, ext_ref, inv_ref, near_count_ref, other_count_ref, raw_ref,
):
    embed(x_ref, base_ref, down_ref, up_ref, unit_ref, ext_ref, inv_ref, raw_ref)
    hard, rows = slots_ref.shape
    n_near = near_count_ref.shape[0]
    n_other = other_count_ref.shape[0]
    n_far = n_other - rows
    where_x, where_y = place_ref[0], place_ref[1]
    near_slot = iota((n_near, rows), 0)
    spot = iota((n_other, rows), 0)
    block = spot // 2
    from_x = (where_x + grid_x - (block // grid_y) % grid_x) % grid_x
    from_y = (where_y + grid_y - block % grid_y) % grid_y
    far_slot = n_near + (from_x * grid_y + from_y) * 2 + spot % 2
    far_slot = jnp.where(spot < n_far, far_slot, -1)
    near_count = jnp.zeros((n_near, rows), f32)
    other_count = jnp.zeros((n_other, rows), f32)
    for k in range(hard):
        slot = slots_ref[k : k + 1, :]
        near_count = near_count + (near_slot == slot).astype(f32)
        other_count = other_count + (far_slot == slot).astype(f32)
    near_count_ref[...] = near_count
    other_count_ref[...] = jnp.where(spot < n_far, other_count, 1.0)


def store_blocks(ref, cols, value):
    size = ref.shape[2]
    step = min(size, cols.stop - cols.start)
    for c in range(cols.start, cols.stop, step):
        at = c % size
        ref[c // size, :, at : at + step] = value[:, c - cols.start : c - cols.start + step]


def load_blocks(ref, cols):
    size = ref.shape[2]
    step = min(size, cols.stop - cols.start)
    parts = []
    for c in range(cols.start, cols.stop, step):
        parts.append(ref[c // size, :, c % size : c % size + step])
    return parts[0] if len(parts) == 1 else jnp.concatenate(parts, axis=1)


def far_kernel(count, *refs):
    far_refs = refs[:count]
    q_ref, unit_ref, p_ext_ref, positive_ref = refs[count : count + 4]
    o_ref, ext_ref, x_far_ref, raw_ref = refs[count + 4 :]
    rows, width = q_ref.shape
    half = width // 2
    total = far_refs[0].shape[0]
    each = total // 4
    n_far = each * count
    out_row = iota((total, total), 0)
    in_row = iota((total, total), 1)
    spot = out_row % each
    undo = (
        (in_row // 8 == spot // 2)
        & (in_row % 2 == spot % 2)
        & ((in_row // 2) % 4 == out_row // each)
    ).astype(bf16)
    for i, far_ref in enumerate(far_refs):
        at = slice(i * each, (i + 1) * each)
        for cols in column_tiles(half):
            later = slice(half + cols.start, half + cols.stop)
            got = dot(undo, far_ref[:, cols]).astype(bf16)
            o_ref[at, cols] = got[0:each]
            o_ref[at, later] = got[each : 2 * each]
            x_far_ref[at, cols] = got[2 * each : 3 * each]
            x_far_ref[at, later] = got[3 * each :]
        ext_ref[at, :] = dot(undo[0:each], far_ref[:, half:]).astype(bf16)
    own = (iota((rows, rows), 0) == positive_ref[...]).astype(bf16)
    own_t = flip(own)
    for cols in column_tiles(width):
        o_ref[n_far:, cols] = dot(own_t, unit_ref[:, cols]).astype(bf16)
    ext_ref[n_far:, :] = dot(own_t, p_ext_ref[...]).astype(bf16)
    raw_ref[...] = dot(o_ref[...], q_ref[...], 1, 1)


def score_kernel(
    slope, rank, near_ref, q_ref, other_raw_hbm, near_count_ref, other_count_ref, up_ref,
    ret_ref, near_g_ref, other_g_ref, near_radial_ref, other_radial_ref, q_radial_ref,
    other_raw_ref, sem,
):
    copy = pltpu.make_async_copy(other_raw_hbm, other_raw_ref, sem)
    copy.start()
    rows, width = q_ref.shape
    n_near = near_ref.shape[0]
    near_raw = dot(near_ref[:, :width], q_ref[...], 1, 1)
    copy.wait()
    other_raw = other_raw_ref[...]
    n_far = other_raw.shape[0] - rows
    near_exp = jnp.exp(near_raw / logit_divisor - offset) * near_count_ref[...]
    other_exp = jnp.exp(other_raw / logit_divisor - offset) * other_count_ref[...]
    partition = jnp.sum(near_exp, axis=0, keepdims=True) + jnp.sum(
        other_exp, axis=0, keepdims=True
    )
    same = iota(other_raw.shape, 0) == iota(other_raw.shape, 1) + n_far
    matched = jnp.sum(jnp.where(same, other_raw, 0.0), axis=0, keepdims=True) / logit_divisor
    loss = jnp.sum(jnp.log(partition) + offset - matched, axis=1, keepdims=True)
    near_g = (near_exp / partition * slope).astype(bf16)
    other_g = ((other_exp / partition - same.astype(f32)) * slope).astype(bf16)
    near_g_ref[...] = near_g
    other_g_ref[...] = other_g
    near_part = near_g.astype(f32) * near_raw
    other_part = other_g.astype(f32) * other_raw
    near_radial = jnp.sum(near_part, axis=1, keepdims=True)
    near_radial_ref[...] = near_radial
    other_radial_ref[...] = jnp.sum(other_part, axis=1, keepdims=True)
    q_radial = jnp.sum(near_part, axis=0, keepdims=True) + jnp.sum(
        other_part, axis=0, keepdims=True
    )
    square = iota((rows, rows), 0) == iota((rows, rows), 1)
    q_radial_ref[...] = jnp.sum(jnp.where(square, q_radial, 0.0), axis=1, keepdims=True)
    back = jnp.zeros((n_near, rank), f32)
    for cols in column_tiles(width):
        tangent = dot(near_g, q_ref[:, cols]) - near_ref[:, cols].astype(f32) * near_radial
        back = back + dot(tangent.astype(bf16), up_ref[:, cols], 1, 1)
    back = dot(back.astype(bf16), eye(rank, lanes))
    lane = iota((n_near, lanes), 1)
    high = loss.astype(bf16).astype(f32)
    back = jnp.where(lane == rank, high, back)
    back = jnp.where(lane == rank + 1, loss - high, back)
    ret_ref[...] = back.astype(bf16)


def local_kernel(
    place_ref, near_ref, o_ref, o_ext_ref, x_far_ref, q_ref, q_ext_ref, q_inv_ref, p_inv_ref, x_q_ref,
    positive_ref, near_g_ref, other_g_ref, near_radial_ref, other_radial_ref, q_radial_ref, up_ref,
    up_keep_ref, up_send_ref, down_ref, row_ref,
):
    rows, width = q_ref.shape
    rank = up_ref.shape[0]
    part = rank // 2
    n_far = o_ref.shape[0] - rows
    even = place_ref[2] == 0
    near_gt, other_gt = near_g_ref[...], other_g_ref[...]
    near_g, other_g = flip(near_gt), flip(other_gt)
    q_lat = flip(q_ext_ref[...])[0:rank]
    near_lat = flip(near_ref[:, width:])[0:rank]
    other_lat = flip(o_ext_ref[...])[0:rank]
    q_back = jnp.zeros((rows, rank), f32)
    other_back = jnp.zeros((n_far + rows, rank), f32)
    for cols in column_tiles(width):
        q = q_ref[:, cols]
        near = near_ref[:, cols]
        other = o_ref[:, cols]
        up = up_ref[:, cols]
        q_t = dot(near_g, near) + dot(other_g, other) - q.astype(f32) * q_radial_ref[...]
        near_t = dot(near_gt, q) - near.astype(f32) * near_radial_ref[...]
        other_t = dot(other_gt, q) - other.astype(f32) * other_radial_ref[...]
        q_t, near_t, other_t = q_t.astype(bf16), near_t.astype(bf16), other_t.astype(bf16)
        q_back = q_back + dot(q_t, up, 1, 1)
        other_back = other_back + dot(other_t, up, 1, 1)
        grad = dot(q_lat, q_t) + dot(near_lat, near_t) + dot(other_lat, other_t)
        grad = adapter_scale * grad
        top, low = grad[0:part], grad[part:]
        store_blocks(up_keep_ref, cols, jnp.where(even, top, low))
        store_blocks(up_send_ref, cols, jnp.where(even, low, top).astype(bf16))
    other_back = other_back.astype(bf16)
    own = (iota((rows, rows), 0) == positive_ref[...]).astype(bf16)
    wide = dot(other_back[n_far:], eye(rank, lanes)).astype(bf16)
    row_sum = dot(own, wide)
    row_ref[...] = jnp.where(iota(row_sum.shape, 1) < rank, row_sum, p_inv_ref[...])
    q_back = q_back.astype(bf16).astype(f32)
    dz_q = (adapter_scale * q_inv_ref[:, 0:1] * q_back).astype(bf16)
    far_ext = o_ext_ref[0:n_far, :].astype(f32)
    far_inv = far_ext[:, rank : rank + 1] + far_ext[:, rank + 1 : rank + 2]
    dz_f = (adapter_scale * far_inv * other_back[0:n_far].astype(f32)).astype(bf16)
    dz_qt, dz_ft = flip(dz_q), flip(dz_f)
    for cols in column_tiles(width):
        down_ref[:, cols] = dot(dz_qt, x_q_ref[:, cols]) + dot(dz_ft, x_far_ref[:, cols])


def down_kernel(
    per_near, place_ref, ret_ref, pick_ref, row_hbm, x_p_ref, down_hbm,
    keep_ref, send_ref, loss_ref, row_ref, down_ref, sems,
):
    row_copy = pltpu.make_async_copy(row_hbm, row_ref, sems.at[0])
    down_copy = pltpu.make_async_copy(down_hbm, down_ref, sems.at[1])
    row_copy.start()
    down_copy.start()
    rank = down_ref.shape[0]
    part = rank // 2
    ret = ret_ref[...]
    row_sum = dot(flip(pick_ref[...]), ret)[:, 0:rank]
    row_copy.wait()
    row_sum = row_sum + row_ref[:, 0:rank]
    dz_t = flip((adapter_scale * row_ref[:, rank : rank + 1] * row_sum).astype(bf16))
    down_copy.wait()
    even = place_ref[2] == 0
    for cols in column_tiles(x_p_ref.shape[1]):
        grad = dot(dz_t, x_p_ref[:, cols]) + down_ref[:, cols]
        top, low = grad[0:part], grad[part:]
        store_blocks(keep_ref, cols, jnp.where(even, top, low))
        store_blocks(send_ref, cols, jnp.where(even, low, top).astype(bf16))
    first = iota(ret.shape, 0) % per_near == 0
    lane = iota(ret.shape, 1)
    chosen = first & ((lane == rank) | (lane == rank + 1))
    share = jnp.sum(jnp.where(chosen, ret.astype(f32), 0.0), axis=1, keepdims=True)
    loss_ref[...] = jnp.broadcast_to(jnp.sum(share, axis=0, keepdims=True), loss_ref.shape)


def add_kernel(down_ref, got_down_ref, up_ref, got_up_ref, out_ref):
    part = down_ref.shape[1]
    for i in range(down_ref.shape[0]):
        out_ref[i, 0:part] = (down_ref[i] + got_down_ref[i].astype(f32)).astype(bf16)
        out_ref[i, part:] = (up_ref[i] + got_up_ref[i].astype(f32)).astype(bf16)


def sum_blocks(ref, *at):
    acc = ref[(0, *at)].astype(f32)
    for i in range(1, ref.shape[0]):
        acc = acc + ref[(i, *at)].astype(f32)
    return acc


def sum_kernel(in_ref, out_ref):
    for j in range(out_ref.shape[0]):
        out_ref[j] = sum_blocks(in_ref, j).astype(bf16)


def spread_kernel(in_ref, out_ref):
    value = sum_blocks(in_ref).astype(bf16)
    for i in range(out_ref.shape[0]):
        out_ref[i] = value


def copy_kernel(in_ref, out_ref):
    for i in range(out_ref.shape[0]):
        out_ref[i] = in_ref[...]


def finish_kernel(in_ref, loss_ref, out_ref):
    loss = loss_ref[...]
    high = loss.astype(bf16).astype(f32)
    row = iota(loss.shape, 0)
    tail = jnp.where(row == 0, high, jnp.where(row == 1, loss - high, 0.0))
    if out_ref.shape[2] > lanes:
        tail = jnp.concatenate([tail] * (out_ref.shape[2] // lanes), axis=1)
    value = jnp.concatenate([sum_blocks(in_ref), tail], axis=0).astype(bf16)
    for i in range(out_ref.shape[0]):
        out_ref[i] = value


def output_kernel(queries, place_ref, mine_ref, other_ref, down_ref, up_ref, loss_ref):
    rank = down_ref.shape[0]
    part = rank // 2
    size = mine_ref.shape[3]
    even = place_ref[2] == 0
    loss = jnp.zeros((8, lanes), f32)
    for i in range(mine_ref.shape[0]):
        for j in range(mine_ref.shape[1]):
            mine, other = mine_ref[i, j].astype(f32), other_ref[i, j].astype(f32)
            at = (i * mine_ref.shape[1] + j) * size
            cols = slice(at, at + size)
            top = jnp.where(even, mine[0:rank], other[0:rank])
            low = jnp.where(even, other[0:rank], mine[0:rank])
            down_ref[0:part, cols] = top[0:part]
            down_ref[part:, cols] = low[0:part]
            up_ref[0:part, cols] = top[part:]
            up_ref[part:, cols] = low[part:]
            loss = loss + mine[rank:, 0:lanes]
    loss_ref[...] = jnp.sum(loss, axis=0, keepdims=True)[:, 0:1] / queries


def call(kernel, outs, args, scratch=(), flops=0, moved=0, hbm=(), out_hbm=(), limit=16):
    specs = []
    for i, a in enumerate(args):
        space = pltpu.SMEM if a.dtype == jnp.int32 and a.ndim == 1 else pltpu.VMEM
        specs.append(pl.BlockSpec(memory_space=pltpu.HBM if i in hbm else space))
    args = [
        pltpu.with_memory_space_constraint(a, pltpu.HBM) if i in hbm else a
        for i, a in enumerate(args)
    ]
    shapes = [
        pltpu.HBM(s, d) if i in out_hbm else jax.ShapeDtypeStruct(s, d)
        for i, (s, d) in enumerate(outs)
    ]
    return pl.pallas_call(
        kernel,
        out_shape=shapes,
        in_specs=specs,
        out_specs=[pl.BlockSpec(memory_space=pltpu.VMEM) for _ in shapes],
        scratch_shapes=[pltpu.VMEM(*s) if isinstance(s, tuple) else s for s in scratch],
        compiler_params=pltpu.CompilerParams(vmem_limit_bytes=limit * 1024 * 1024),
        cost_estimate=pl.CostEstimate(flops=flops, bytes_accessed=moved, transcendentals=0),
    )(*args)


def exchange(x, axis, groups=None):
    return lax.all_to_all(
        x, axis, split_axis=0, concat_axis=0, tiled=True, axis_index_groups=groups
    )


def far_exchange(pieces, grid_x, grid_y):
    group = [(x, y) for x in range(grid_x) for y in range(grid_y)]
    got = [pieces[0]]
    for dy in range(1, grid_y):
        pairs = [(x * grid_y + y, x * grid_y + (y + dy) % grid_y) for x, y in group]
        got.append(lax.ppermute(pieces[dy], "group", pairs))
    ended = []
    for dx in range(grid_x):
        piece = jnp.concatenate([g[dx * 8 : (dx + 1) * 8] for g in got], axis=0)
        if dx:
            pairs = [(x * grid_y + y, (x + dx) % grid_x * grid_y + y) for x, y in group]
            piece = lax.ppermute(piece, "group", pairs)
        ended.append(piece)
    return ended


def make_body(grid_x, grid_y):
    def body(
        query_layer_input,
        query_frozen_base,
        passage_layer_input,
        passage_frozen_base,
        adapter_down_weight,
        adapter_up_weight,
        positive_passage_index,
        hard_negative_slots,
        group_peer_rows,
        remote_group_rows,
    ):
        n_dp = lax.axis_size("dp")
        n_group = lax.axis_size("group")
        rows, width = query_layer_input.shape
        rank = adapter_up_weight.shape[0]
        part = rank // 2
        queries = rows * n_dp * n_group
        slope = 16.0 / math.sqrt(queries) / logit_divisor
        g = lax.axis_index("group")
        place = jnp.stack([g // grid_y, g % grid_y, lax.axis_index("dp") % 2]).astype(jnp.int32)
        down_t = adapter_down_weight.T
        near_ids, far_ids = group_peer_rows.T, remote_group_rows.T
        per_near = group_peer_rows.shape[1]
        n_near = n_dp * per_near
        n_far = n_group * 2
        n_other = n_far + rows
        half = width // 2
        block = width // n_group
        near, *rest = call(
            lambda *refs: passage_kernel(grid_x, grid_y, *refs),
            [((n_near, width + lanes), bf16)]
            + [((grid_x * 8, half + lanes), bf16)] * grid_y
            + [
                ((rows, width), bf16),
                ((rows, lanes), bf16),
                ((rows, lanes), f32),
                ((n_near, rows), bf16),
            ],
            (
                place, passage_layer_input, passage_frozen_base, down_t, adapter_up_weight,
                near_ids, far_ids,
            ),
            [
                ((rows, width), bf16),
                ((rows, width), bf16),
                (down_t.shape, bf16),
                (adapter_up_weight.shape, bf16),
                (near_ids.shape, jnp.int32),
                (far_ids.shape, jnp.int32),
                ((rows, width), f32),
                pltpu.SemaphoreType.DMA((6,)),
            ],
            flops=400_000_000, moved=6_000_000, hbm=range(1, 7),
        )
        far, (p_unit, p_ext, p_inv, pick) = rest[:grid_y], rest[grid_y:]
        near = exchange(near.reshape(n_dp, per_near, width + lanes), "dp")
        near = near.reshape(n_near, width + lanes)
        far = far_exchange(far, grid_x, grid_y)
        q_unit, q_ext, q_inv, near_count, other_count = call(
            lambda *refs: query_kernel(grid_x, grid_y, *refs),
            [
                ((rows, width), bf16),
                ((rows, lanes), bf16),
                ((rows, lanes), f32),
                ((n_near, rows), f32),
                ((n_other, rows), f32),
            ],
            (
                place, query_layer_input, query_frozen_base, down_t, adapter_up_weight,
                hard_negative_slots.T,
            ),
            [((rows, width), f32)], flops=100_000_000, moved=3_000_000,
        )
        positive = positive_passage_index.reshape(1, rows)
        other, other_ext, x_far, other_raw = call(
            lambda *refs: far_kernel(grid_x, *refs),
            [
                ((n_other, width), bf16),
                ((n_other, lanes), bf16),
                ((n_far, width), bf16),
                ((n_other, rows), f32),
            ],
            (*far, q_unit, p_unit, p_ext, positive),
            flops=300_000_000, moved=4_000_000, out_hbm=(3,),
        )
        ret, near_g, other_g, near_radial, other_radial, q_radial = call(
            lambda *refs: score_kernel(slope, rank, *refs),
            [
                ((n_near, lanes), bf16),
                ((n_near, rows), bf16),
                ((n_other, rows), bf16),
                ((n_near, 1), f32),
                ((n_other, 1), f32),
                ((rows, 1), f32),
            ],
            (near, q_unit, other_raw, near_count, other_count, adapter_up_weight),
            [((n_other, rows), f32), pltpu.SemaphoreType.DMA(())],
            flops=300_000_000, moved=3_000_000, hbm=(2,),
        )
        ret = exchange(ret.reshape(n_dp, per_near, lanes), "dp").reshape(n_near, lanes)
        up_keep, up_send, down_part, row_part = call(
            local_kernel,
            [
                ((n_group, part, block), f32),
                ((n_group, part, block), bf16),
                ((rank, width), f32),
                ((rows, lanes), f32),
            ],
            (
                place, near, other, other_ext, x_far, q_unit, q_ext, q_inv, p_inv, query_layer_input,
                positive, near_g, other_g, near_radial, other_radial, q_radial, adapter_up_weight,
            ),
            flops=900_000_000, moved=9_000_000, out_hbm=(2, 3),
        )
        swap = [(i, i ^ 1) for i in range(n_dp)]
        up_got = lax.ppermute(up_send, "dp", swap)
        keep, send, loss = call(
            lambda *refs: down_kernel(per_near, *refs),
            [
                ((n_group, part, block), f32),
                ((n_group, part, block), bf16),
                ((8, lanes), f32),
            ],
            (place, ret, pick, row_part, passage_layer_input, down_part),
            [((rows, lanes), f32), ((rank, width), f32), pltpu.SemaphoreType.DMA((2,))],
            flops=100_000_000, moved=3_000_000, hbm=(3, 5),
        )
        got = lax.ppermute(send, "dp", swap)
        (sums,) = call(
            add_kernel,
            [((n_group, rank, block), bf16)],
            (keep, got, up_keep, up_got),
            moved=2_500_000,
        )
        cores = [list(range(c, n_dp, 2)) for c in range(2)]
        along_x = [[x * grid_y + y for x in range(grid_x)] for y in range(grid_y)]
        along_y = [[x * grid_y + y for y in range(grid_y)] for x in range(grid_x)]
        sums = exchange(sums.reshape(grid_x, grid_y, rank, block), "group", along_x)
        (sums,) = call(sum_kernel, [((grid_y, rank, block), bf16)], (sums,), moved=600_000)
        sums = exchange(sums, "group", along_y)
        (sums,) = call(
            spread_kernel, [((n_dp // 2, rank, block), bf16)], (sums,), moved=600_000
        )
        sums = exchange(sums, "dp", cores)
        (sums,) = call(
            finish_kernel, [((grid_y, rank + 8, block), bf16)], (sums, loss), moved=600_000
        )
        sums = exchange(sums, "group", along_y)
        (sums,) = call(
            copy_kernel, [((grid_x, grid_y, rank + 8, block), bf16)], (sums,), moved=600_000
        )
        sums = exchange(sums, "group", along_x)
        other_sums = lax.ppermute(sums, "dp", swap)
        down, up, loss = call(
            lambda *refs: output_kernel(queries, *refs),
            [((rank, width), f32), ((rank, width), f32), ((1, 1), f32)],
            (place, sums, other_sums),
            moved=3_500_000,
        )
        return (down.T, up, loss.reshape(()))

    return body


def solution(mesh):
    n_group = mesh.shape["group"]
    grid_x = {32: 4, 4: 2}[n_group]
    both = P(("dp", "group"), None)
    placed = (both, both, both, both, P(), P(), P(("dp", "group")), both, both, both)
    return jax.shard_map(
        make_body(grid_x, n_group // grid_x),
        mesh=mesh,
        in_specs=placed,
        out_specs=(P(), P(), P()),
        check_vma=False,
    )
```

```python
import math

import jax
import jax.numpy as jnp
from jax import lax
from jax.experimental import pallas as pl
from jax.experimental.pallas import tpu as pltpu
from jax.sharding import PartitionSpec as P

f32 = jnp.float32
bf16 = jnp.bfloat16
adapter_scale = 2.0
logit_divisor = 0.05
epsilon = 1e-06
offset = 1.0 / logit_divisor
tile = 512
lanes = 128


def dot(a, b, ca=1, cb=0):
    return lax.dot_general(a, b, (((ca,), (cb,)), ((), ())), preferred_element_type=f32)


def iota(shape, dim):
    return lax.broadcasted_iota(jnp.int32, shape, dim)


def eye(n, m):
    return (iota((n, m), 0) == iota((n, m), 1)).astype(bf16)


def flip(a):
    return dot(eye(a.shape[1], a.shape[1]), a, 1, 1).astype(bf16)


def column_tiles(width):
    step = min(tile, width)
    return [slice(c, c + step) for c in range(0, width, step)]


def embed(x_ref, base_ref, down_ref, up_ref, unit_ref, ext_ref, inv_ref, raw_ref, ready=None):
    rows, width = x_ref.shape
    rank = up_ref.shape[0]
    latent = dot(x_ref[...], down_ref[...], 1, 1).astype(bf16)
    if ready is not None:
        ready()
    squares = jnp.zeros((rows, 1), f32)
    for cols in column_tiles(width):
        raw = base_ref[:, cols].astype(f32) + adapter_scale * dot(latent, up_ref[:, cols])
        raw_ref[:, cols] = raw
        squares = squares + jnp.sum(raw * raw, axis=1, keepdims=True)
    inverse = lax.rsqrt(squares + epsilon)
    for cols in column_tiles(width):
        unit_ref[0:rows, cols] = (raw_ref[:, cols] * inverse).astype(bf16)
    scaled = (latent.astype(f32) * inverse).astype(bf16)
    high = inverse.astype(bf16).astype(f32)
    lane = iota((rows, lanes), 1)
    ext = dot(scaled, eye(rank, lanes))
    ext = jnp.where(lane == rank, high, ext)
    ext = jnp.where(lane == rank + 1, inverse - high, ext)
    ext_ref[...] = ext.astype(bf16)
    inv_ref[...] = jnp.broadcast_to(inverse, inv_ref.shape)


def fetch(pairs, sems):
    copies = [pltpu.make_async_copy(a, b, sems.at[i]) for i, (a, b) in enumerate(pairs)]
    for c in copies:
        c.start()
    return copies


def passage_kernel(
    x_hbm, base_hbm, down_hbm, up_hbm, near_ids_hbm,
    near_hbm, unit_ref, ext_ref, inv_ref, pick_ref,
    x_ref, base_ref, down_ref, up_ref, near_ids_ref, raw_ref, near_ref, sems, out_sems,
):
    pairs = [
        (x_hbm, x_ref), (down_hbm, down_ref), (base_hbm, base_ref), (up_hbm, up_ref),
        (near_ids_hbm, near_ids_ref),
    ]
    copies = fetch(pairs, sems)
    copies[0].wait()
    copies[1].wait()

    def ready():
        copies[2].wait()
        copies[3].wait()

    embed(x_ref, base_ref, down_ref, up_ref, unit_ref, ext_ref, inv_ref, raw_ref, ready)
    copies[4].wait()
    rows, width = x_ref.shape
    per_near, n_near = near_ids_ref.shape
    count = per_near * n_near
    ids = near_ids_ref[...].astype(f32).astype(bf16)
    spread = (iota((count, n_near), 0) // per_near == iota((count, n_near), 1)).astype(bf16)
    table = dot(spread, ids, 1, 1)
    mine = iota((count, per_near), 0) % per_near == iota((count, per_near), 1)
    wanted = jnp.sum(jnp.where(mine, table, 0.0), axis=1, keepdims=True).astype(jnp.int32)
    pick = (iota((count, rows), 1) == wanted).astype(bf16)
    pick_ref[...] = pick
    near_ref[:, width:] = dot(pick, ext_ref[...]).astype(bf16)
    sent = []
    for i, cols in enumerate([slice(width, width + lanes), *column_tiles(width)]):
        if i:
            near_ref[:, cols] = dot(pick, unit_ref[:, cols]).astype(bf16)
        copy = pltpu.make_async_copy(near_ref.at[:, cols], near_hbm.at[:, cols], out_sems.at[i])
        copy.start()
        sent.append(copy)
    for copy in sent:
        copy.wait()


def far_pick_kernel(grid_x, grid_y, place_ref, x_ref, unit_ref, ext_ref, far_ids_ref, *far_refs):
    rows, width = x_ref.shape
    half = width // 2
    n_far = far_ids_ref.shape[1]
    total = n_far * 8
    size = grid_x * 8
    where_x, where_y = place_ref[0], place_ref[1]
    ids = far_ids_ref[...].astype(f32).astype(bf16)
    block = iota((total, n_far), 0) // 8
    to_x = (where_x + block % grid_x) % grid_x
    to_y = (where_y + block // grid_x) % grid_y
    spread = (to_x * grid_y + to_y == iota((total, n_far), 1)).astype(bf16)
    table = dot(spread, ids, 1, 1)
    mine = iota((total, 2), 0) % 2 == iota((total, 2), 1)
    wanted = jnp.sum(jnp.where(mine, table, 0.0), axis=1, keepdims=True).astype(jnp.int32)
    kind = (iota((total, 4 * rows), 0) // 2) % 4
    source = iota((total, 4 * rows), 1)
    choose = ((source // rows == kind) & (source % rows == wanted)).astype(bf16)
    for cols in column_tiles(half):
        later = slice(half + cols.start, half + cols.stop)
        stack = jnp.concatenate(
            [unit_ref[:, cols], unit_ref[:, later], x_ref[:, cols], x_ref[:, later]], axis=0
        )
        got = dot(choose, stack).astype(bf16)
        for dy in range(grid_y):
            far_refs[dy][:, cols] = got[dy * size : (dy + 1) * size]
    first = jnp.where(iota((total, rows), 0) // 2 % 4 == 0, wanted, -1)
    got = dot((iota((total, rows), 1) == first).astype(bf16), ext_ref[...]).astype(bf16)
    for dy in range(grid_y):
        far_refs[dy][:, half:] = got[dy * size : (dy + 1) * size]


def query_kernel(
    grid_x, grid_y, place_ref, x_ref, base_ref, down_ref, up_ref, slots_ref,
    pair_ref, ext_ref, inv_ref, near_count_ref, other_count_ref, shadow_ref, raw_ref,
):
    hard, rows = slots_ref.shape
    embed(x_ref, base_ref, down_ref, up_ref, pair_ref, ext_ref, inv_ref, raw_ref)
    pair_ref[rows:, :] = up_ref[...]
    product = dot(pair_ref[0:rows, :], up_ref[...], 1, 1)
    high = product.astype(bf16)
    shadow_ref[0:rows, :] = high
    shadow_ref[rows:, :] = (product - high.astype(f32)).astype(bf16)
    n_near = near_count_ref.shape[0]
    n_other = other_count_ref.shape[0]
    n_far = n_other - rows
    where_x, where_y = place_ref[0], place_ref[1]
    near_slot = iota((n_near, rows), 0)
    spot = iota((n_other, rows), 0)
    block = spot // 2
    from_x = (where_x + grid_x - (block // grid_y) % grid_x) % grid_x
    from_y = (where_y + grid_y - block % grid_y) % grid_y
    far_slot = n_near + (from_x * grid_y + from_y) * 2 + spot % 2
    far_slot = jnp.where(spot < n_far, far_slot, -1)
    near_count = jnp.zeros((n_near, rows), f32)
    other_count = jnp.zeros((n_other, rows), f32)
    for k in range(hard):
        slot = slots_ref[k : k + 1, :]
        near_count = near_count + (near_slot == slot).astype(f32)
        other_count = other_count + (far_slot == slot).astype(f32)
    near_count_ref[...] = near_count
    other_count_ref[...] = jnp.where(spot < n_far, other_count, 1.0)


def store_blocks(ref, cols, value):
    size = ref.shape[2]
    step = min(size, cols.stop - cols.start)
    for c in range(cols.start, cols.stop, step):
        at = c % size
        ref[c // size, :, at : at + step] = value[:, c - cols.start : c - cols.start + step]


def load_blocks(ref, cols):
    size = ref.shape[2]
    step = min(size, cols.stop - cols.start)
    parts = []
    for c in range(cols.start, cols.stop, step):
        parts.append(ref[c // size, :, c % size : c % size + step])
    return parts[0] if len(parts) == 1 else jnp.concatenate(parts, axis=1)


def regroup_kernel(*refs):
    size = 8
    count = refs[0].shape[0] // size
    n_in = len(refs) - count
    for dx in range(0, count, 2):
        for dy in range(0, n_in, 2):
            a, b = [refs[dy + i][dx * size : (dx + 2) * size, :] for i in range(2)]
            at = slice(dy * size, (dy + 2) * size)
            refs[n_in + dx][at, :] = jnp.concatenate([a[:size], b[:size]], axis=0)
            refs[n_in + dx + 1][at, :] = jnp.concatenate([a[size:], b[size:]], axis=0)


def far_kernel(count, *refs):
    far_refs = refs[:count]
    q_ref, unit_ref, p_ext_ref, positive_ref = refs[count : count + 4]
    o_ref, ext_ref, x_far_ref, raw_ref = refs[count + 4 :]
    rows, width = unit_ref.shape
    half = width // 2
    total = far_refs[0].shape[0]
    each = total // 4
    n_far = each * count
    out_row = iota((total, total), 0)
    in_row = iota((total, total), 1)
    spot = out_row % each
    undo = (
        (in_row // 8 == spot // 2)
        & (in_row % 2 == spot % 2)
        & ((in_row // 2) % 4 == out_row // each)
    ).astype(bf16)
    for i, far_ref in enumerate(far_refs):
        at = slice(i * each, (i + 1) * each)
        for cols in column_tiles(half):
            later = slice(half + cols.start, half + cols.stop)
            got = dot(undo, far_ref[:, cols]).astype(bf16)
            o_ref[at, cols] = got[0:each]
            o_ref[at, later] = got[each : 2 * each]
            x_far_ref[at, cols] = got[2 * each : 3 * each]
            x_far_ref[at, later] = got[3 * each :]
        ext_ref[at, :] = dot(undo[0:each], far_ref[:, half:]).astype(bf16)
    own = (iota((rows, rows), 0) == positive_ref[...]).astype(bf16)
    own_t = flip(own)
    for cols in column_tiles(width):
        o_ref[n_far:, cols] = dot(own_t, unit_ref[:, cols]).astype(bf16)
    ext_ref[n_far:, :] = dot(own_t, p_ext_ref[...]).astype(bf16)
    raw_ref[...] = dot(o_ref[...], q_ref[0:rows, :], 1, 1)


def score_kernel(
    slope, rank, near_ref, pair_ref, other_raw_hbm, near_count_ref, other_count_ref, shadow_ref,
    ret_ref, g_ref, radial_ref, other_raw_ref, sem,
):
    copy = pltpu.make_async_copy(other_raw_hbm, other_raw_ref, sem)
    copy.start()
    width = pair_ref.shape[1]
    n_near, rows = near_count_ref.shape
    both = dot(near_ref[:, :width], pair_ref[...], 1, 1)
    near_raw, near_up = both[:, 0:rows], both[:, rows:]
    copy.wait()
    other_raw = other_raw_ref[...]
    n_other = other_raw.shape[0]
    n_far = n_other - rows
    near_exp = jnp.exp(near_raw / logit_divisor - offset) * near_count_ref[...]
    other_exp = jnp.exp(other_raw / logit_divisor - offset) * other_count_ref[...]
    partition = jnp.sum(near_exp, axis=0, keepdims=True) + jnp.sum(
        other_exp, axis=0, keepdims=True
    )
    same = iota(other_raw.shape, 0) == iota(other_raw.shape, 1) + n_far
    matched = jnp.sum(jnp.where(same, other_raw, 0.0), axis=0, keepdims=True) / logit_divisor
    loss = jnp.sum(jnp.log(partition) + offset - matched, axis=1, keepdims=True)
    near_g = (near_exp / partition * slope).astype(bf16)
    other_g = ((other_exp / partition - same.astype(f32)) * slope).astype(bf16)
    g_ref[0:n_near, :] = near_g
    g_ref[n_near:, :] = other_g
    near_part = near_g.astype(f32) * near_raw
    other_part = other_g.astype(f32) * other_raw
    near_radial = jnp.sum(near_part, axis=1, keepdims=True)
    radial_ref[0:n_near, :] = near_radial
    radial_ref[n_near : n_near + n_other, :] = jnp.sum(other_part, axis=1, keepdims=True)
    q_radial = jnp.sum(near_part, axis=0, keepdims=True) + jnp.sum(
        other_part, axis=0, keepdims=True
    )
    square = iota((rows, rows), 0) == iota((rows, rows), 1)
    radial_ref[n_near + n_other :, :] = jnp.sum(
        jnp.where(square, q_radial, 0.0), axis=1, keepdims=True
    )
    back = dot(near_g, shadow_ref[0:rows, :]) + dot(near_g, shadow_ref[rows:, :])
    back = back - near_radial * near_up
    back = dot(back.astype(bf16), eye(rank, lanes))
    lane = iota((n_near, lanes), 1)
    high = loss.astype(bf16).astype(f32)
    back = jnp.where(lane == rank, high, back)
    back = jnp.where(lane == rank + 1, loss - high, back)
    ret_ref[...] = back.astype(bf16)


def local_kernel(
    near_ref, pair_ref, o_hbm, o_ext_hbm, x_far_hbm, q_ext_hbm, q_inv_hbm, p_inv_hbm, x_q_hbm,
    positive_hbm, g_hbm, radial_hbm, place_hbm,
    up_keep_ref, up_send_ref, down_ref, row_ref,
    o_ref, o_ext_ref, x_far_ref, q_ext_ref, q_inv_ref, p_inv_ref, x_q_ref, positive_ref, g_ref,
    radial_ref, place_ref, sems,
):
    pairs = [
        (g_hbm, g_ref), (radial_hbm, radial_ref), (o_hbm, o_ref), (o_ext_hbm, o_ext_ref),
        (q_ext_hbm, q_ext_ref), (place_hbm, place_ref), (positive_hbm, positive_ref),
        (q_inv_hbm, q_inv_ref), (p_inv_hbm, p_inv_ref), (x_far_hbm, x_far_ref), (x_q_hbm, x_q_ref),
    ]
    copies = fetch(pairs, sems)
    for c in copies[:6]:
        c.wait()
    rows, width = x_q_ref.shape
    rank = pair_ref.shape[0] - rows
    part = rank // 2
    n_near = near_ref.shape[0]
    n_far = o_ref.shape[0] - rows
    n_all = n_near + n_far + rows
    even = place_ref[0:1, 2:3] == 0
    near_gt, other_gt = g_ref[0:n_near, :], g_ref[n_near:, :]
    near_g, other_g = flip(near_gt), flip(other_gt)
    near_radial = radial_ref[0:n_near, :]
    other_radial = radial_ref[n_near:n_all, :]
    q_radial = radial_ref[n_all:, :]
    q_lat = flip(q_ext_ref[...])[0:rank]
    near_lat = flip(near_ref[:, width:])[0:rank]
    other_lat = flip(o_ext_ref[...])[0:rank]
    q_back = jnp.zeros((rows, rank), f32)
    other_back = jnp.zeros((n_far + rows, rank), f32)
    for cols in column_tiles(width):
        q = pair_ref[0:rows, cols]
        near = near_ref[:, cols]
        other = o_ref[:, cols]
        up = pair_ref[rows:, cols]
        q_t = dot(near_g, near) + dot(other_g, other) - q.astype(f32) * q_radial
        near_t = dot(near_gt, q) - near.astype(f32) * near_radial
        other_t = dot(other_gt, q) - other.astype(f32) * other_radial
        q_t, near_t, other_t = q_t.astype(bf16), near_t.astype(bf16), other_t.astype(bf16)
        q_back = q_back + dot(q_t, up, 1, 1)
        other_back = other_back + dot(other_t, up, 1, 1)
        grad = dot(q_lat, q_t) + dot(near_lat, near_t) + dot(other_lat, other_t)
        grad = adapter_scale * grad
        top, low = grad[0:part], grad[part:]
        store_blocks(up_keep_ref, cols, jnp.where(even, top, low))
        store_blocks(up_send_ref, cols, jnp.where(even, low, top).astype(bf16))
    for c in copies[6:]:
        c.wait()
    other_back = other_back.astype(bf16)
    own = (iota((rows, rows), 0) == positive_ref[...]).astype(bf16)
    wide = dot(other_back[n_far:], eye(rank, lanes)).astype(bf16)
    row_sum = dot(own, wide)
    row_ref[...] = jnp.where(iota(row_sum.shape, 1) < rank, row_sum, p_inv_ref[...])
    q_back = q_back.astype(bf16).astype(f32)
    dz_q = (adapter_scale * q_inv_ref[:, 0:1] * q_back).astype(bf16)
    far_ext = o_ext_ref[0:n_far, :].astype(f32)
    far_inv = far_ext[:, rank : rank + 1] + far_ext[:, rank + 1 : rank + 2]
    dz_f = (adapter_scale * far_inv * other_back[0:n_far].astype(f32)).astype(bf16)
    dz_qt, dz_ft = flip(dz_q), flip(dz_f)
    for cols in column_tiles(width):
        down_ref[:, cols] = dot(dz_qt, x_q_ref[:, cols]) + dot(dz_ft, x_far_ref[:, cols])


def down_kernel(
    per_near, place_ref, ret_ref, pick_ref, row_hbm, x_p_ref, down_hbm,
    keep_ref, send_ref, loss_ref, row_ref, down_ref, sems,
):
    row_copy = pltpu.make_async_copy(row_hbm, row_ref, sems.at[0])
    down_copy = pltpu.make_async_copy(down_hbm, down_ref, sems.at[1])
    row_copy.start()
    down_copy.start()
    rank = down_ref.shape[0]
    part = rank // 2
    ret = ret_ref[...]
    row_sum = dot(flip(pick_ref[...]), ret)[:, 0:rank]
    row_copy.wait()
    row_sum = row_sum + row_ref[:, 0:rank]
    dz_t = flip((adapter_scale * row_ref[:, rank : rank + 1] * row_sum).astype(bf16))
    down_copy.wait()
    even = place_ref[2] == 0
    for cols in column_tiles(x_p_ref.shape[1]):
        grad = dot(dz_t, x_p_ref[:, cols]) + down_ref[:, cols]
        top, low = grad[0:part], grad[part:]
        store_blocks(keep_ref, cols, jnp.where(even, top, low))
        store_blocks(send_ref, cols, jnp.where(even, low, top).astype(bf16))
    first = iota(ret.shape, 0) % per_near == 0
    lane = iota(ret.shape, 1)
    chosen = first & ((lane == rank) | (lane == rank + 1))
    share = jnp.sum(jnp.where(chosen, ret.astype(f32), 0.0), axis=1, keepdims=True)
    loss_ref[...] = jnp.broadcast_to(jnp.sum(share, axis=0, keepdims=True), loss_ref.shape)


def add_kernel(down_ref, got_down_ref, up_ref, got_up_ref, out_ref):
    part = down_ref.shape[1]
    for i in range(down_ref.shape[0]):
        out_ref[i, 0:part] = (down_ref[i] + got_down_ref[i].astype(f32)).astype(bf16)
        out_ref[i, part:] = (up_ref[i] + got_up_ref[i].astype(f32)).astype(bf16)


def sum_blocks(ref, *at):
    acc = ref[(0, *at)].astype(f32)
    for i in range(1, ref.shape[0]):
        acc = acc + ref[(i, *at)].astype(f32)
    return acc


def spread_kernel(in_ref, out_ref):
    value = sum_blocks(in_ref).astype(bf16)
    for i in range(out_ref.shape[0]):
        out_ref[i] = value


def finish_kernel(in_ref, loss_ref, out_ref):
    loss = loss_ref[...]
    high = loss.astype(bf16).astype(f32)
    row = iota(loss.shape, 0)
    tail = jnp.where(row == 0, high, jnp.where(row == 1, loss - high, 0.0))
    if out_ref.shape[2] > lanes:
        tail = jnp.concatenate([tail] * (out_ref.shape[2] // lanes), axis=1)
    value = jnp.concatenate([sum_blocks(in_ref), tail], axis=0).astype(bf16)
    for i in range(out_ref.shape[0]):
        out_ref[i] = value


def output_kernel(queries, place_ref, mine_ref, other_ref, down_ref, up_ref, loss_ref):
    rank = down_ref.shape[0]
    part = rank // 2
    size = mine_ref.shape[2]
    even = place_ref[2] == 0
    loss = jnp.zeros((8, lanes), f32)
    for i in range(mine_ref.shape[0]):
        mine, other = mine_ref[i].astype(f32), other_ref[i].astype(f32)
        cols = slice(i * size, (i + 1) * size)
        top = jnp.where(even, mine[0:rank], other[0:rank])
        low = jnp.where(even, other[0:rank], mine[0:rank])
        down_ref[0:part, cols] = top[0:part]
        down_ref[part:, cols] = low[0:part]
        up_ref[0:part, cols] = top[part:]
        up_ref[part:, cols] = low[part:]
        loss = loss + mine[rank:, 0:lanes]
    loss_ref[...] = jnp.sum(loss, axis=0, keepdims=True)[:, 0:1] / queries


def call(kernel, outs, args, scratch=(), flops=0, moved=0, hbm=(), out_hbm=(), out_raw=(), limit=16):
    specs = []
    for i, a in enumerate(args):
        space = pltpu.SMEM if a.dtype == jnp.int32 and a.ndim == 1 else pltpu.VMEM
        specs.append(pl.BlockSpec(memory_space=pltpu.HBM if i in hbm else space))
    args = [
        pltpu.with_memory_space_constraint(a, pltpu.HBM) if i in hbm else a
        for i, a in enumerate(args)
    ]
    shapes = [
        pltpu.HBM(s, d) if i in out_hbm else jax.ShapeDtypeStruct(s, d)
        for i, (s, d) in enumerate(outs)
    ]
    return pl.pallas_call(
        kernel,
        out_shape=shapes,
        in_specs=specs,
        out_specs=[
            pl.BlockSpec(memory_space=pltpu.HBM if i in out_raw else pltpu.VMEM)
            for i in range(len(shapes))
        ],
        scratch_shapes=[pltpu.VMEM(*s) if isinstance(s, tuple) else s for s in scratch],
        compiler_params=pltpu.CompilerParams(vmem_limit_bytes=limit * 1024 * 1024),
        cost_estimate=pl.CostEstimate(flops=flops, bytes_accessed=moved, transcendentals=0),
    )(*args)


def exchange(x, axis, groups=None):
    return lax.all_to_all(
        x, axis, split_axis=0, concat_axis=0, tiled=True, axis_index_groups=groups
    )


def far_exchange(pieces, grid_x, grid_y):
    group = [(x, y) for x in range(grid_x) for y in range(grid_y)]
    got = [pieces[0]]
    for dy in range(1, grid_y):
        pairs = [(x * grid_y + y, x * grid_y + (y + dy) % grid_y) for x, y in group]
        got.append(lax.ppermute(pieces[dy], "group", pairs))
    lines = call(regroup_kernel, [((grid_y * 8, got[0].shape[1]), bf16)] * grid_x, got, moved=1000)
    ended = []
    for dx, piece in enumerate(lines):
        if dx:
            pairs = [(x * grid_y + y, (x + dx) % grid_x * grid_y + y) for x, y in group]
            piece = lax.ppermute(piece, "group", pairs)
        ended.append(piece)
    return ended


def make_body(grid_x, grid_y):
    def body(
        query_layer_input,
        query_frozen_base,
        passage_layer_input,
        passage_frozen_base,
        adapter_down_weight,
        adapter_up_weight,
        positive_passage_index,
        hard_negative_slots,
        group_peer_rows,
        remote_group_rows,
    ):
        n_dp = lax.axis_size("dp")
        n_group = lax.axis_size("group")
        rows, width = query_layer_input.shape
        rank = adapter_up_weight.shape[0]
        part = rank // 2
        queries = rows * n_dp * n_group
        slope = 16.0 / math.sqrt(queries) / logit_divisor
        g = lax.axis_index("group")
        place = jnp.stack([g // grid_y, g % grid_y, lax.axis_index("dp") % 2]).astype(jnp.int32)
        down_t = adapter_down_weight.T
        near_ids, far_ids = group_peer_rows.T, remote_group_rows.T
        per_near = group_peer_rows.shape[1]
        n_near = n_dp * per_near
        n_far = n_group * 2
        n_other = n_far + rows
        half = width // 2
        block = width // n_group
        near, p_unit, p_ext, p_inv, pick = call(
            passage_kernel,
            [
                ((n_near, width + lanes), bf16),
                ((rows, width), bf16),
                ((rows, lanes), bf16),
                ((rows, lanes), f32),
                ((n_near, rows), bf16),
            ],
            (passage_layer_input, passage_frozen_base, down_t, adapter_up_weight, near_ids),
            [
                ((rows, width), bf16),
                ((rows, width), bf16),
                (down_t.shape, bf16),
                (adapter_up_weight.shape, bf16),
                (near_ids.shape, jnp.int32),
                ((rows, width), f32),
                ((n_near, width + lanes), bf16),
                pltpu.SemaphoreType.DMA((5,)),
                pltpu.SemaphoreType.DMA((1 + len(column_tiles(width)),)),
            ],
            flops=300_000_000, moved=5_000_000, hbm=range(5), out_hbm=(0, 3), out_raw=(0,),
        )
        far = call(
            lambda *refs: far_pick_kernel(grid_x, grid_y, *refs),
            [((grid_x * 8, half + lanes), bf16)] * grid_y,
            (place, passage_layer_input, p_unit, p_ext, far_ids),
            flops=1000, moved=1000,
        )
        near = exchange(near.reshape(n_dp, per_near, width + lanes), "dp")
        near = near.reshape(n_near, width + lanes)
        far = far_exchange(far, grid_x, grid_y)
        q_pair, q_ext, q_inv, near_count, other_count, shadow = call(
            lambda *refs: query_kernel(grid_x, grid_y, *refs),
            [
                ((rows + rank, width), bf16),
                ((rows, lanes), bf16),
                ((rows, lanes), f32),
                ((n_near, rows), f32),
                ((n_other, rows), f32),
                ((2 * rows, rank), bf16),
            ],
            (
                place, query_layer_input, query_frozen_base, down_t, adapter_up_weight,
                hard_negative_slots.T,
            ),
            [((rows, width), f32)], flops=1000, moved=1000, out_hbm=(1, 2),
        )
        positive = positive_passage_index.reshape(1, rows)
        other, other_ext, x_far, other_raw = call(
            lambda *refs: far_kernel(grid_x, *refs),
            [
                ((n_other, width), bf16),
                ((n_other, lanes), bf16),
                ((n_far, width), bf16),
                ((n_other, rows), f32),
            ],
            (*far, q_pair, p_unit, p_ext, positive),
            flops=1000, moved=1000, out_hbm=range(4),
        )
        ret, weights, radial = call(
            lambda *refs: score_kernel(slope, rank, *refs),
            [
                ((n_near, lanes), bf16),
                ((n_near + n_other, rows), bf16),
                ((n_near + n_other + rows, 1), f32),
            ],
            (near, q_pair, other_raw, near_count, other_count, shadow),
            [((n_other, rows), f32), pltpu.SemaphoreType.DMA(())],
            flops=200_000_000, moved=3_000_000, hbm=(2,), out_hbm=(1, 2),
        )
        ret = exchange(ret.reshape(n_dp, per_near, lanes), "dp").reshape(n_near, lanes)
        up_keep, up_send, down_part, row_part = call(
            local_kernel,
            [
                ((n_group, part, block), f32),
                ((n_group, part, block), bf16),
                ((rank, width), f32),
                ((rows, lanes), f32),
            ],
            (
                near, q_pair, other, other_ext, x_far, q_ext, q_inv, p_inv, query_layer_input,
                positive, weights, radial, place.reshape(1, 3),
            ),
            [
                ((n_other, width), bf16),
                ((n_other, lanes), bf16),
                ((n_far, width), bf16),
                ((rows, lanes), bf16),
                ((rows, lanes), f32),
                ((rows, lanes), f32),
                ((rows, width), bf16),
                ((1, rows), jnp.int32),
                (weights.shape, bf16),
                (radial.shape, f32),
                ((1, 3), jnp.int32),
                pltpu.SemaphoreType.DMA((11,)),
            ],
            flops=900_000_000, moved=9_000_000, hbm=range(2, 13), out_hbm=(2, 3),
        )
        swap = [(i, i ^ 1) for i in range(n_dp)]
        up_got = lax.ppermute(up_send, "dp", swap)
        keep, send, loss = call(
            lambda *refs: down_kernel(per_near, *refs),
            [
                ((n_group, part, block), f32),
                ((n_group, part, block), bf16),
                ((8, lanes), f32),
            ],
            (place, ret, pick, row_part, passage_layer_input, down_part),
            [((rows, lanes), f32), ((rank, width), f32), pltpu.SemaphoreType.DMA((2,))],
            flops=100_000_000, moved=3_000_000, hbm=(3, 5),
        )
        got = lax.ppermute(send, "dp", swap)
        (sums,) = call(
            add_kernel,
            [((n_group, rank, block), bf16)],
            (keep, got, up_keep, up_got),
            moved=2_500_000,
        )
        cores = [list(range(c, n_dp, 2)) for c in range(2)]
        sums = exchange(sums, "group")
        (sums,) = call(
            spread_kernel, [((n_dp // 2, rank, block), bf16)], (sums,), moved=1_000_000
        )
        sums = exchange(sums, "dp", cores)
        (sums,) = call(
            finish_kernel, [((n_group, rank + 8, block), bf16)], (sums, loss), moved=1_000_000
        )
        sums = exchange(sums, "group")
        other_sums = lax.ppermute(sums, "dp", swap)
        down, up, loss = call(
            lambda *refs: output_kernel(queries, *refs),
            [((rank, width), f32), ((rank, width), f32), ((1, 1), f32)],
            (place, sums, other_sums),
            moved=3_500_000,
        )
        return (down.T, up, loss.reshape(()))

    return body


def solution(mesh):
    n_group = mesh.shape["group"]
    grid_x = {32: 4, 4: 2}[n_group]
    both = P(("dp", "group"), None)
    placed = (both, both, both, both, P(), P(), P(("dp", "group")), both, both, both)
    return jax.shard_map(
        make_body(grid_x, n_group // grid_x),
        mesh=mesh,
        in_specs=placed,
        out_specs=(P(), P(), P()),
        check_vma=False,
    )
```

```python
import math

import jax
import jax.numpy as jnp
from jax import lax
from jax.experimental import pallas as pl
from jax.experimental.pallas import tpu as pltpu
from jax.sharding import PartitionSpec as P

f32 = jnp.float32
bf16 = jnp.bfloat16
adapter_scale = 2.0
logit_divisor = 0.05
epsilon = 1e-06
offset = 1.0 / logit_divisor
tile = 512
lanes = 128


def dot(a, b, ca=1, cb=0):
    return lax.dot_general(a, b, (((ca,), (cb,)), ((), ())), preferred_element_type=f32)


def iota(shape, dim):
    return lax.broadcasted_iota(jnp.int32, shape, dim)


def eye(n, m):
    return (iota((n, m), 0) == iota((n, m), 1)).astype(bf16)


def flip(a):
    return dot(eye(a.shape[1], a.shape[1]), a, 1, 1).astype(bf16)


def column_tiles(width):
    step = min(tile, width)
    return [slice(c, c + step) for c in range(0, width, step)]


def embed(x_ref, base_ref, down_ref, up_ref, unit_ref, ext_ref, inv_ref, raw_ref, ready=None):
    rows, width = x_ref.shape
    rank = up_ref.shape[0]
    latent = dot(x_ref[...], down_ref[...], 1, 1).astype(bf16)
    if ready is not None:
        ready()
    squares = jnp.zeros((rows, 1), f32)
    for cols in column_tiles(width):
        raw = base_ref[:, cols].astype(f32) + adapter_scale * dot(latent, up_ref[:, cols])
        raw_ref[:, cols] = raw
        squares = squares + jnp.sum(raw * raw, axis=1, keepdims=True)
    inverse = lax.rsqrt(squares + epsilon)
    for cols in column_tiles(width):
        unit_ref[0:rows, cols] = (raw_ref[:, cols] * inverse).astype(bf16)
    scaled = (latent.astype(f32) * inverse).astype(bf16)
    high = inverse.astype(bf16).astype(f32)
    lane = iota((rows, lanes), 1)
    ext = dot(scaled, eye(rank, lanes))
    ext = jnp.where(lane == rank, high, ext)
    ext = jnp.where(lane == rank + 1, inverse - high, ext)
    ext_ref[...] = ext.astype(bf16)
    inv_ref[...] = jnp.broadcast_to(inverse, inv_ref.shape)


def fetch(pairs, sems):
    copies = [pltpu.make_async_copy(a, b, sems.at[i]) for i, (a, b) in enumerate(pairs)]
    for c in copies:
        c.start()
    return copies


def passage_kernel(
    x_hbm, base_hbm, down_hbm, up_hbm, near_ids_hbm,
    near_hbm, unit_ref, ext_ref, inv_ref, pick_ref,
    x_ref, base_ref, down_ref, up_ref, near_ids_ref, raw_ref, near_ref, sems, out_sems,
):
    pairs = [
        (x_hbm, x_ref), (down_hbm, down_ref), (base_hbm, base_ref), (up_hbm, up_ref),
        (near_ids_hbm, near_ids_ref),
    ]
    copies = fetch(pairs, sems)
    copies[0].wait()
    copies[1].wait()

    def ready():
        copies[2].wait()
        copies[3].wait()

    embed(x_ref, base_ref, down_ref, up_ref, unit_ref, ext_ref, inv_ref, raw_ref, ready)
    copies[4].wait()
    rows, width = x_ref.shape
    per_near, n_near = near_ids_ref.shape
    count = per_near * n_near
    ids = near_ids_ref[...].astype(f32).astype(bf16)
    spread = (iota((count, n_near), 0) // per_near == iota((count, n_near), 1)).astype(bf16)
    table = dot(spread, ids, 1, 1)
    mine = iota((count, per_near), 0) % per_near == iota((count, per_near), 1)
    wanted = jnp.sum(jnp.where(mine, table, 0.0), axis=1, keepdims=True).astype(jnp.int32)
    pick = (iota((count, rows), 1) == wanted).astype(bf16)
    pick_ref[...] = pick
    near_ref[:, width:] = dot(pick, ext_ref[...]).astype(bf16)
    sent = []
    for i, cols in enumerate([slice(width, width + lanes), *column_tiles(width)]):
        if i:
            near_ref[:, cols] = dot(pick, unit_ref[:, cols]).astype(bf16)
        copy = pltpu.make_async_copy(near_ref.at[:, cols], near_hbm.at[:, cols], out_sems.at[i])
        copy.start()
        sent.append(copy)
    for copy in sent:
        copy.wait()


def far_pick_kernel(grid_x, grid_y, place_ref, x_ref, unit_ref, ext_ref, far_ids_ref, *far_refs):
    rows, width = x_ref.shape
    half = width // 2
    n_far = far_ids_ref.shape[1]
    total = n_far * 8
    size = grid_x * 8
    where_x, where_y = place_ref[0], place_ref[1]
    ids = far_ids_ref[...].astype(f32).astype(bf16)
    block = iota((total, n_far), 0) // 8
    to_x = (where_x + block % grid_x) % grid_x
    to_y = (where_y + block // grid_x) % grid_y
    spread = (to_x * grid_y + to_y == iota((total, n_far), 1)).astype(bf16)
    table = dot(spread, ids, 1, 1)
    mine = iota((total, 2), 0) % 2 == iota((total, 2), 1)
    wanted = jnp.sum(jnp.where(mine, table, 0.0), axis=1, keepdims=True).astype(jnp.int32)
    kind = (iota((total, 4 * rows), 0) // 2) % 4
    source = iota((total, 4 * rows), 1)
    choose = ((source // rows == kind) & (source % rows == wanted)).astype(bf16)
    for cols in column_tiles(half):
        later = slice(half + cols.start, half + cols.stop)
        stack = jnp.concatenate(
            [unit_ref[:, cols], unit_ref[:, later], x_ref[:, cols], x_ref[:, later]], axis=0
        )
        got = dot(choose, stack).astype(bf16)
        for dy in range(grid_y):
            far_refs[dy][:, cols] = got[dy * size : (dy + 1) * size]
    first = jnp.where(iota((total, rows), 0) // 2 % 4 == 0, wanted, -1)
    got = dot((iota((total, rows), 1) == first).astype(bf16), ext_ref[...]).astype(bf16)
    for dy in range(grid_y):
        far_refs[dy][:, half:] = got[dy * size : (dy + 1) * size]


def query_kernel(
    grid_x, grid_y, place_ref, x_ref, base_ref, down_ref, up_ref, slots_ref,
    pair_ref, ext_ref, inv_ref, near_count_ref, other_count_ref, shadow_ref, raw_ref,
):
    hard, rows = slots_ref.shape
    embed(x_ref, base_ref, down_ref, up_ref, pair_ref, ext_ref, inv_ref, raw_ref)
    pair_ref[rows:, :] = up_ref[...]
    product = dot(pair_ref[0:rows, :], up_ref[...], 1, 1)
    high = product.astype(bf16)
    shadow_ref[0:rows, :] = high
    shadow_ref[rows:, :] = (product - high.astype(f32)).astype(bf16)
    n_near = near_count_ref.shape[0]
    n_other = other_count_ref.shape[0]
    n_far = n_other - rows
    where_x, where_y = place_ref[0], place_ref[1]
    near_slot = iota((n_near, rows), 0)
    spot = iota((n_other, rows), 0)
    block = spot // 2
    from_x = (where_x + grid_x - (block // grid_y) % grid_x) % grid_x
    from_y = (where_y + grid_y - block % grid_y) % grid_y
    far_slot = n_near + (from_x * grid_y + from_y) * 2 + spot % 2
    far_slot = jnp.where(spot < n_far, far_slot, -1)
    near_count = jnp.zeros((n_near, rows), f32)
    other_count = jnp.zeros((n_other, rows), f32)
    for k in range(hard):
        slot = slots_ref[k : k + 1, :]
        near_count = near_count + (near_slot == slot).astype(f32)
        other_count = other_count + (far_slot == slot).astype(f32)
    near_count_ref[...] = near_count
    other_count_ref[...] = jnp.where(spot < n_far, other_count, 1.0)


def store_blocks(ref, cols, value):
    size = ref.shape[2]
    step = min(size, cols.stop - cols.start)
    for c in range(cols.start, cols.stop, step):
        at = c % size
        block = value[:, c - cols.start : c - cols.start + step]
        ref[c // size, 0 : value.shape[0], at : at + step] = block


def regroup_kernel(order, *refs):
    size = 8
    count = refs[0].shape[0] // size
    n_in = len(order)
    refs = [refs[order.index(dy)] for dy in range(n_in)] + list(refs[n_in:])
    for dx in range(0, count, 2):
        for dy in range(0, n_in, 2):
            a, b = [refs[dy + i][dx * size : (dx + 2) * size, :] for i in range(2)]
            at = slice(dy * size, (dy + 2) * size)
            refs[n_in + dx][at, :] = jnp.concatenate([a[:size], b[:size]], axis=0)
            refs[n_in + dx + 1][at, :] = jnp.concatenate([a[size:], b[size:]], axis=0)


def far_kernel(count, *refs):
    order = far_order(count)
    far_refs = [refs[order.index(dx)] for dx in range(count)]
    pair_ref, unit_ref, p_ext_ref, positive_ref = refs[count : count + 4]
    o_ref, ext_ref, x_far_ref, both_ref = refs[count + 4 :]
    rows, width = unit_ref.shape
    half = width // 2
    total = far_refs[0].shape[0]
    each = total // 4
    n_far = each * count
    out_row = iota((total, total), 0)
    in_row = iota((total, total), 1)
    spot = out_row % each
    undo = (
        (in_row // 8 == spot // 2)
        & (in_row % 2 == spot % 2)
        & ((in_row // 2) % 4 == out_row // each)
    ).astype(bf16)
    for i, far_ref in enumerate(far_refs):
        at = slice(i * each, (i + 1) * each)
        for cols in column_tiles(half):
            later = slice(half + cols.start, half + cols.stop)
            got = dot(undo, far_ref[:, cols]).astype(bf16)
            o_ref[at, cols] = got[0:each]
            o_ref[at, later] = got[each : 2 * each]
            x_far_ref[at, cols] = got[2 * each : 3 * each]
            x_far_ref[at, later] = got[3 * each :]
        ext_ref[at, :] = dot(undo[0:each], far_ref[:, half:]).astype(bf16)
    own = (iota((rows, rows), 0) == positive_ref[...]).astype(bf16)
    own_t = flip(own)
    for cols in column_tiles(width):
        o_ref[n_far:, cols] = dot(own_t, unit_ref[:, cols]).astype(bf16)
    ext_ref[n_far:, :] = dot(own_t, p_ext_ref[...]).astype(bf16)
    both_ref[...] = dot(o_ref[...], pair_ref[...], 1, 1)


def score_kernel(
    slope, rank, near_ref, pair_ref, other_both_hbm, near_count_ref, other_count_ref, shadow_hbm,
    ret_ref, g_ref, radial_ref, near_up_ref, other_both_ref, shadow_ref, sems,
):
    copies = fetch([(other_both_hbm, other_both_ref), (shadow_hbm, shadow_ref)], sems)
    width = pair_ref.shape[1]
    n_near, rows = near_count_ref.shape
    both = dot(near_ref[:, :width], pair_ref[...], 1, 1)
    near_raw, near_up = both[:, 0:rows], both[:, rows:]
    near_up_ref[...] = near_up
    for c in copies:
        c.wait()
    other_raw = other_both_ref[:, 0:rows]
    n_other = other_raw.shape[0]
    n_far = n_other - rows
    near_exp = jnp.exp(near_raw / logit_divisor - offset) * near_count_ref[...]
    other_exp = jnp.exp(other_raw / logit_divisor - offset) * other_count_ref[...]
    partition = jnp.sum(near_exp, axis=0, keepdims=True) + jnp.sum(
        other_exp, axis=0, keepdims=True
    )
    same = iota(other_raw.shape, 0) == iota(other_raw.shape, 1) + n_far
    matched = jnp.sum(jnp.where(same, other_raw, 0.0), axis=0, keepdims=True) / logit_divisor
    loss = jnp.sum(jnp.log(partition) + offset - matched, axis=1, keepdims=True)
    near_g = (near_exp / partition * slope).astype(bf16)
    other_g = ((other_exp / partition - same.astype(f32)) * slope).astype(bf16)
    g_ref[0:n_near, :] = near_g
    g_ref[n_near:, :] = other_g
    near_part = near_g.astype(f32) * near_raw
    other_part = other_g.astype(f32) * other_raw
    near_radial = jnp.sum(near_part, axis=1, keepdims=True)
    radial_ref[0:n_near, :] = near_radial
    radial_ref[n_near : n_near + n_other, :] = jnp.sum(other_part, axis=1, keepdims=True)
    q_radial = jnp.sum(near_part, axis=0, keepdims=True) + jnp.sum(
        other_part, axis=0, keepdims=True
    )
    square = iota((rows, rows), 0) == iota((rows, rows), 1)
    radial_ref[n_near + n_other :, :] = jnp.sum(
        jnp.where(square, q_radial, 0.0), axis=1, keepdims=True
    )
    back = dot(near_g, shadow_ref[0:rows, :]) + dot(near_g, shadow_ref[rows:, :])
    back = back - near_radial * near_up
    back = dot(back.astype(bf16), eye(rank, lanes))
    lane = iota((n_near, lanes), 1)
    high = loss.astype(bf16).astype(f32)
    back = jnp.where(lane == rank, high, back)
    back = jnp.where(lane == rank + 1, loss - high, back)
    ret_ref[...] = back.astype(bf16)


def halves(value):
    high = value.astype(bf16)
    return high, (value - high.astype(f32)).astype(bf16)


def wide_dot(a, value):
    high, low = halves(value)
    return dot(a, high) + dot(a, low)


def local_kernel(
    place_ref, near_ref, pair_ref, shadow_hbm, o_hbm, o_ext_hbm, x_far_hbm, q_ext_hbm, q_inv_hbm,
    p_inv_hbm, x_q_hbm, positive_hbm, g_hbm, radial_hbm, near_up_hbm, other_both_hbm,
    up_keep_ref, up_send_ref, down_ref, row_ref,
    shadow_ref, o_ref, o_ext_ref, x_far_ref, q_ext_ref, q_inv_ref, p_inv_ref, x_q_ref,
    positive_ref, g_ref, radial_ref, near_up_ref, other_both_ref, sems,
):
    pairs = [
        (g_hbm, g_ref), (radial_hbm, radial_ref), (q_ext_hbm, q_ext_ref), (o_ext_hbm, o_ext_ref),
        (o_hbm, o_ref), (positive_hbm, positive_ref), (q_inv_hbm, q_inv_ref), (p_inv_hbm, p_inv_ref),
        (shadow_hbm, shadow_ref), (near_up_hbm, near_up_ref), (other_both_hbm, other_both_ref),
        (x_far_hbm, x_far_ref), (x_q_hbm, x_q_ref),
    ]
    copies = fetch(pairs, sems)
    for c in copies[:4]:
        c.wait()
    rows, width = x_q_ref.shape
    rank = pair_ref.shape[0] - rows
    part = rank // 2
    n_near = near_ref.shape[0]
    n_far = o_ref.shape[0] - rows
    n_all = n_near + n_far + rows
    even = place_ref[2] == 0
    near_gt, other_gt = g_ref[0:n_near, :], g_ref[n_near:, :]
    near_g, other_g = flip(near_gt), flip(other_gt)
    near_radial = radial_ref[0:n_near, :]
    other_radial = radial_ref[n_near:n_all, :]
    q_radial = radial_ref[n_all:, :]
    q_ext, near_ext, o_ext = q_ext_ref[...], near_ref[:, width:], o_ext_ref[...]

    def spread(value):
        high, low = halves(value)
        return jnp.concatenate([flip(high)[0:rank], flip(low)[0:rank]], axis=0)

    near_a = spread(dot(near_gt, q_ext) - near_ext.astype(f32) * near_radial)
    other_a = spread(dot(other_gt, q_ext) - o_ext.astype(f32) * other_radial)
    q_a = spread(dot(near_g, near_ext) + dot(other_g, o_ext) - q_ext.astype(f32) * q_radial)
    copies[4].wait()
    for cols in column_tiles(width):
        grad = (
            dot(near_a, near_ref[:, cols])
            + dot(other_a, o_ref[:, cols])
            + dot(q_a, pair_ref[0:rows, cols])
        )
        grad = adapter_scale * (grad[0:rank] + grad[rank:])
        top, low = grad[0:part], grad[part:]
        store_blocks(up_keep_ref, cols, jnp.where(even, top, low))
        store_blocks(up_send_ref, cols, jnp.where(even, low, top).astype(bf16))
    for c in copies[5:]:
        c.wait()
    other_up = other_both_ref[:, rows:]
    q_back = wide_dot(near_g, near_up_ref[...]) + wide_dot(other_g, other_up)
    q_up = shadow_ref[0:rows, :].astype(f32) + shadow_ref[rows:, :].astype(f32)
    q_back = (q_back - q_up * q_radial).astype(bf16).astype(f32)
    other_back = dot(other_gt, shadow_ref[0:rows, :]) + dot(other_gt, shadow_ref[rows:, :])
    other_back = (other_back - other_up * other_radial).astype(bf16)
    own = (iota((rows, rows), 0) == positive_ref[...]).astype(bf16)
    wide = dot(other_back[n_far:], eye(rank, lanes)).astype(bf16)
    row_sum = dot(own, wide)
    row_ref[...] = jnp.where(iota(row_sum.shape, 1) < rank, row_sum, p_inv_ref[...])
    dz_q = (adapter_scale * q_inv_ref[:, 0:1] * q_back).astype(bf16)
    far_ext = o_ext[0:n_far, :].astype(f32)
    far_inv = far_ext[:, rank : rank + 1] + far_ext[:, rank + 1 : rank + 2]
    dz_f = (adapter_scale * far_inv * other_back[0:n_far].astype(f32)).astype(bf16)
    dz_qt, dz_ft = flip(dz_q), flip(dz_f)
    for cols in column_tiles(width):
        down_ref[:, cols] = dot(dz_qt, x_q_ref[:, cols]) + dot(dz_ft, x_far_ref[:, cols])


def down_kernel(
    per_near, place_ref, ret_ref, pick_ref, row_hbm, x_p_ref, down_hbm, up_keep_hbm, up_send_hbm,
    keep_ref, send_ref, loss_ref, row_ref, down_ref, sems,
):
    rank = down_ref.shape[0]
    part = rank // 2
    pairs = [
        (row_hbm, row_ref), (down_hbm, down_ref),
        (up_send_hbm, send_ref.at[:, part:]), (up_keep_hbm, keep_ref.at[:, part:]),
    ]
    copies = fetch(pairs, sems)
    ret = ret_ref[...]
    row_sum = dot(flip(pick_ref[...]), ret)[:, 0:rank]
    copies[0].wait()
    row_sum = row_sum + row_ref[:, 0:rank]
    dz_t = flip((adapter_scale * row_ref[:, rank : rank + 1] * row_sum).astype(bf16))
    copies[1].wait()
    even = place_ref[2] == 0
    for cols in column_tiles(x_p_ref.shape[1]):
        grad = dot(dz_t, x_p_ref[:, cols]) + down_ref[:, cols]
        top, low = grad[0:part], grad[part:]
        store_blocks(keep_ref, cols, jnp.where(even, top, low))
        store_blocks(send_ref, cols, jnp.where(even, low, top).astype(bf16))
    first = iota(ret.shape, 0) % per_near == 0
    lane = iota(ret.shape, 1)
    chosen = first & ((lane == rank) | (lane == rank + 1))
    share = jnp.sum(jnp.where(chosen, ret.astype(f32), 0.0), axis=1, keepdims=True)
    loss_ref[...] = jnp.broadcast_to(jnp.sum(share, axis=0, keepdims=True), loss_ref.shape)
    copies[2].wait()
    copies[3].wait()


def add_kernel(keep_ref, got_ref, out_ref):
    for i in range(keep_ref.shape[0]):
        out_ref[i] = (keep_ref[i] + got_ref[i].astype(f32)).astype(bf16)


def sum_blocks(ref, *at):
    acc = ref[(0, *at)].astype(f32)
    for i in range(1, ref.shape[0]):
        acc = acc + ref[(i, *at)].astype(f32)
    return acc


def spread_kernel(in_ref, out_ref):
    value = sum_blocks(in_ref).astype(bf16)
    for i in range(out_ref.shape[0]):
        out_ref[i] = value


def finish_kernel(in_ref, loss_ref, out_ref):
    loss = loss_ref[...]
    high = loss.astype(bf16).astype(f32)
    row = iota(loss.shape, 0)
    tail = jnp.where(row == 0, high, jnp.where(row == 1, loss - high, 0.0))
    if out_ref.shape[2] > lanes:
        tail = jnp.concatenate([tail] * (out_ref.shape[2] // lanes), axis=1)
    value = jnp.concatenate([sum_blocks(in_ref), tail], axis=0).astype(bf16)
    for i in range(out_ref.shape[0]):
        out_ref[i] = value


def output_kernel(queries, place_ref, mine_ref, other_ref, down_ref, up_ref, loss_ref):
    rank = down_ref.shape[0]
    part = rank // 2
    size = mine_ref.shape[2]
    even = place_ref[2] == 0
    loss = jnp.zeros((8, lanes), f32)
    for i in range(mine_ref.shape[0]):
        mine, other = mine_ref[i].astype(f32), other_ref[i].astype(f32)
        cols = slice(i * size, (i + 1) * size)
        top = jnp.where(even, mine[0:rank], other[0:rank])
        low = jnp.where(even, other[0:rank], mine[0:rank])
        down_ref[0:part, cols] = top[0:part]
        down_ref[part:, cols] = low[0:part]
        up_ref[0:part, cols] = top[part:]
        up_ref[part:, cols] = low[part:]
        loss = loss + mine[rank:, 0:lanes]
    loss_ref[...] = jnp.sum(loss, axis=0, keepdims=True)[:, 0:1] / queries


def call(kernel, outs, args, scratch=(), flops=0, moved=0, hbm=(), out_hbm=(), out_raw=(), limit=16):
    specs = []
    for i, a in enumerate(args):
        space = pltpu.SMEM if a.dtype == jnp.int32 and a.ndim == 1 else pltpu.VMEM
        specs.append(pl.BlockSpec(memory_space=pltpu.HBM if i in hbm else space))
    args = [
        pltpu.with_memory_space_constraint(a, pltpu.HBM) if i in hbm else a
        for i, a in enumerate(args)
    ]
    shapes = [
        pltpu.HBM(s, d) if i in out_hbm else jax.ShapeDtypeStruct(s, d)
        for i, (s, d) in enumerate(outs)
    ]
    return pl.pallas_call(
        kernel,
        out_shape=shapes,
        in_specs=specs,
        out_specs=[
            pl.BlockSpec(memory_space=pltpu.HBM if i in out_raw else pltpu.VMEM)
            for i in range(len(shapes))
        ],
        scratch_shapes=[pltpu.VMEM(*s) if isinstance(s, tuple) else s for s in scratch],
        compiler_params=pltpu.CompilerParams(vmem_limit_bytes=limit * 1024 * 1024),
        cost_estimate=pl.CostEstimate(flops=flops, bytes_accessed=moved, transcendentals=0),
    )(*args)


def exchange(x, axis, groups=None):
    return lax.all_to_all(
        x, axis, split_axis=0, concat_axis=0, tiled=True, axis_index_groups=groups
    )


def both_ways(size):
    ahead = [1] + list(range(size // 2, 1, -1))
    behind = [size - 1] + list(range(size // 2 + 1, size - 1))
    order = []
    for i in range(len(ahead)):
        order += ahead[i : i + 1] + behind[i : i + 1]
    return [d for i, d in enumerate(order) if d not in order[:i]]


def far_exchange(pieces, grid_x, grid_y):
    group = [(x, y) for x in range(grid_x) for y in range(grid_y)]
    order = [0, *both_ways(grid_y)]
    got = [pieces[0]]
    for dy in order[1:]:
        pairs = [(x * grid_y + y, x * grid_y + (y + dy) % grid_y) for x, y in group]
        got.append(lax.ppermute(pieces[dy], "group", pairs))
    lines = call(
        lambda *refs: regroup_kernel(order, *refs),
        [((grid_y * 8, got[0].shape[1]), bf16)] * grid_x,
        got,
        moved=1000,
    )
    ended = [lines[0]]
    for dx in far_order(grid_x)[1:]:
        pairs = [(x * grid_y + y, (x + dx) % grid_x * grid_y + y) for x, y in group]
        ended.append(lax.ppermute(lines[dx], "group", pairs))
    return ended


def far_order(size):
    return [0, *sorted(range(1, size), key=lambda d: -min(d, size - d))]


def make_body(grid_x, grid_y):
    def body(
        query_layer_input,
        query_frozen_base,
        passage_layer_input,
        passage_frozen_base,
        adapter_down_weight,
        adapter_up_weight,
        positive_passage_index,
        hard_negative_slots,
        group_peer_rows,
        remote_group_rows,
    ):
        n_dp = lax.axis_size("dp")
        n_group = lax.axis_size("group")
        rows, width = query_layer_input.shape
        rank = adapter_up_weight.shape[0]
        part = rank // 2
        queries = rows * n_dp * n_group
        slope = 16.0 / math.sqrt(queries) / logit_divisor
        g = lax.axis_index("group")
        place = jnp.stack([g // grid_y, g % grid_y, lax.axis_index("dp") % 2]).astype(jnp.int32)
        down_t = adapter_down_weight.T
        near_ids, far_ids = group_peer_rows.T, remote_group_rows.T
        per_near = group_peer_rows.shape[1]
        n_near = n_dp * per_near
        n_far = n_group * 2
        n_other = n_far + rows
        half = width // 2
        block = width // n_group
        near, p_unit, p_ext, p_inv, pick = call(
            passage_kernel,
            [
                ((n_near, width + lanes), bf16),
                ((rows, width), bf16),
                ((rows, lanes), bf16),
                ((rows, lanes), f32),
                ((n_near, rows), bf16),
            ],
            (passage_layer_input, passage_frozen_base, down_t, adapter_up_weight, near_ids),
            [
                ((rows, width), bf16),
                ((rows, width), bf16),
                (down_t.shape, bf16),
                (adapter_up_weight.shape, bf16),
                (near_ids.shape, jnp.int32),
                ((rows, width), f32),
                ((n_near, width + lanes), bf16),
                pltpu.SemaphoreType.DMA((5,)),
                pltpu.SemaphoreType.DMA((1 + len(column_tiles(width)),)),
            ],
            flops=300_000_000, moved=5_000_000, hbm=range(5), out_hbm=(0, 3), out_raw=(0,),
        )
        far = call(
            lambda *refs: far_pick_kernel(grid_x, grid_y, *refs),
            [((grid_x * 8, half + lanes), bf16)] * grid_y,
            (place, passage_layer_input, p_unit, p_ext, far_ids),
            flops=1000, moved=1000,
        )
        near = exchange(near.reshape(n_dp, per_near, width + lanes), "dp")
        near = near.reshape(n_near, width + lanes)
        far = far_exchange(far, grid_x, grid_y)
        q_pair, q_ext, q_inv, near_count, other_count, shadow = call(
            lambda *refs: query_kernel(grid_x, grid_y, *refs),
            [
                ((rows + rank, width), bf16),
                ((rows, lanes), bf16),
                ((rows, lanes), f32),
                ((n_near, rows), f32),
                ((n_other, rows), f32),
                ((2 * rows, rank), bf16),
            ],
            (
                place, query_layer_input, query_frozen_base, down_t, adapter_up_weight,
                hard_negative_slots.T,
            ),
            [((rows, width), f32)], flops=1000, moved=1000, out_hbm=(1, 2, 5),
        )
        positive = positive_passage_index.reshape(1, rows)
        other, other_ext, x_far, other_both = call(
            lambda *refs: far_kernel(grid_x, *refs),
            [
                ((n_other, width), bf16),
                ((n_other, lanes), bf16),
                ((n_far, width), bf16),
                ((n_other, rows + rank), f32),
            ],
            (*far, q_pair, p_unit, p_ext, positive),
            flops=1000, moved=1000, out_hbm=range(4),
        )
        ret, weights, radial, near_up = call(
            lambda *refs: score_kernel(slope, rank, *refs),
            [
                ((n_near, lanes), bf16),
                ((n_near + n_other, rows), bf16),
                ((n_near + n_other + rows, 1), f32),
                ((n_near, rank), f32),
            ],
            (near, q_pair, other_both, near_count, other_count, shadow),
            [
                ((n_other, rows + rank), f32),
                (shadow.shape, bf16),
                pltpu.SemaphoreType.DMA((2,)),
            ],
            flops=200_000_000, moved=3_000_000, hbm=(2, 5), out_hbm=(1, 2, 3),
        )
        ret = exchange(ret.reshape(n_dp, per_near, lanes), "dp").reshape(n_near, lanes)
        up_keep, up_send, down_part, row_part = call(
            local_kernel,
            [
                ((n_group, part, block), f32),
                ((n_group, part, block), bf16),
                ((rank, width), f32),
                ((rows, lanes), f32),
            ],
            (
                place, near, q_pair, shadow, other, other_ext, x_far, q_ext, q_inv, p_inv,
                query_layer_input, positive, weights, radial, near_up, other_both,
            ),
            [
                (shadow.shape, bf16),
                ((n_other, width), bf16),
                ((n_other, lanes), bf16),
                ((n_far, width), bf16),
                ((rows, lanes), bf16),
                ((rows, lanes), f32),
                ((rows, lanes), f32),
                ((rows, width), bf16),
                ((1, rows), jnp.int32),
                (weights.shape, bf16),
                (radial.shape, f32),
                (near_up.shape, f32),
                (other_both.shape, f32),
                pltpu.SemaphoreType.DMA((13,)),
            ],
            flops=900_000_000, moved=9_000_000, hbm=range(3, 16), out_hbm=range(4),
        )
        swap = [(i, i ^ 1) for i in range(n_dp)]
        keep, send, loss = call(
            lambda *refs: down_kernel(per_near, *refs),
            [
                ((n_group, rank, block), f32),
                ((n_group, rank, block), bf16),
                ((8, lanes), f32),
            ],
            (place, ret, pick, row_part, passage_layer_input, down_part, up_keep, up_send),
            [((rows, lanes), f32), ((rank, width), f32), pltpu.SemaphoreType.DMA((4,))],
            flops=100_000_000, moved=3_000_000, hbm=(3, 5, 6, 7),
        )
        got = lax.ppermute(send, "dp", swap)
        (sums,) = call(add_kernel, [((n_group, rank, block), bf16)], (keep, got), moved=2_500_000)
        cores = [list(range(c, n_dp, 2)) for c in range(2)]
        sums = exchange(sums, "group")
        (sums,) = call(
            spread_kernel, [((n_dp // 2, rank, block), bf16)], (sums,), moved=1_000_000
        )
        sums = exchange(sums, "dp", cores)
        (sums,) = call(
            finish_kernel, [((n_group, rank + 8, block), bf16)], (sums, loss), moved=1_000_000
        )
        sums = exchange(sums, "group")
        other_sums = lax.ppermute(sums, "dp", swap)
        down, up, loss = call(
            lambda *refs: output_kernel(queries, *refs),
            [((rank, width), f32), ((rank, width), f32), ((1, 1), f32)],
            (place, sums, other_sums),
            moved=3_500_000,
        )
        return (down.T, up, loss.reshape(()))

    return body


def solution(mesh):
    n_group = mesh.shape["group"]
    grid_x = {32: 4, 4: 2}[n_group]
    both = P(("dp", "group"), None)
    placed = (both, both, both, both, P(), P(), P(("dp", "group")), both, both, both)
    return jax.shard_map(
        make_body(grid_x, n_group // grid_x),
        mesh=mesh,
        in_specs=placed,
        out_specs=(P(), P(), P()),
        check_vma=False,
    )
```

```python
import math

import jax
import jax.numpy as jnp
from jax import lax
from jax.experimental import pallas as pl
from jax.experimental.pallas import tpu as pltpu
from jax.sharding import PartitionSpec as P

f32 = jnp.float32
bf16 = jnp.bfloat16
adapter_scale = 2.0
logit_divisor = 0.05
epsilon = 1e-06
offset = 1.0 / logit_divisor
tile = 512
lanes = 128


def dot(a, b, ca=1, cb=0):
    return lax.dot_general(a, b, (((ca,), (cb,)), ((), ())), preferred_element_type=f32)


def iota(shape, dim):
    return lax.broadcasted_iota(jnp.int32, shape, dim)


def eye(n, m):
    return (iota((n, m), 0) == iota((n, m), 1)).astype(bf16)


def flip(a):
    return dot(eye(a.shape[1], a.shape[1]), a, 1, 1).astype(bf16)


def column_tiles(width):
    step = min(tile, width)
    return [slice(c, c + step) for c in range(0, width, step)]


def embed(x_ref, base_ref, down_ref, up_ref, unit_ref, ext_ref, inv_ref, raw_ref, ready=None):
    rows, width = x_ref.shape
    rank = up_ref.shape[0]
    latent = dot(x_ref[...], down_ref[...], 1, 1).astype(bf16)
    if ready is not None:
        ready()
    squares = jnp.zeros((rows, 1), f32)
    for cols in column_tiles(width):
        raw = base_ref[:, cols].astype(f32) + adapter_scale * dot(latent, up_ref[:, cols])
        raw_ref[:, cols] = raw
        squares = squares + jnp.sum(raw * raw, axis=1, keepdims=True)
    inverse = lax.rsqrt(squares + epsilon)
    for cols in column_tiles(width):
        unit_ref[0:rows, cols] = (raw_ref[:, cols] * inverse).astype(bf16)
    scaled = (latent.astype(f32) * inverse).astype(bf16)
    high = inverse.astype(bf16).astype(f32)
    lane = iota((rows, lanes), 1)
    ext = dot(scaled, eye(rank, lanes))
    ext = jnp.where(lane == rank, high, ext)
    ext = jnp.where(lane == rank + 1, inverse - high, ext)
    ext_ref[...] = ext.astype(bf16)
    inv_ref[...] = jnp.broadcast_to(inverse, inv_ref.shape)


def fetch(pairs, sems):
    copies = [pltpu.make_async_copy(a, b, sems.at[i]) for i, (a, b) in enumerate(pairs)]
    for c in copies:
        c.start()
    return copies


def stride_of(chips):
    return {12: 5, 8: 3, 3: 2}.get(chips, 1)


def ring_spot(position, n_dp):
    chips = n_dp // 2
    return (position // 2 * stride_of(chips)) % chips * 2 + position % 2


def passage_kernel(
    x_hbm, base_hbm, down_hbm, up_hbm, near_ids_hbm,
    near_hbm, unit_ref, ext_ref, inv_ref, pick_ref,
    x_ref, base_ref, down_ref, up_ref, near_ids_ref, raw_ref, near_ref, sems, out_sems,
):
    pairs = [
        (x_hbm, x_ref), (down_hbm, down_ref), (base_hbm, base_ref), (up_hbm, up_ref),
        (near_ids_hbm, near_ids_ref),
    ]
    copies = fetch(pairs, sems)
    copies[0].wait()
    copies[1].wait()

    def ready():
        copies[2].wait()
        copies[3].wait()

    embed(x_ref, base_ref, down_ref, up_ref, unit_ref, ext_ref, inv_ref, raw_ref, ready)
    copies[4].wait()
    rows, width = x_ref.shape
    per_near, n_near = near_ids_ref.shape
    count = per_near * n_near
    ids = near_ids_ref[...].astype(f32).astype(bf16)
    spot = ring_spot(iota((count, n_near), 0) // per_near, n_near)
    spread = (spot == iota((count, n_near), 1)).astype(bf16)
    table = dot(spread, ids, 1, 1)
    mine = iota((count, per_near), 0) % per_near == iota((count, per_near), 1)
    wanted = jnp.sum(jnp.where(mine, table, 0.0), axis=1, keepdims=True).astype(jnp.int32)
    pick = (iota((count, rows), 1) == wanted).astype(bf16)
    pick_ref[...] = pick
    near_ref[:, width:] = dot(pick, ext_ref[...]).astype(bf16)
    sent = []
    for i, cols in enumerate([slice(width, width + lanes), *column_tiles(width)]):
        if i:
            near_ref[:, cols] = dot(pick, unit_ref[:, cols]).astype(bf16)
        copy = pltpu.make_async_copy(near_ref.at[:, cols], near_hbm.at[:, cols], out_sems.at[i])
        copy.start()
        sent.append(copy)
    for copy in sent:
        copy.wait()


def far_pick_kernel(grid_x, grid_y, place_ref, x_ref, unit_ref, ext_ref, far_ids_ref, *far_refs):
    rows, width = x_ref.shape
    half = width // 2
    n_far = far_ids_ref.shape[1]
    total = n_far * 8
    size = grid_x * 8
    where_x, where_y = place_ref[0], place_ref[1]
    ids = far_ids_ref[...].astype(f32).astype(bf16)
    block = iota((total, n_far), 0) // 8
    to_x = (where_x + block % grid_x) % grid_x
    to_y = (where_y + block // grid_x) % grid_y
    spread = (to_x * grid_y + to_y == iota((total, n_far), 1)).astype(bf16)
    table = dot(spread, ids, 1, 1)
    mine = iota((total, 2), 0) % 2 == iota((total, 2), 1)
    wanted = jnp.sum(jnp.where(mine, table, 0.0), axis=1, keepdims=True).astype(jnp.int32)
    kind = (iota((total, 4 * rows), 0) // 2) % 4
    source = iota((total, 4 * rows), 1)
    choose = ((source // rows == kind) & (source % rows == wanted)).astype(bf16)
    for cols in column_tiles(half):
        later = slice(half + cols.start, half + cols.stop)
        stack = jnp.concatenate(
            [unit_ref[:, cols], unit_ref[:, later], x_ref[:, cols], x_ref[:, later]], axis=0
        )
        got = dot(choose, stack).astype(bf16)
        for dy in range(grid_y):
            far_refs[dy][:, cols] = got[dy * size : (dy + 1) * size]
    first = jnp.where(iota((total, rows), 0) // 2 % 4 == 0, wanted, -1)
    got = dot((iota((total, rows), 1) == first).astype(bf16), ext_ref[...]).astype(bf16)
    for dy in range(grid_y):
        far_refs[dy][:, half:] = got[dy * size : (dy + 1) * size]


def query_kernel(
    grid_x, grid_y, per_near, place_ref, x_hbm, base_hbm, down_hbm, up_hbm, slots_hbm,
    pair_ref, ext_ref, inv_ref, near_count_ref, other_count_ref, shadow_ref,
    x_ref, base_ref, down_ref, up_ref, slots_ref, raw_ref, sems,
):
    pairs = [
        (x_hbm, x_ref), (down_hbm, down_ref), (base_hbm, base_ref), (up_hbm, up_ref),
        (slots_hbm, slots_ref),
    ]
    for c in fetch(pairs, sems):
        c.wait()
    hard, rows = slots_ref.shape
    embed(x_ref, base_ref, down_ref, up_ref, pair_ref, ext_ref, inv_ref, raw_ref)
    pair_ref[rows:, :] = up_ref[...]
    product = dot(pair_ref[0:rows, :], up_ref[...], 1, 1)
    high = product.astype(bf16)
    shadow_ref[0:rows, :] = high
    shadow_ref[rows:, :] = (product - high.astype(f32)).astype(bf16)
    n_near = near_count_ref.shape[0]
    n_other = other_count_ref.shape[0]
    n_far = n_other - rows
    where_x, where_y = place_ref[0], place_ref[1]
    near_slot = iota((n_near, rows), 0)
    near_slot = ring_spot(near_slot // per_near, n_near // per_near) * per_near + near_slot % per_near
    spot = iota((n_other, rows), 0)
    block = spot // 2
    from_x = (where_x + grid_x - (block // grid_y) % grid_x) % grid_x
    from_y = (where_y + grid_y - block % grid_y) % grid_y
    far_slot = n_near + (from_x * grid_y + from_y) * 2 + spot % 2
    far_slot = jnp.where(spot < n_far, far_slot, -1)
    near_count = jnp.zeros((n_near, rows), f32)
    other_count = jnp.zeros((n_other, rows), f32)
    for k in range(hard):
        slot = slots_ref[k : k + 1, :]
        near_count = near_count + (near_slot == slot).astype(f32)
        other_count = other_count + (far_slot == slot).astype(f32)
    near_count_ref[...] = near_count
    other_count_ref[...] = jnp.where(spot < n_far, other_count, 1.0)


def store_blocks(ref, cols, value):
    size = ref.shape[2]
    step = min(size, cols.stop - cols.start)
    for c in range(cols.start, cols.stop, step):
        at = c % size
        block = value[:, c - cols.start : c - cols.start + step]
        ref[c // size, 0 : value.shape[0], at : at + step] = block


def regroup_kernel(order, *refs):
    size = 8
    count = refs[0].shape[0] // size
    n_in = len(order)
    refs = [refs[order.index(dy)] for dy in range(n_in)] + list(refs[n_in:])
    for dx in range(0, count, 2):
        for dy in range(0, n_in, 2):
            a, b = [refs[dy + i][dx * size : (dx + 2) * size, :] for i in range(2)]
            at = slice(dy * size, (dy + 2) * size)
            refs[n_in + dx][at, :] = jnp.concatenate([a[:size], b[:size]], axis=0)
            refs[n_in + dx + 1][at, :] = jnp.concatenate([a[size:], b[size:]], axis=0)


def far_kernel(count, *refs):
    order = far_order(count)
    far_refs = [refs[order.index(dx)] for dx in range(count)]
    pair_ref, unit_ref, p_ext_ref, positive_ref = refs[count : count + 4]
    o_ref, ext_ref, x_far_ref, both_ref = refs[count + 4 :]
    rows, width = unit_ref.shape
    half = width // 2
    total = far_refs[0].shape[0]
    each = total // 4
    n_far = each * count
    out_row = iota((total, total), 0)
    in_row = iota((total, total), 1)
    spot = out_row % each
    undo = (
        (in_row // 8 == spot // 2)
        & (in_row % 2 == spot % 2)
        & ((in_row // 2) % 4 == out_row // each)
    ).astype(bf16)
    for i, far_ref in enumerate(far_refs):
        at = slice(i * each, (i + 1) * each)
        for cols in column_tiles(half):
            later = slice(half + cols.start, half + cols.stop)
            got = dot(undo, far_ref[:, cols]).astype(bf16)
            o_ref[at, cols] = got[0:each]
            o_ref[at, later] = got[each : 2 * each]
            x_far_ref[at, cols] = got[2 * each : 3 * each]
            x_far_ref[at, later] = got[3 * each :]
        ext_ref[at, :] = dot(undo[0:each], far_ref[:, half:]).astype(bf16)
    own = (iota((rows, rows), 0) == positive_ref[...]).astype(bf16)
    own_t = flip(own)
    for cols in column_tiles(width):
        o_ref[n_far:, cols] = dot(own_t, unit_ref[:, cols]).astype(bf16)
    ext_ref[n_far:, :] = dot(own_t, p_ext_ref[...]).astype(bf16)
    both_ref[...] = dot(o_ref[...], pair_ref[...], 1, 1)


def score_kernel(
    slope, rank, near_ref, pair_ref, other_both_hbm, near_count_ref, other_count_ref, shadow_hbm,
    ret_ref, g_ref, radial_ref, near_up_ref, other_both_ref, shadow_ref, sems,
):
    copies = fetch([(other_both_hbm, other_both_ref), (shadow_hbm, shadow_ref)], sems)
    width = pair_ref.shape[1]
    n_near, rows = near_count_ref.shape
    both = dot(near_ref[:, :width], pair_ref[...], 1, 1)
    near_raw, near_up = both[:, 0:rows], both[:, rows:]
    near_up_ref[...] = near_up
    for c in copies:
        c.wait()
    other_raw = other_both_ref[:, 0:rows]
    n_other = other_raw.shape[0]
    n_far = n_other - rows
    near_exp = jnp.exp(near_raw / logit_divisor - offset) * near_count_ref[...]
    other_exp = jnp.exp(other_raw / logit_divisor - offset) * other_count_ref[...]
    partition = jnp.sum(near_exp, axis=0, keepdims=True) + jnp.sum(
        other_exp, axis=0, keepdims=True
    )
    same = iota(other_raw.shape, 0) == iota(other_raw.shape, 1) + n_far
    matched = jnp.sum(jnp.where(same, other_raw, 0.0), axis=0, keepdims=True) / logit_divisor
    loss = jnp.sum(jnp.log(partition) + offset - matched, axis=1, keepdims=True)
    near_g = (near_exp / partition * slope).astype(bf16)
    other_g = ((other_exp / partition - same.astype(f32)) * slope).astype(bf16)
    g_ref[0:n_near, :] = near_g
    g_ref[n_near:, :] = other_g
    near_part = near_g.astype(f32) * near_raw
    other_part = other_g.astype(f32) * other_raw
    near_radial = jnp.sum(near_part, axis=1, keepdims=True)
    radial_ref[0:n_near, :] = near_radial
    radial_ref[n_near : n_near + n_other, :] = jnp.sum(other_part, axis=1, keepdims=True)
    q_radial = jnp.sum(near_part, axis=0, keepdims=True) + jnp.sum(
        other_part, axis=0, keepdims=True
    )
    square = iota((rows, rows), 0) == iota((rows, rows), 1)
    radial_ref[n_near + n_other :, :] = jnp.sum(
        jnp.where(square, q_radial, 0.0), axis=1, keepdims=True
    )
    back = dot(near_g, shadow_ref[0:rows, :]) + dot(near_g, shadow_ref[rows:, :])
    back = back - near_radial * near_up
    back = dot(back.astype(bf16), eye(rank, lanes))
    lane = iota((n_near, lanes), 1)
    high = loss.astype(bf16).astype(f32)
    back = jnp.where(lane == rank, high, back)
    back = jnp.where(lane == rank + 1, loss - high, back)
    ret_ref[...] = back.astype(bf16)


def halves(value):
    high = value.astype(bf16)
    return high, (value - high.astype(f32)).astype(bf16)


def wide_dot(a, value):
    high, low = halves(value)
    return dot(a, high) + dot(a, low)


def local_kernel(
    place_ref, near_ref, pair_ref, shadow_hbm, o_hbm, o_ext_hbm, x_far_hbm, q_ext_hbm, q_inv_hbm,
    p_inv_hbm, x_q_hbm, positive_hbm, g_hbm, radial_hbm, near_up_hbm, other_both_hbm,
    up_keep_ref, up_send_ref, down_ref, row_ref,
    shadow_ref, o_ref, o_ext_ref, x_far_ref, q_ext_ref, q_inv_ref, p_inv_ref, x_q_ref,
    positive_ref, g_ref, radial_ref, near_up_ref, other_both_ref, sems,
):
    pairs = [
        (g_hbm, g_ref), (radial_hbm, radial_ref), (q_ext_hbm, q_ext_ref), (o_ext_hbm, o_ext_ref),
        (o_hbm, o_ref), (positive_hbm, positive_ref), (q_inv_hbm, q_inv_ref), (p_inv_hbm, p_inv_ref),
        (shadow_hbm, shadow_ref), (near_up_hbm, near_up_ref), (other_both_hbm, other_both_ref),
        (x_far_hbm, x_far_ref), (x_q_hbm, x_q_ref),
    ]
    copies = fetch(pairs, sems)
    for c in copies[:4]:
        c.wait()
    rows, width = x_q_ref.shape
    rank = pair_ref.shape[0] - rows
    part = rank // 2
    n_near = near_ref.shape[0]
    n_far = o_ref.shape[0] - rows
    n_all = n_near + n_far + rows
    even = place_ref[2] == 0
    near_gt, other_gt = g_ref[0:n_near, :], g_ref[n_near:, :]
    near_g, other_g = flip(near_gt), flip(other_gt)
    near_radial = radial_ref[0:n_near, :]
    other_radial = radial_ref[n_near:n_all, :]
    q_radial = radial_ref[n_all:, :]
    q_ext, near_ext, o_ext = q_ext_ref[...], near_ref[:, width:], o_ext_ref[...]

    def spread(value):
        high, low = halves(value)
        return jnp.concatenate([flip(high)[0:rank], flip(low)[0:rank]], axis=0)

    near_a = spread(dot(near_gt, q_ext) - near_ext.astype(f32) * near_radial)
    other_a = spread(dot(other_gt, q_ext) - o_ext.astype(f32) * other_radial)
    q_a = spread(dot(near_g, near_ext) + dot(other_g, o_ext) - q_ext.astype(f32) * q_radial)
    copies[4].wait()
    for cols in column_tiles(width):
        grad = (
            dot(near_a, near_ref[:, cols])
            + dot(other_a, o_ref[:, cols])
            + dot(q_a, pair_ref[0:rows, cols])
        )
        grad = adapter_scale * (grad[0:rank] + grad[rank:])
        top, low = grad[0:part], grad[part:]
        store_blocks(up_keep_ref, cols, jnp.where(even, top, low))
        store_blocks(up_send_ref, cols, jnp.where(even, low, top).astype(bf16))
    for c in copies[5:]:
        c.wait()
    other_up = other_both_ref[:, rows:]
    q_back = wide_dot(near_g, near_up_ref[...]) + wide_dot(other_g, other_up)
    q_up = shadow_ref[0:rows, :].astype(f32) + shadow_ref[rows:, :].astype(f32)
    q_back = (q_back - q_up * q_radial).astype(bf16).astype(f32)
    other_back = dot(other_gt, shadow_ref[0:rows, :]) + dot(other_gt, shadow_ref[rows:, :])
    other_back = (other_back - other_up * other_radial).astype(bf16)
    own = (iota((rows, rows), 0) == positive_ref[...]).astype(bf16)
    wide = dot(other_back[n_far:], eye(rank, lanes)).astype(bf16)
    row_sum = dot(own, wide)
    row_ref[...] = jnp.where(iota(row_sum.shape, 1) < rank, row_sum, p_inv_ref[...])
    dz_q = (adapter_scale * q_inv_ref[:, 0:1] * q_back).astype(bf16)
    far_ext = o_ext[0:n_far, :].astype(f32)
    far_inv = far_ext[:, rank : rank + 1] + far_ext[:, rank + 1 : rank + 2]
    dz_f = (adapter_scale * far_inv * other_back[0:n_far].astype(f32)).astype(bf16)
    dz_qt, dz_ft = flip(dz_q), flip(dz_f)
    for cols in column_tiles(width):
        down_ref[:, cols] = dot(dz_qt, x_q_ref[:, cols]) + dot(dz_ft, x_far_ref[:, cols])


def down_kernel(
    per_near, place_ref, ret_ref, pick_ref, row_hbm, x_p_ref, down_hbm, up_keep_hbm, up_send_hbm,
    keep_ref, send_ref, loss_ref, row_ref, down_ref, sems,
):
    rank = down_ref.shape[0]
    part = rank // 2
    pairs = [
        (row_hbm, row_ref), (down_hbm, down_ref),
        (up_send_hbm, send_ref.at[:, part:]), (up_keep_hbm, keep_ref.at[:, part:]),
    ]
    copies = fetch(pairs, sems)
    ret = ret_ref[...]
    row_sum = dot(flip(pick_ref[...]), ret)[:, 0:rank]
    copies[0].wait()
    row_sum = row_sum + row_ref[:, 0:rank]
    dz_t = flip((adapter_scale * row_ref[:, rank : rank + 1] * row_sum).astype(bf16))
    copies[1].wait()
    even = place_ref[2] == 0
    for cols in column_tiles(x_p_ref.shape[1]):
        grad = dot(dz_t, x_p_ref[:, cols]) + down_ref[:, cols]
        top, low = grad[0:part], grad[part:]
        store_blocks(keep_ref, cols, jnp.where(even, top, low))
        store_blocks(send_ref, cols, jnp.where(even, low, top).astype(bf16))
    first = iota(ret.shape, 0) % per_near == 0
    lane = iota(ret.shape, 1)
    chosen = first & ((lane == rank) | (lane == rank + 1))
    share = jnp.sum(jnp.where(chosen, ret.astype(f32), 0.0), axis=1, keepdims=True)
    loss_ref[...] = jnp.broadcast_to(jnp.sum(share, axis=0, keepdims=True), loss_ref.shape)
    copies[2].wait()
    copies[3].wait()


def add_kernel(keep_ref, got_ref, out_ref):
    for i in range(keep_ref.shape[0]):
        out_ref[i] = (keep_ref[i] + got_ref[i].astype(f32)).astype(bf16)


def sum_blocks(ref, *at):
    acc = ref[(0, *at)].astype(f32)
    for i in range(1, ref.shape[0]):
        acc = acc + ref[(i, *at)].astype(f32)
    return acc


def spread_kernel(in_ref, out_ref):
    value = sum_blocks(in_ref).astype(bf16)
    for i in range(out_ref.shape[0]):
        out_ref[i] = value


def finish_kernel(in_ref, loss_ref, out_ref):
    loss = loss_ref[...]
    high = loss.astype(bf16).astype(f32)
    row = iota(loss.shape, 0)
    tail = jnp.where(row == 0, high, jnp.where(row == 1, loss - high, 0.0))
    if out_ref.shape[2] > lanes:
        tail = jnp.concatenate([tail] * (out_ref.shape[2] // lanes), axis=1)
    value = jnp.concatenate([sum_blocks(in_ref), tail], axis=0).astype(bf16)
    for i in range(out_ref.shape[0]):
        out_ref[i] = value


def output_kernel(queries, place_ref, mine_ref, other_ref, down_ref, up_ref, loss_ref):
    rank = down_ref.shape[0]
    part = rank // 2
    size = mine_ref.shape[2]
    even = place_ref[2] == 0
    loss = jnp.zeros((8, lanes), f32)
    for i in range(mine_ref.shape[0]):
        mine, other = mine_ref[i].astype(f32), other_ref[i].astype(f32)
        cols = slice(i * size, (i + 1) * size)
        top = jnp.where(even, mine[0:rank], other[0:rank])
        low = jnp.where(even, other[0:rank], mine[0:rank])
        down_ref[0:part, cols] = top[0:part]
        down_ref[part:, cols] = low[0:part]
        up_ref[0:part, cols] = top[part:]
        up_ref[part:, cols] = low[part:]
        loss = loss + mine[rank:, 0:lanes]
    loss_ref[...] = jnp.sum(loss, axis=0, keepdims=True)[:, 0:1] / queries


def call(kernel, outs, args, scratch=(), flops=0, moved=0, hbm=(), out_hbm=(), out_raw=(), limit=16):
    specs = []
    for i, a in enumerate(args):
        space = pltpu.SMEM if a.dtype == jnp.int32 and a.ndim == 1 else pltpu.VMEM
        specs.append(pl.BlockSpec(memory_space=pltpu.HBM if i in hbm else space))
    args = [
        pltpu.with_memory_space_constraint(a, pltpu.HBM) if i in hbm else a
        for i, a in enumerate(args)
    ]
    shapes = [
        pltpu.HBM(s, d) if i in out_hbm else jax.ShapeDtypeStruct(s, d)
        for i, (s, d) in enumerate(outs)
    ]
    return pl.pallas_call(
        kernel,
        out_shape=shapes,
        in_specs=specs,
        out_specs=[
            pl.BlockSpec(memory_space=pltpu.HBM if i in out_raw else pltpu.VMEM)
            for i in range(len(shapes))
        ],
        scratch_shapes=[pltpu.VMEM(*s) if isinstance(s, tuple) else s for s in scratch],
        compiler_params=pltpu.CompilerParams(vmem_limit_bytes=limit * 1024 * 1024),
        cost_estimate=pl.CostEstimate(flops=flops, bytes_accessed=moved, transcendentals=0),
    )(*args)


def exchange(x, axis, groups=None):
    return lax.all_to_all(
        x, axis, split_axis=0, concat_axis=0, tiled=True, axis_index_groups=groups
    )


def both_ways(size):
    ahead = [1] + list(range(size // 2, 1, -1))
    behind = [size - 1] + list(range(size // 2 + 1, size - 1))
    order = []
    for i in range(len(ahead)):
        order += ahead[i : i + 1] + behind[i : i + 1]
    return [d for i, d in enumerate(order) if d not in order[:i]]


def far_exchange(pieces, grid_x, grid_y):
    group = [(x, y) for x in range(grid_x) for y in range(grid_y)]
    order = [0, *both_ways(grid_y)]
    got = [pieces[0]]
    for dy in order[1:]:
        pairs = [(x * grid_y + y, x * grid_y + (y + dy) % grid_y) for x, y in group]
        got.append(lax.ppermute(pieces[dy], "group", pairs))
    lines = call(
        lambda *refs: regroup_kernel(order, *refs),
        [((grid_y * 8, got[0].shape[1]), bf16)] * grid_x,
        got,
        moved=1000,
    )
    ended = [lines[0]]
    for dx in far_order(grid_x)[1:]:
        pairs = [(x * grid_y + y, (x + dx) % grid_x * grid_y + y) for x, y in group]
        ended.append(lax.ppermute(lines[dx], "group", pairs))
    return ended


def far_order(size):
    return [0, *sorted(range(1, size), key=lambda d: -min(d, size - d))]


def make_body(grid_x, grid_y):
    def body(
        query_layer_input,
        query_frozen_base,
        passage_layer_input,
        passage_frozen_base,
        adapter_down_weight,
        adapter_up_weight,
        positive_passage_index,
        hard_negative_slots,
        group_peer_rows,
        remote_group_rows,
    ):
        n_dp = lax.axis_size("dp")
        n_group = lax.axis_size("group")
        rows, width = query_layer_input.shape
        rank = adapter_up_weight.shape[0]
        part = rank // 2
        queries = rows * n_dp * n_group
        slope = 16.0 / math.sqrt(queries) / logit_divisor
        g = lax.axis_index("group")
        place = jnp.stack([g // grid_y, g % grid_y, lax.axis_index("dp") % 2]).astype(jnp.int32)
        down_t = adapter_down_weight.T
        near_ids, far_ids = group_peer_rows.T, remote_group_rows.T
        per_near = group_peer_rows.shape[1]
        n_near = n_dp * per_near
        n_far = n_group * 2
        n_other = n_far + rows
        half = width // 2
        block = width // n_group
        near, p_unit, p_ext, p_inv, pick = call(
            passage_kernel,
            [
                ((n_near, width + lanes), bf16),
                ((rows, width), bf16),
                ((rows, lanes), bf16),
                ((rows, lanes), f32),
                ((n_near, rows), bf16),
            ],
            (passage_layer_input, passage_frozen_base, down_t, adapter_up_weight, near_ids),
            [
                ((rows, width), bf16),
                ((rows, width), bf16),
                (down_t.shape, bf16),
                (adapter_up_weight.shape, bf16),
                (near_ids.shape, jnp.int32),
                ((rows, width), f32),
                ((n_near, width + lanes), bf16),
                pltpu.SemaphoreType.DMA((5,)),
                pltpu.SemaphoreType.DMA((1 + len(column_tiles(width)),)),
            ],
            flops=300_000_000, moved=5_000_000, hbm=range(5), out_hbm=(0, 3), out_raw=(0,),
        )
        far = call(
            lambda *refs: far_pick_kernel(grid_x, grid_y, *refs),
            [((grid_x * 8, half + lanes), bf16)] * grid_y,
            (place, passage_layer_input, p_unit, p_ext, far_ids),
            flops=1000, moved=1000,
        )
        ring = [ring_spot(i, n_dp) for i in range(n_dp)]
        step = stride_of(grid_y)
        plane = [x * grid_y + y * step % grid_y for x in range(grid_x) for y in range(grid_y)]
        near = exchange(near.reshape(n_dp, per_near, width + lanes), "dp", [ring])
        near = near.reshape(n_near, width + lanes)
        far = far_exchange(far, grid_x, grid_y)
        q_pair, q_ext, q_inv, near_count, other_count, shadow = call(
            lambda *refs: query_kernel(grid_x, grid_y, per_near, *refs),
            [
                ((rows + rank, width), bf16),
                ((rows, lanes), bf16),
                ((rows, lanes), f32),
                ((n_near, rows), f32),
                ((n_other, rows), f32),
                ((2 * rows, rank), bf16),
            ],
            (
                place, query_layer_input, query_frozen_base, down_t, adapter_up_weight,
                hard_negative_slots.T,
            ),
            [
                ((rows, width), bf16),
                ((rows, width), bf16),
                (down_t.shape, bf16),
                (adapter_up_weight.shape, bf16),
                (hard_negative_slots.T.shape, jnp.int32),
                ((rows, width), f32),
                pltpu.SemaphoreType.DMA((5,)),
            ],
            flops=1000, moved=1000, hbm=range(1, 6), out_hbm=(1, 2, 5),
        )
        positive = positive_passage_index.reshape(1, rows)
        other, other_ext, x_far, other_both = call(
            lambda *refs: far_kernel(grid_x, *refs),
            [
                ((n_other, width), bf16),
                ((n_other, lanes), bf16),
                ((n_far, width), bf16),
                ((n_other, rows + rank), f32),
            ],
            (*far, q_pair, p_unit, p_ext, positive),
            flops=1000, moved=1000, out_hbm=range(4),
        )
        ret, weights, radial, near_up = call(
            lambda *refs: score_kernel(slope, rank, *refs),
            [
                ((n_near, lanes), bf16),
                ((n_near + n_other, rows), bf16),
                ((n_near + n_other + rows, 1), f32),
                ((n_near, rank), f32),
            ],
            (near, q_pair, other_both, near_count, other_count, shadow),
            [
                ((n_other, rows + rank), f32),
                (shadow.shape, bf16),
                pltpu.SemaphoreType.DMA((2,)),
            ],
            flops=200_000_000, moved=3_000_000, hbm=(2, 5), out_hbm=(1, 2, 3),
        )
        ret = exchange(ret.reshape(n_dp, per_near, lanes), "dp", [ring]).reshape(n_near, lanes)
        up_keep, up_send, down_part, row_part = call(
            local_kernel,
            [
                ((n_group, part, block), f32),
                ((n_group, part, block), bf16),
                ((rank, width), f32),
                ((rows, lanes), f32),
            ],
            (
                place, near, q_pair, shadow, other, other_ext, x_far, q_ext, q_inv, p_inv,
                query_layer_input, positive, weights, radial, near_up, other_both,
            ),
            [
                (shadow.shape, bf16),
                ((n_other, width), bf16),
                ((n_other, lanes), bf16),
                ((n_far, width), bf16),
                ((rows, lanes), bf16),
                ((rows, lanes), f32),
                ((rows, lanes), f32),
                ((rows, width), bf16),
                ((1, rows), jnp.int32),
                (weights.shape, bf16),
                (radial.shape, f32),
                (near_up.shape, f32),
                (other_both.shape, f32),
                pltpu.SemaphoreType.DMA((13,)),
            ],
            flops=900_000_000, moved=9_000_000, hbm=range(3, 16), out_hbm=range(4),
        )
        swap = [(i, i ^ 1) for i in range(n_dp)]
        keep, send, loss = call(
            lambda *refs: down_kernel(per_near, *refs),
            [
                ((n_group, rank, block), f32),
                ((n_group, rank, block), bf16),
                ((8, lanes), f32),
            ],
            (place, ret, pick, row_part, passage_layer_input, down_part, up_keep, up_send),
            [((rows, lanes), f32), ((rank, width), f32), pltpu.SemaphoreType.DMA((4,))],
            flops=100_000_000, moved=3_000_000, hbm=(3, 5, 6, 7),
        )
        got = lax.ppermute(send, "dp", swap)
        (sums,) = call(add_kernel, [((n_group, rank, block), bf16)], (keep, got), moved=2_500_000)
        cores = [ring[c::2] for c in range(2)]
        sums = exchange(sums, "group", [plane])
        (sums,) = call(
            spread_kernel, [((n_dp // 2, rank, block), bf16)], (sums,), moved=1_000_000
        )
        sums = exchange(sums, "dp", cores)
        (sums,) = call(
            finish_kernel, [((n_group, rank + 8, block), bf16)], (sums, loss), moved=1_000_000
        )
        sums = exchange(sums, "group", [plane])
        other_sums = lax.ppermute(sums, "dp", swap)
        down, up, loss = call(
            lambda *refs: output_kernel(queries, *refs),
            [((rank, width), f32), ((rank, width), f32), ((1, 1), f32)],
            (place, sums, other_sums),
            moved=3_500_000,
        )
        return (down.T, up, loss.reshape(()))

    return body


def solution(mesh):
    n_group = mesh.shape["group"]
    grid_x = {32: 4, 4: 2}[n_group]
    both = P(("dp", "group"), None)
    placed = (both, both, both, both, P(), P(), P(("dp", "group")), both, both, both)
    return jax.shard_map(
        make_body(grid_x, n_group // grid_x),
        mesh=mesh,
        in_specs=placed,
        out_specs=(P(), P(), P()),
        check_vma=False,
    )
```

```python
import math

import jax
import jax.numpy as jnp
from jax import lax
from jax.experimental import pallas as pl
from jax.experimental.pallas import tpu as pltpu
from jax.sharding import PartitionSpec as P

f32 = jnp.float32
bf16 = jnp.bfloat16
adapter_scale = 2.0
logit_divisor = 0.05
epsilon = 1e-06
offset = 1.0 / logit_divisor
tile = 512
lanes = 128


def dot(a, b, ca=1, cb=0):
    return lax.dot_general(a, b, (((ca,), (cb,)), ((), ())), preferred_element_type=f32)


def iota(shape, dim):
    return lax.broadcasted_iota(jnp.int32, shape, dim)


def eye(n, m):
    return (iota((n, m), 0) == iota((n, m), 1)).astype(bf16)


def flip(a):
    return dot(eye(a.shape[1], a.shape[1]), a, 1, 1).astype(bf16)


def column_tiles(width):
    step = min(tile, width)
    return [slice(c, c + step) for c in range(0, width, step)]


def embed(x_ref, base_ref, down_ref, up_ref, unit_ref, ext_ref, inv_ref, raw_ref, ready=None):
    rows, width = x_ref.shape
    rank = up_ref.shape[0]
    latent = dot(x_ref[...], down_ref[...], 1, 1).astype(bf16)
    if ready is not None:
        ready()
    squares = jnp.zeros((rows, 1), f32)
    for cols in column_tiles(width):
        raw = base_ref[:, cols].astype(f32) + adapter_scale * dot(latent, up_ref[:, cols])
        raw_ref[:, cols] = raw
        squares = squares + jnp.sum(raw * raw, axis=1, keepdims=True)
    inverse = lax.rsqrt(squares + epsilon)
    for cols in column_tiles(width):
        unit_ref[0:rows, cols] = (raw_ref[:, cols] * inverse).astype(bf16)
    scaled = (latent.astype(f32) * inverse).astype(bf16)
    high = inverse.astype(bf16).astype(f32)
    lane = iota((rows, lanes), 1)
    ext = dot(scaled, eye(rank, lanes))
    ext = jnp.where(lane == rank, high, ext)
    ext = jnp.where(lane == rank + 1, inverse - high, ext)
    ext_ref[...] = ext.astype(bf16)
    inv_ref[...] = jnp.broadcast_to(inverse, inv_ref.shape)


def fetch(pairs, sems):
    copies = [pltpu.make_async_copy(a, b, sems.at[i]) for i, (a, b) in enumerate(pairs)]
    for c in copies:
        c.start()
    return copies


def stride_of(chips):
    return {12: 5, 8: 3, 3: 2}.get(chips, 1)


def ring_spot(position, n_dp):
    chips = n_dp // 2
    return (position // 2 * stride_of(chips)) % chips * 2 + position % 2


def passage_kernel(
    x_hbm, base_hbm, down_hbm, up_hbm, near_ids_hbm,
    near_hbm, unit_ref, ext_ref, inv_ref, pick_ref,
    x_ref, base_ref, down_ref, up_ref, near_ids_ref, raw_ref, near_ref, sems, out_sems,
):
    pairs = [
        (x_hbm, x_ref), (down_hbm, down_ref), (base_hbm, base_ref), (up_hbm, up_ref),
        (near_ids_hbm, near_ids_ref),
    ]
    copies = fetch(pairs, sems)
    copies[0].wait()
    copies[1].wait()

    def ready():
        copies[2].wait()
        copies[3].wait()

    embed(x_ref, base_ref, down_ref, up_ref, unit_ref, ext_ref, inv_ref, raw_ref, ready)
    copies[4].wait()
    rows, width = x_ref.shape
    per_near, n_near = near_ids_ref.shape
    count = per_near * n_near
    ids = near_ids_ref[...].astype(f32).astype(bf16)
    spot = ring_spot(iota((count, n_near), 0) // per_near, n_near)
    spread = (spot == iota((count, n_near), 1)).astype(bf16)
    table = dot(spread, ids, 1, 1)
    mine = iota((count, per_near), 0) % per_near == iota((count, per_near), 1)
    wanted = jnp.sum(jnp.where(mine, table, 0.0), axis=1, keepdims=True).astype(jnp.int32)
    pick = (iota((count, rows), 1) == wanted).astype(bf16)
    pick_ref[...] = pick
    near_ref[:, width:] = dot(pick, ext_ref[...]).astype(bf16)
    sent = []
    for i, cols in enumerate([slice(width, width + lanes), *column_tiles(width)]):
        if i:
            near_ref[:, cols] = dot(pick, unit_ref[:, cols]).astype(bf16)
        copy = pltpu.make_async_copy(near_ref.at[:, cols], near_hbm.at[:, cols], out_sems.at[i])
        copy.start()
        sent.append(copy)
    for copy in sent:
        copy.wait()


def far_pick_kernel(grid_x, grid_y, place_ref, x_ref, unit_ref, ext_ref, far_ids_ref, *far_refs):
    rows, width = x_ref.shape
    half = width // 2
    n_far = far_ids_ref.shape[1]
    total = n_far * 8
    size = grid_x * 8
    where_x, where_y = place_ref[0], place_ref[1]
    ids = far_ids_ref[...].astype(f32).astype(bf16)
    block = iota((total, n_far), 0) // 8
    to_x = (where_x + block % grid_x) % grid_x
    to_y = (where_y + block // grid_x) % grid_y
    spread = (to_x * grid_y + to_y == iota((total, n_far), 1)).astype(bf16)
    table = dot(spread, ids, 1, 1)
    mine = iota((total, 2), 0) % 2 == iota((total, 2), 1)
    wanted = jnp.sum(jnp.where(mine, table, 0.0), axis=1, keepdims=True).astype(jnp.int32)
    kind = (iota((total, 4 * rows), 0) // 2) % 4
    source = iota((total, 4 * rows), 1)
    choose = ((source // rows == kind) & (source % rows == wanted)).astype(bf16)
    for cols in column_tiles(half):
        later = slice(half + cols.start, half + cols.stop)
        stack = jnp.concatenate(
            [unit_ref[:, cols], unit_ref[:, later], x_ref[:, cols], x_ref[:, later]], axis=0
        )
        got = dot(choose, stack).astype(bf16)
        for dy in range(grid_y):
            far_refs[dy][:, cols] = got[dy * size : (dy + 1) * size]
    first = jnp.where(iota((total, rows), 0) // 2 % 4 == 0, wanted, -1)
    got = dot((iota((total, rows), 1) == first).astype(bf16), ext_ref[...]).astype(bf16)
    for dy in range(grid_y):
        far_refs[dy][:, half:] = got[dy * size : (dy + 1) * size]


def query_kernel(
    grid_x, grid_y, per_near, place_ref, x_hbm, base_hbm, down_hbm, up_hbm, slots_hbm,
    pair_ref, ext_ref, inv_ref, near_count_ref, other_count_ref, shadow_ref,
    x_ref, base_ref, down_ref, up_ref, slots_ref, raw_ref, sems,
):
    pairs = [
        (x_hbm, x_ref), (down_hbm, down_ref), (base_hbm, base_ref), (up_hbm, up_ref),
        (slots_hbm, slots_ref),
    ]
    for c in fetch(pairs, sems):
        c.wait()
    hard, rows = slots_ref.shape
    embed(x_ref, base_ref, down_ref, up_ref, pair_ref, ext_ref, inv_ref, raw_ref)
    pair_ref[rows:, :] = up_ref[...]
    product = dot(pair_ref[0:rows, :], up_ref[...], 1, 1)
    high = product.astype(bf16)
    shadow_ref[0:rows, :] = high
    shadow_ref[rows:, :] = (product - high.astype(f32)).astype(bf16)
    n_near = near_count_ref.shape[0]
    n_other = other_count_ref.shape[0]
    n_far = n_other - rows
    where_x, where_y = place_ref[0], place_ref[1]
    near_slot = iota((n_near, rows), 0)
    near_slot = ring_spot(near_slot // per_near, n_near // per_near) * per_near + near_slot % per_near
    spot = iota((n_other, rows), 0)
    block = spot // 2
    from_x = (where_x + grid_x - (block // grid_y) % grid_x) % grid_x
    from_y = (where_y + grid_y - block % grid_y) % grid_y
    far_slot = n_near + (from_x * grid_y + from_y) * 2 + spot % 2
    far_slot = jnp.where(spot < n_far, far_slot, -1)
    near_count = jnp.zeros((n_near, rows), f32)
    other_count = jnp.zeros((n_other, rows), f32)
    for k in range(hard):
        slot = slots_ref[k : k + 1, :]
        near_count = near_count + (near_slot == slot).astype(f32)
        other_count = other_count + (far_slot == slot).astype(f32)
    near_count_ref[...] = near_count
    other_count_ref[...] = jnp.where(spot < n_far, other_count, 1.0)


def store_blocks(ref, cols, value):
    size = ref.shape[2]
    step = min(size, cols.stop - cols.start)
    for c in range(cols.start, cols.stop, step):
        at = c % size
        block = value[:, c - cols.start : c - cols.start + step]
        ref[c // size, 0 : value.shape[0], at : at + step] = block


def regroup_kernel(order, *refs):
    size = 8
    count = refs[0].shape[0] // size
    n_in = len(order)
    x_hbm, ext_ref, pick_ref, mate_ref = refs[n_in : n_in + 4]
    rows, width = x_hbm.shape
    copy = pltpu.make_async_copy(x_hbm, mate_ref.at[:, 0:width], refs[-1])
    copy.start()
    refs = [refs[order.index(dy)] for dy in range(n_in)] + list(refs[n_in + 4 : -1])
    mate_ref[:, width : width + lanes] = ext_ref[...]
    for i in range(0, pick_ref.shape[0], rows):
        piece = dot(pick_ref[i : i + rows, :], eye(rows, lanes)).astype(bf16)
        at = width + lanes * (1 + i // rows)
        mate_ref[0 : piece.shape[0], at : at + lanes] = piece
    for dx in range(0, count, 2):
        for dy in range(0, n_in, 2):
            a, b = [refs[dy + i][dx * size : (dx + 2) * size, :] for i in range(2)]
            at = slice(dy * size, (dy + 2) * size)
            refs[n_in + dx][at, :] = jnp.concatenate([a[:size], b[:size]], axis=0)
            refs[n_in + dx + 1][at, :] = jnp.concatenate([a[size:], b[size:]], axis=0)
    copy.wait()


def far_kernel(count, per_near, place_ref, *refs):
    order = far_order(count)
    far_refs = [refs[order.index(dx)] for dx in range(count)]
    pair_ref, unit_ref, p_ext_ref, positive_ref, pick_ref, mate_ref = refs[count : count + 6]
    o_ref, ext_ref, x_far_ref, both_ref, owner_ref, mate_inv_ref = refs[count + 6 :]
    rows, width = unit_ref.shape
    half = width // 2
    total = far_refs[0].shape[0] * count
    n_far = total // 4
    out_row = iota((total, total), 0)
    in_row = iota((total, total), 1)
    spot = out_row % n_far
    undo = (
        (in_row // 8 == spot // 2)
        & (in_row % 2 == spot % 2)
        & ((in_row // 2) % 4 == out_row // n_far)
    ).astype(bf16)
    for cols in column_tiles(half):
        later = slice(half + cols.start, half + cols.stop)
        got = dot(undo, jnp.concatenate([r[:, cols] for r in far_refs], axis=0)).astype(bf16)
        o_ref[0:n_far, cols] = got[0:n_far]
        o_ref[0:n_far, later] = got[n_far : 2 * n_far]
        x_far_ref[:, cols] = got[2 * n_far : 3 * n_far]
        x_far_ref[:, later] = got[3 * n_far :]
    tail = jnp.concatenate([r[:, half:] for r in far_refs], axis=0)
    ext_ref[0:n_far, :] = dot(undo[0:n_far], tail).astype(bf16)
    own = (iota((rows, rows), 0) == positive_ref[...]).astype(bf16)
    own_t = flip(own)
    for cols in column_tiles(width):
        o_ref[n_far:, cols] = dot(own_t, unit_ref[:, cols]).astype(bf16)
    ext_ref[n_far:, :] = dot(own_t, p_ext_ref[...]).astype(bf16)
    both_ref[...] = dot(o_ref[...], pair_ref[...], 1, 1)
    n_near = pick_ref.shape[0]
    mate_ext = mate_ref[:, width : width + lanes].astype(f32)
    rank = pair_ref.shape[0] - rows
    mate_inv_ref[...] = jnp.broadcast_to(
        mate_ext[:, rank : rank + 1] + mate_ext[:, rank + 1 : rank + 2], mate_inv_ref.shape
    )
    parts = []
    for i in range(0, n_near, rows):
        at = width + lanes * (1 + i // rows)
        parts.append(mate_ref[0 : min(rows, n_near - i), at : at + lanes])
    mate_pick = jnp.concatenate(parts, axis=0) if len(parts) > 1 else parts[0]
    row = iota((n_near, n_near), 0)
    col = iota((n_near, n_near), 1)
    core = place_ref[2]
    listed = (col // per_near) % 2 == core
    mine = (row == col) & listed
    shift = jnp.where(core == 0, per_near, -per_near)
    theirs = (row == col + shift) & listed
    own_rows = dot(mine.astype(bf16), pick_ref[...]).astype(bf16)
    mate_rows = dot(theirs.astype(bf16), mate_pick).astype(bf16)
    owner_ref[0:rows, :] = flip(own_rows)
    owner_ref[rows:, :] = flip(mate_rows)[0:rows]


def score_kernel(
    slope, rank, near_ref, pair_ref, other_both_hbm, near_count_ref, other_count_ref, shadow_hbm,
    ret_ref, g_ref, radial_ref, near_up_ref, other_both_ref, shadow_ref, sems,
):
    copies = fetch([(other_both_hbm, other_both_ref), (shadow_hbm, shadow_ref)], sems)
    width = pair_ref.shape[1]
    n_near, rows = near_count_ref.shape
    both = dot(near_ref[:, :width], pair_ref[...], 1, 1)
    near_raw, near_up = both[:, 0:rows], both[:, rows:]
    near_up_ref[...] = near_up
    for c in copies:
        c.wait()
    other_raw = other_both_ref[:, 0:rows]
    n_other = other_raw.shape[0]
    n_far = n_other - rows
    near_exp = jnp.exp(near_raw / logit_divisor - offset) * near_count_ref[...]
    other_exp = jnp.exp(other_raw / logit_divisor - offset) * other_count_ref[...]
    partition = jnp.sum(near_exp, axis=0, keepdims=True) + jnp.sum(
        other_exp, axis=0, keepdims=True
    )
    same = iota(other_raw.shape, 0) == iota(other_raw.shape, 1) + n_far
    matched = jnp.sum(jnp.where(same, other_raw, 0.0), axis=0, keepdims=True) / logit_divisor
    loss = jnp.sum(jnp.log(partition) + offset - matched, axis=1, keepdims=True)
    near_g = (near_exp / partition * slope).astype(bf16)
    other_g = ((other_exp / partition - same.astype(f32)) * slope).astype(bf16)
    g_ref[0:n_near, :] = near_g
    g_ref[n_near:, :] = other_g
    near_part = near_g.astype(f32) * near_raw
    other_part = other_g.astype(f32) * other_raw
    near_radial = jnp.sum(near_part, axis=1, keepdims=True)
    radial_ref[0:n_near, :] = near_radial
    radial_ref[n_near : n_near + n_other, :] = jnp.sum(other_part, axis=1, keepdims=True)
    q_radial = jnp.sum(near_part, axis=0, keepdims=True) + jnp.sum(
        other_part, axis=0, keepdims=True
    )
    square = iota((rows, rows), 0) == iota((rows, rows), 1)
    radial_ref[n_near + n_other :, :] = jnp.sum(
        jnp.where(square, q_radial, 0.0), axis=1, keepdims=True
    )
    back = dot(near_g, shadow_ref[0:rows, :]) + dot(near_g, shadow_ref[rows:, :])
    back = back - near_radial * near_up
    back = dot(back.astype(bf16), eye(rank, lanes))
    lane = iota((n_near, lanes), 1)
    high = loss.astype(bf16).astype(f32)
    back = jnp.where(lane == rank, high, back)
    back = jnp.where(lane == rank + 1, loss - high, back)
    ret_ref[...] = back.astype(bf16)


def halves(value):
    high = value.astype(bf16)
    return high, (value - high.astype(f32)).astype(bf16)


def wide_dot(a, value):
    high, low = halves(value)
    return dot(a, high) + dot(a, low)


def local_kernel(
    place_ref, near_ref, pair_ref, shadow_hbm, o_hbm, o_ext_hbm, x_far_hbm, q_ext_hbm, q_inv_hbm,
    p_inv_hbm, x_q_hbm, positive_hbm, g_hbm, radial_hbm, near_up_hbm, other_both_hbm,
    up_keep_ref, up_send_ref, down_ref, row_ref,
    shadow_ref, o_ref, o_ext_ref, x_far_ref, q_ext_ref, q_inv_ref, p_inv_ref, x_q_ref,
    positive_ref, g_ref, radial_ref, near_up_ref, other_both_ref, sems,
):
    pairs = [
        (g_hbm, g_ref), (radial_hbm, radial_ref), (q_ext_hbm, q_ext_ref), (o_ext_hbm, o_ext_ref),
        (o_hbm, o_ref), (positive_hbm, positive_ref), (q_inv_hbm, q_inv_ref), (p_inv_hbm, p_inv_ref),
        (shadow_hbm, shadow_ref), (near_up_hbm, near_up_ref), (other_both_hbm, other_both_ref),
        (x_far_hbm, x_far_ref), (x_q_hbm, x_q_ref),
    ]
    copies = fetch(pairs, sems)
    for c in copies[:4]:
        c.wait()
    rows, width = x_q_ref.shape
    rank = pair_ref.shape[0] - rows
    part = rank // 2
    n_near = near_ref.shape[0]
    n_far = o_ref.shape[0] - rows
    n_all = n_near + n_far + rows
    even = place_ref[2] == 0
    near_gt, other_gt = g_ref[0:n_near, :], g_ref[n_near:, :]
    near_g, other_g = flip(near_gt), flip(other_gt)
    near_radial = radial_ref[0:n_near, :]
    other_radial = radial_ref[n_near:n_all, :]
    q_radial = radial_ref[n_all:, :]
    q_ext, near_ext, o_ext = q_ext_ref[...], near_ref[:, width:], o_ext_ref[...]

    def spread(value):
        high, low = halves(value)
        return jnp.concatenate([flip(high)[0:rank], flip(low)[0:rank]], axis=0)

    near_a = spread(dot(near_gt, q_ext) - near_ext.astype(f32) * near_radial)
    other_a = spread(dot(other_gt, q_ext) - o_ext.astype(f32) * other_radial)
    q_a = spread(dot(near_g, near_ext) + dot(other_g, o_ext) - q_ext.astype(f32) * q_radial)
    all_a = jnp.concatenate([near_a, other_a, q_a], axis=1)
    copies[4].wait()
    for cols in column_tiles(width):
        stack = [near_ref[:, cols], o_ref[:, cols], pair_ref[0:rows, cols]]
        grad = dot(all_a, jnp.concatenate(stack, axis=0))
        grad = adapter_scale * (grad[0:rank] + grad[rank:])
        top, low = grad[0:part], grad[part:]
        store_blocks(up_keep_ref, cols, jnp.where(even, top, low))
        store_blocks(up_send_ref, cols, jnp.where(even, low, top).astype(bf16))
    for c in copies[5:]:
        c.wait()
    other_up = other_both_ref[:, rows:]
    q_back = wide_dot(near_g, near_up_ref[...]) + wide_dot(other_g, other_up)
    q_up = shadow_ref[0:rows, :].astype(f32) + shadow_ref[rows:, :].astype(f32)
    q_back = (q_back - q_up * q_radial).astype(bf16).astype(f32)
    other_back = dot(other_gt, shadow_ref[0:rows, :]) + dot(other_gt, shadow_ref[rows:, :])
    other_back = (other_back - other_up * other_radial).astype(bf16)
    own = (iota((rows, rows), 0) == positive_ref[...]).astype(bf16)
    wide = dot(other_back[n_far:], eye(rank, lanes)).astype(bf16)
    row_sum = dot(own, wide)
    row_ref[...] = jnp.where(iota(row_sum.shape, 1) < rank, row_sum, p_inv_ref[...])
    dz_q = (adapter_scale * q_inv_ref[:, 0:1] * q_back).astype(bf16)
    far_ext = o_ext[0:n_far, :].astype(f32)
    far_inv = far_ext[:, rank : rank + 1] + far_ext[:, rank + 1 : rank + 2]
    dz_f = (adapter_scale * far_inv * other_back[0:n_far].astype(f32)).astype(bf16)
    dz_t = flip(jnp.concatenate([dz_q, dz_f], axis=0))
    for cols in column_tiles(width):
        stack = jnp.concatenate([x_q_ref[:, cols], x_far_ref[:, cols]], axis=0)
        down_ref[:, cols] = dot(dz_t, stack)


def down_kernel(
    per_near, place_ref, ret_ref, owner_hbm, row_hbm, x_p_hbm, mate_hbm, mate_inv_hbm, down_hbm,
    up_keep_hbm, up_send_hbm,
    keep_ref, send_ref, loss_ref, owner_ref, row_ref, x_ref, mate_inv_ref, down_ref, sems,
):
    rank, width = down_ref.shape
    rows = row_ref.shape[0]
    part = rank // 2
    pairs = [
        (owner_hbm, owner_ref), (row_hbm, row_ref), (mate_inv_hbm, mate_inv_ref),
        (x_p_hbm, x_ref.at[0:rows]), (mate_hbm.at[:, 0:width], x_ref.at[rows : 2 * rows]),
        (down_hbm, down_ref),
        (up_send_hbm, send_ref.at[:, part:]), (up_keep_hbm, keep_ref.at[:, part:]),
    ]
    copies = fetch(pairs, sems)
    ret = ret_ref[...]
    for c in copies[:3]:
        c.wait()
    row_sum = dot(owner_ref[...], ret)[:, 0:rank]
    own = row_ref[:, rank : rank + 1] * (row_sum[0:rows] + row_ref[:, 0:rank])
    mate = mate_inv_ref[:, 0:1] * row_sum[rows:]
    dz_t = flip((adapter_scale * jnp.concatenate([own, mate], axis=0)).astype(bf16))
    for c in copies[3:6]:
        c.wait()
    even = place_ref[2] == 0
    for cols in column_tiles(width):
        grad = dot(dz_t, x_ref[:, cols]) + down_ref[:, cols]
        top, low = grad[0:part], grad[part:]
        store_blocks(keep_ref, cols, jnp.where(even, top, low))
        store_blocks(send_ref, cols, jnp.where(even, low, top).astype(bf16))
    first = iota(ret.shape, 0) % (2 * per_near) == 0
    lane = iota(ret.shape, 1)
    chosen = first & ((lane == rank) | (lane == rank + 1))
    share = jnp.sum(jnp.where(chosen, ret.astype(f32), 0.0), axis=1, keepdims=True)
    loss_ref[...] = jnp.broadcast_to(jnp.sum(share, axis=0, keepdims=True), loss_ref.shape)
    copies[6].wait()
    copies[7].wait()


def add_kernel(keep_ref, got_ref, out_ref):
    for i in range(keep_ref.shape[0]):
        out_ref[i] = (keep_ref[i] + got_ref[i].astype(f32)).astype(bf16)


def sum_blocks(ref, *at):
    acc = ref[(0, *at)].astype(f32)
    for i in range(1, ref.shape[0]):
        acc = acc + ref[(i, *at)].astype(f32)
    return acc


def spread_kernel(in_ref, out_ref):
    value = sum_blocks(in_ref).astype(bf16)
    for i in range(out_ref.shape[0]):
        out_ref[i] = value


def finish_kernel(in_ref, loss_ref, out_ref):
    loss = loss_ref[...]
    high = loss.astype(bf16).astype(f32)
    row = iota(loss.shape, 0)
    tail = jnp.where(row == 0, high, jnp.where(row == 1, loss - high, 0.0))
    if out_ref.shape[2] > lanes:
        tail = jnp.concatenate([tail] * (out_ref.shape[2] // lanes), axis=1)
    value = jnp.concatenate([sum_blocks(in_ref), tail], axis=0).astype(bf16)
    for i in range(out_ref.shape[0]):
        out_ref[i] = value


def output_kernel(queries, place_ref, mine_ref, other_ref, down_ref, up_ref, loss_ref):
    rank = down_ref.shape[0]
    part = rank // 2
    size = mine_ref.shape[2]
    even = place_ref[2] == 0
    loss = jnp.zeros((8, lanes), f32)
    for i in range(mine_ref.shape[0]):
        mine, other = mine_ref[i].astype(f32), other_ref[i].astype(f32)
        cols = slice(i * size, (i + 1) * size)
        top = jnp.where(even, mine[0:rank], other[0:rank])
        low = jnp.where(even, other[0:rank], mine[0:rank])
        down_ref[0:part, cols] = top[0:part]
        down_ref[part:, cols] = low[0:part]
        up_ref[0:part, cols] = top[part:]
        up_ref[part:, cols] = low[part:]
        loss = loss + mine[rank:, 0:lanes] + other[rank:, 0:lanes]
    loss_ref[...] = jnp.sum(loss, axis=0, keepdims=True)[:, 0:1] / queries


def call(kernel, outs, args, scratch=(), flops=0, moved=0, hbm=(), out_hbm=(), out_raw=(), limit=16):
    specs = []
    for i, a in enumerate(args):
        space = pltpu.SMEM if a.dtype == jnp.int32 and a.ndim == 1 else pltpu.VMEM
        specs.append(pl.BlockSpec(memory_space=pltpu.HBM if i in hbm else space))
    args = [
        pltpu.with_memory_space_constraint(a, pltpu.HBM) if i in hbm else a
        for i, a in enumerate(args)
    ]
    shapes = [
        pltpu.HBM(s, d) if i in out_hbm else jax.ShapeDtypeStruct(s, d)
        for i, (s, d) in enumerate(outs)
    ]
    return pl.pallas_call(
        kernel,
        out_shape=shapes,
        in_specs=specs,
        out_specs=[
            pl.BlockSpec(memory_space=pltpu.HBM if i in out_raw else pltpu.VMEM)
            for i in range(len(shapes))
        ],
        scratch_shapes=[pltpu.VMEM(*s) if isinstance(s, tuple) else s for s in scratch],
        compiler_params=pltpu.CompilerParams(vmem_limit_bytes=limit * 1024 * 1024),
        cost_estimate=pl.CostEstimate(flops=flops, bytes_accessed=moved, transcendentals=0),
    )(*args)


def exchange(x, axis, groups=None):
    return lax.all_to_all(
        x, axis, split_axis=0, concat_axis=0, tiled=True, axis_index_groups=groups
    )


def both_ways(size):
    ahead = [1] + list(range(size // 2, 1, -1))
    behind = [size - 1] + list(range(size // 2 + 1, size - 1))
    order = []
    for i in range(len(ahead)):
        order += ahead[i : i + 1] + behind[i : i + 1]
    return [d for i, d in enumerate(order) if d not in order[:i]]


def far_exchange(pieces, grid_x, grid_y, for_mate):
    group = [(x, y) for x in range(grid_x) for y in range(grid_y)]
    order = [0, *both_ways(grid_y)]
    got = [pieces[0]]
    for dy in order[1:]:
        pairs = [(x * grid_y + y, x * grid_y + (y + dy) % grid_y) for x, y in group]
        got.append(lax.ppermute(pieces[dy], "group", pairs))
    x, _, pick = for_mate
    rows, width = x.shape
    mate_width = width + lanes * (1 + -(-pick.shape[0] // rows))
    mate, *lines = call(
        lambda *refs: regroup_kernel(order, *refs),
        [((rows, mate_width), bf16)] + [((grid_y * 8, got[0].shape[1]), bf16)] * grid_x,
        (*got, *for_mate),
        [pltpu.SemaphoreType.DMA(())],
        moved=1000,
        hbm=(len(got),),
    )
    ended = [lines[0]]
    for dx in far_order(grid_x)[1:]:
        pairs = [(x * grid_y + y, (x + dx) % grid_x * grid_y + y) for x, y in group]
        ended.append(lax.ppermute(lines[dx], "group", pairs))
    return ended, mate


def far_order(size):
    return [0, *sorted(range(1, size), key=lambda d: -min(d, size - d))]


def make_body(grid_x, grid_y):
    def body(
        query_layer_input,
        query_frozen_base,
        passage_layer_input,
        passage_frozen_base,
        adapter_down_weight,
        adapter_up_weight,
        positive_passage_index,
        hard_negative_slots,
        group_peer_rows,
        remote_group_rows,
    ):
        n_dp = lax.axis_size("dp")
        n_group = lax.axis_size("group")
        rows, width = query_layer_input.shape
        rank = adapter_up_weight.shape[0]
        part = rank // 2
        queries = rows * n_dp * n_group
        slope = 16.0 / math.sqrt(queries) / logit_divisor
        g = lax.axis_index("group")
        place = jnp.stack([g // grid_y, g % grid_y, lax.axis_index("dp") % 2]).astype(jnp.int32)
        down_t = adapter_down_weight.T
        near_ids, far_ids = group_peer_rows.T, remote_group_rows.T
        per_near = group_peer_rows.shape[1]
        n_near = n_dp * per_near
        n_far = n_group * 2
        n_other = n_far + rows
        half = width // 2
        block = width // n_group
        near, p_unit, p_ext, p_inv, pick = call(
            passage_kernel,
            [
                ((n_near, width + lanes), bf16),
                ((rows, width), bf16),
                ((rows, lanes), bf16),
                ((rows, lanes), f32),
                ((n_near, rows), bf16),
            ],
            (passage_layer_input, passage_frozen_base, down_t, adapter_up_weight, near_ids),
            [
                ((rows, width), bf16),
                ((rows, width), bf16),
                (down_t.shape, bf16),
                (adapter_up_weight.shape, bf16),
                (near_ids.shape, jnp.int32),
                ((rows, width), f32),
                ((n_near, width + lanes), bf16),
                pltpu.SemaphoreType.DMA((5,)),
                pltpu.SemaphoreType.DMA((1 + len(column_tiles(width)),)),
            ],
            flops=300_000_000, moved=5_000_000, hbm=range(5), out_hbm=(0, 3), out_raw=(0,),
        )
        far = call(
            lambda *refs: far_pick_kernel(grid_x, grid_y, *refs),
            [((grid_x * 8, half + lanes), bf16)] * grid_y,
            (place, passage_layer_input, p_unit, p_ext, far_ids),
            flops=1000, moved=1000,
        )
        ring = [ring_spot(i, n_dp) for i in range(n_dp)]
        step = stride_of(grid_y)
        plane = [x * grid_y + y * step % grid_y for x in range(grid_x) for y in range(grid_y)]
        near = exchange(near.reshape(n_dp, per_near, width + lanes), "dp", [ring])
        near = near.reshape(n_near, width + lanes)
        far, mate = far_exchange(far, grid_x, grid_y, (passage_layer_input, p_ext, pick))
        swap = [(i, i ^ 1) for i in range(n_dp)]
        mate = lax.ppermute(mate, "dp", swap)
        q_pair, q_ext, q_inv, near_count, other_count, shadow = call(
            lambda *refs: query_kernel(grid_x, grid_y, per_near, *refs),
            [
                ((rows + rank, width), bf16),
                ((rows, lanes), bf16),
                ((rows, lanes), f32),
                ((n_near, rows), f32),
                ((n_other, rows), f32),
                ((2 * rows, rank), bf16),
            ],
            (
                place, query_layer_input, query_frozen_base, down_t, adapter_up_weight,
                hard_negative_slots.T,
            ),
            [
                ((rows, width), bf16),
                ((rows, width), bf16),
                (down_t.shape, bf16),
                (adapter_up_weight.shape, bf16),
                (hard_negative_slots.T.shape, jnp.int32),
                ((rows, width), f32),
                pltpu.SemaphoreType.DMA((5,)),
            ],
            flops=1000, moved=1000, hbm=range(1, 6), out_hbm=(1, 2, 5),
        )
        positive = positive_passage_index.reshape(1, rows)
        other, other_ext, x_far, other_both, owner, mate_inv = call(
            lambda *refs: far_kernel(grid_x, per_near, *refs),
            [
                ((n_other, width), bf16),
                ((n_other, lanes), bf16),
                ((n_far, width), bf16),
                ((n_other, rows + rank), f32),
                ((2 * rows, n_near), bf16),
                ((rows, lanes), f32),
            ],
            (place, *far, q_pair, p_unit, p_ext, positive, pick, mate),
            flops=1000, moved=1000, out_hbm=range(6),
        )
        ret, weights, radial, near_up = call(
            lambda *refs: score_kernel(slope, rank, *refs),
            [
                ((n_near, lanes), bf16),
                ((n_near + n_other, rows), bf16),
                ((n_near + n_other + rows, 1), f32),
                ((n_near, rank), f32),
            ],
            (near, q_pair, other_both, near_count, other_count, shadow),
            [
                ((n_other, rows + rank), f32),
                (shadow.shape, bf16),
                pltpu.SemaphoreType.DMA((2,)),
            ],
            flops=200_000_000, moved=3_000_000, hbm=(2, 5), out_hbm=(1, 2, 3),
        )
        cores = [ring[c::2] for c in range(2)]
        ret = exchange(ret.reshape(n_dp // 2, 2 * per_near, lanes), "dp", cores)
        ret = ret.reshape(n_near, lanes)
        up_keep, up_send, down_part, row_part = call(
            local_kernel,
            [
                ((n_group, part, block), f32),
                ((n_group, part, block), bf16),
                ((rank, width), f32),
                ((rows, lanes), f32),
            ],
            (
                place, near, q_pair, shadow, other, other_ext, x_far, q_ext, q_inv, p_inv,
                query_layer_input, positive, weights, radial, near_up, other_both,
            ),
            [
                (shadow.shape, bf16),
                ((n_other, width), bf16),
                ((n_other, lanes), bf16),
                ((n_far, width), bf16),
                ((rows, lanes), bf16),
                ((rows, lanes), f32),
                ((rows, lanes), f32),
                ((rows, width), bf16),
                ((1, rows), jnp.int32),
                (weights.shape, bf16),
                (radial.shape, f32),
                (near_up.shape, f32),
                (other_both.shape, f32),
                pltpu.SemaphoreType.DMA((13,)),
            ],
            flops=900_000_000, moved=9_000_000, hbm=range(3, 16), out_hbm=range(4),
        )
        keep, send, loss = call(
            lambda *refs: down_kernel(per_near, *refs),
            [
                ((n_group, rank, block), f32),
                ((n_group, rank, block), bf16),
                ((8, lanes), f32),
            ],
            (
                place, ret, owner, row_part, passage_layer_input, mate, mate_inv, down_part,
                up_keep, up_send,
            ),
            [
                (owner.shape, bf16),
                ((rows, lanes), f32),
                ((2 * rows, width), bf16),
                ((rows, lanes), f32),
                ((rank, width), f32),
                pltpu.SemaphoreType.DMA((8,)),
            ],
            flops=100_000_000, moved=3_000_000, hbm=range(2, 10),
        )
        got = lax.ppermute(send, "dp", swap)
        (sums,) = call(add_kernel, [((n_group, rank, block), bf16)], (keep, got), moved=2_500_000)
        sums = exchange(sums, "group", [plane])
        (sums,) = call(
            spread_kernel, [((n_dp // 2, rank, block), bf16)], (sums,), moved=1_000_000
        )
        sums = exchange(sums, "dp", cores)
        (sums,) = call(
            finish_kernel, [((n_group, rank + 8, block), bf16)], (sums, loss), moved=1_000_000
        )
        sums = exchange(sums, "group", [plane])
        other_sums = lax.ppermute(sums, "dp", swap)
        down, up, loss = call(
            lambda *refs: output_kernel(queries, *refs),
            [((rank, width), f32), ((rank, width), f32), ((1, 1), f32)],
            (place, sums, other_sums),
            moved=3_500_000,
        )
        return (down.T, up, loss.reshape(()))

    return body


def solution(mesh):
    n_group = mesh.shape["group"]
    grid_x = {32: 4, 4: 2}[n_group]
    both = P(("dp", "group"), None)
    placed = (both, both, both, both, P(), P(), P(("dp", "group")), both, both, both)
    return jax.shard_map(
        make_body(grid_x, n_group // grid_x),
        mesh=mesh,
        in_specs=placed,
        out_specs=(P(), P(), P()),
        check_vma=False,
    )
```

```python
import math

import jax
import jax.numpy as jnp
from jax import lax
from jax.experimental import pallas as pl
from jax.experimental.pallas import tpu as pltpu
from jax.sharding import PartitionSpec as P

f32 = jnp.float32
bf16 = jnp.bfloat16
adapter_scale = 2.0
logit_divisor = 0.05
epsilon = 1e-06
offset = 1.0 / logit_divisor
tile = 512
lanes = 128


def dot(a, b, ca=1, cb=0):
    return lax.dot_general(a, b, (((ca,), (cb,)), ((), ())), preferred_element_type=f32)


def iota(shape, dim):
    return lax.broadcasted_iota(jnp.int32, shape, dim)


def eye(n, m):
    return (iota((n, m), 0) == iota((n, m), 1)).astype(bf16)


def flip(a):
    return dot(eye(a.shape[1], a.shape[1]), a, 1, 1).astype(bf16)


def column_tiles(width):
    step = min(tile, width)
    return [slice(c, c + step) for c in range(0, width, step)]


def embed(x_ref, base_ref, down_ref, up_ref, unit_ref, ext_ref, inv_ref, raw_ref, ready=None):
    rows, width = x_ref.shape
    rank = up_ref.shape[0]
    latent = dot(x_ref[...], down_ref[...], 1, 1).astype(bf16)
    if ready is not None:
        ready()
    squares = jnp.zeros((rows, 1), f32)
    for cols in column_tiles(width):
        raw = base_ref[:, cols].astype(f32) + adapter_scale * dot(latent, up_ref[:, cols])
        raw_ref[:, cols] = raw
        squares = squares + jnp.sum(raw * raw, axis=1, keepdims=True)
    inverse = lax.rsqrt(squares + epsilon)
    for cols in column_tiles(width):
        unit_ref[0:rows, cols] = (raw_ref[:, cols] * inverse).astype(bf16)
    scaled = (latent.astype(f32) * inverse).astype(bf16)
    high = inverse.astype(bf16).astype(f32)
    lane = iota((rows, lanes), 1)
    ext = dot(scaled, eye(rank, lanes))
    ext = jnp.where(lane == rank, high, ext)
    ext = jnp.where(lane == rank + 1, inverse - high, ext)
    ext_ref[...] = ext.astype(bf16)
    inv_ref[...] = jnp.broadcast_to(inverse, inv_ref.shape)


def fetch(pairs, sems):
    copies = [pltpu.make_async_copy(a, b, sems.at[i]) for i, (a, b) in enumerate(pairs)]
    for c in copies:
        c.start()
    return copies


def stride_of(chips):
    return {12: 5, 8: 3, 3: 2}.get(chips, 1)


def ring_spot(position, n_dp):
    chips = n_dp // 2
    return (position // 2 * stride_of(chips)) % chips * 2 + position % 2


def passage_kernel(
    x_hbm, base_hbm, down_hbm, up_hbm, near_ids_hbm,
    near_hbm, unit_ref, ext_ref, inv_ref, pick_ref,
    x_ref, base_ref, down_ref, up_ref, near_ids_ref, raw_ref, near_ref, sems, out_sems,
):
    pairs = [
        (near_ids_hbm, near_ids_ref), (x_hbm, x_ref), (down_hbm, down_ref), (base_hbm, base_ref),
        (up_hbm, up_ref),
    ]
    copies = fetch(pairs, sems)
    copies[0].wait()
    rows, width = x_ref.shape
    per_near, n_near = near_ids_ref.shape
    count = per_near * n_near
    ids = near_ids_ref[...].astype(f32).astype(bf16)
    spot = ring_spot(iota((count, n_near), 0) // per_near, n_near)
    spread = (spot == iota((count, n_near), 1)).astype(bf16)
    table = dot(spread, ids, 1, 1)
    mine = iota((count, per_near), 0) % per_near == iota((count, per_near), 1)
    wanted = jnp.sum(jnp.where(mine, table, 0.0), axis=1, keepdims=True).astype(jnp.int32)
    pick = (iota((count, rows), 1) == wanted).astype(bf16)
    pick_ref[...] = pick
    copies[1].wait()
    copies[2].wait()

    def ready():
        copies[3].wait()
        copies[4].wait()

    embed(x_ref, base_ref, down_ref, up_ref, unit_ref, ext_ref, inv_ref, raw_ref, ready)
    near_ref[:, width:] = dot(pick, ext_ref[...]).astype(bf16)
    sent = []
    for i, cols in enumerate([slice(width, width + lanes), *column_tiles(width)]):
        if i:
            near_ref[:, cols] = dot(pick, unit_ref[:, cols]).astype(bf16)
        copy = pltpu.make_async_copy(near_ref.at[:, cols], near_hbm.at[:, cols], out_sems.at[i])
        copy.start()
        sent.append(copy)
    for copy in sent:
        copy.wait()


def far_pick_kernel(grid_x, grid_y, place_ref, x_ref, unit_ref, ext_ref, far_ids_ref, *far_refs):
    rows, width = x_ref.shape
    half = width // 2
    n_far = far_ids_ref.shape[1]
    total = n_far * 8
    size = grid_x * 8
    where_x, where_y = place_ref[0], place_ref[1]
    ids = far_ids_ref[...].astype(f32).astype(bf16)
    block = iota((total, n_far), 0) // 8
    to_x = (where_x + block % grid_x) % grid_x
    to_y = (where_y + block // grid_x) % grid_y
    spread = (to_x * grid_y + to_y == iota((total, n_far), 1)).astype(bf16)
    table = dot(spread, ids, 1, 1)
    mine = iota((total, 2), 0) % 2 == iota((total, 2), 1)
    wanted = jnp.sum(jnp.where(mine, table, 0.0), axis=1, keepdims=True).astype(jnp.int32)
    kind = (iota((total, 4 * rows), 0) // 2) % 4
    source = iota((total, 4 * rows), 1)
    choose = ((source // rows == kind) & (source % rows == wanted)).astype(bf16)
    for cols in column_tiles(half):
        later = slice(half + cols.start, half + cols.stop)
        stack = jnp.concatenate(
            [unit_ref[:, cols], unit_ref[:, later], x_ref[:, cols], x_ref[:, later]], axis=0
        )
        got = dot(choose, stack).astype(bf16)
        for dy in range(grid_y):
            far_refs[dy][:, cols] = got[dy * size : (dy + 1) * size]
    first = jnp.where(iota((total, rows), 0) // 2 % 4 == 0, wanted, -1)
    got = dot((iota((total, rows), 1) == first).astype(bf16), ext_ref[...]).astype(bf16)
    for dy in range(grid_y):
        far_refs[dy][:, half:] = got[dy * size : (dy + 1) * size]


def query_kernel(
    grid_x, grid_y, per_near, place_ref, x_hbm, base_hbm, down_hbm, up_hbm, slots_hbm,
    pair_ref, ext_ref, inv_ref, near_count_ref, other_count_ref, shadow_ref,
    x_ref, base_ref, down_ref, up_ref, slots_ref, raw_ref, sems,
):
    pairs = [
        (x_hbm, x_ref), (down_hbm, down_ref), (base_hbm, base_ref), (up_hbm, up_ref),
        (slots_hbm, slots_ref),
    ]
    for c in fetch(pairs, sems):
        c.wait()
    hard, rows = slots_ref.shape
    embed(x_ref, base_ref, down_ref, up_ref, pair_ref, ext_ref, inv_ref, raw_ref)
    pair_ref[rows:, :] = up_ref[...]
    product = dot(pair_ref[0:rows, :], up_ref[...], 1, 1)
    high = product.astype(bf16)
    shadow_ref[0:rows, :] = high
    shadow_ref[rows:, :] = (product - high.astype(f32)).astype(bf16)
    n_near = near_count_ref.shape[0]
    n_other = other_count_ref.shape[0]
    n_far = n_other - rows
    where_x, where_y = place_ref[0], place_ref[1]
    near_slot = iota((n_near, rows), 0)
    near_slot = ring_spot(near_slot // per_near, n_near // per_near) * per_near + near_slot % per_near
    spot = iota((n_other, rows), 0)
    block = spot // 2
    from_x = (where_x + grid_x - (block // grid_y) % grid_x) % grid_x
    from_y = (where_y + grid_y - block % grid_y) % grid_y
    far_slot = n_near + (from_x * grid_y + from_y) * 2 + spot % 2
    far_slot = jnp.where(spot < n_far, far_slot, -1)
    near_count = jnp.zeros((n_near, rows), f32)
    other_count = jnp.zeros((n_other, rows), f32)
    for k in range(hard):
        slot = slots_ref[k : k + 1, :]
        near_count = near_count + (near_slot == slot).astype(f32)
        other_count = other_count + (far_slot == slot).astype(f32)
    near_count_ref[...] = near_count
    other_count_ref[...] = jnp.where(spot < n_far, other_count, 1.0)


def store_blocks(ref, cols, value):
    size = ref.shape[2]
    step = min(size, cols.stop - cols.start)
    for c in range(cols.start, cols.stop, step):
        at = c % size
        block = value[:, c - cols.start : c - cols.start + step]
        ref[c // size, 0 : value.shape[0], at : at + step] = block


def regroup_kernel(order, *refs):
    size = 8
    count = refs[0].shape[0] // size
    n_in = len(order)
    refs = [refs[order.index(dy)] for dy in range(n_in)] + list(refs[n_in:])
    for dx in range(0, count, 2):
        for dy in range(0, n_in, 2):
            a, b = [refs[dy + i][dx * size : (dx + 2) * size, :] for i in range(2)]
            at = slice(dy * size, (dy + 2) * size)
            refs[n_in + dx][at, :] = jnp.concatenate([a[:size], b[:size]], axis=0)
            refs[n_in + dx + 1][at, :] = jnp.concatenate([a[size:], b[size:]], axis=0)


def far_kernel(count, *refs):
    order = far_order(count)
    far_refs = [refs[order.index(dx)] for dx in range(count)]
    pair_ref, unit_ref, p_ext_ref, positive_ref = refs[count : count + 4]
    o_ref, ext_ref, x_far_ref, both_ref = refs[count + 4 :]
    rows, width = unit_ref.shape
    half = width // 2
    total = far_refs[0].shape[0]
    each = total // 4
    n_far = each * count
    out_row = iota((total, total), 0)
    in_row = iota((total, total), 1)
    spot = out_row % each
    undo = (
        (in_row // 8 == spot // 2)
        & (in_row % 2 == spot % 2)
        & ((in_row // 2) % 4 == out_row // each)
    ).astype(bf16)
    for i, far_ref in enumerate(far_refs):
        at = slice(i * each, (i + 1) * each)
        for cols in column_tiles(half):
            later = slice(half + cols.start, half + cols.stop)
            got = dot(undo, far_ref[:, cols]).astype(bf16)
            o_ref[at, cols] = got[0:each]
            o_ref[at, later] = got[each : 2 * each]
            x_far_ref[at, cols] = got[2 * each : 3 * each]
            x_far_ref[at, later] = got[3 * each :]
        ext_ref[at, :] = dot(undo[0:each], far_ref[:, half:]).astype(bf16)
    own = (iota((rows, rows), 0) == positive_ref[...]).astype(bf16)
    own_t = flip(own)
    for cols in column_tiles(width):
        o_ref[n_far:, cols] = dot(own_t, unit_ref[:, cols]).astype(bf16)
    ext_ref[n_far:, :] = dot(own_t, p_ext_ref[...]).astype(bf16)
    both_ref[...] = dot(o_ref[...], pair_ref[...], 1, 1)


def score_kernel(
    slope, rank, near_ref, pair_ref, other_both_hbm, near_count_ref, other_count_ref, shadow_hbm,
    ret_ref, g_ref, radial_ref, near_up_ref, other_both_ref, shadow_ref, sems,
):
    copies = fetch([(other_both_hbm, other_both_ref), (shadow_hbm, shadow_ref)], sems)
    width = pair_ref.shape[1]
    n_near, rows = near_count_ref.shape
    both = dot(near_ref[:, :width], pair_ref[...], 1, 1)
    near_raw, near_up = both[:, 0:rows], both[:, rows:]
    near_up_ref[...] = near_up
    for c in copies:
        c.wait()
    other_raw = other_both_ref[:, 0:rows]
    n_other = other_raw.shape[0]
    n_far = n_other - rows
    near_exp = jnp.exp(near_raw / logit_divisor - offset) * near_count_ref[...]
    other_exp = jnp.exp(other_raw / logit_divisor - offset) * other_count_ref[...]
    partition = jnp.sum(near_exp, axis=0, keepdims=True) + jnp.sum(
        other_exp, axis=0, keepdims=True
    )
    same = iota(other_raw.shape, 0) == iota(other_raw.shape, 1) + n_far
    matched = jnp.sum(jnp.where(same, other_raw, 0.0), axis=0, keepdims=True) / logit_divisor
    loss = jnp.sum(jnp.log(partition) + offset - matched, axis=1, keepdims=True)
    near_g = (near_exp / partition * slope).astype(bf16)
    other_g = ((other_exp / partition - same.astype(f32)) * slope).astype(bf16)
    g_ref[0:n_near, :] = near_g
    g_ref[n_near:, :] = other_g
    near_part = near_g.astype(f32) * near_raw
    other_part = other_g.astype(f32) * other_raw
    near_radial = jnp.sum(near_part, axis=1, keepdims=True)
    radial_ref[0:n_near, :] = near_radial
    radial_ref[n_near : n_near + n_other, :] = jnp.sum(other_part, axis=1, keepdims=True)
    q_radial = jnp.sum(near_part, axis=0, keepdims=True) + jnp.sum(
        other_part, axis=0, keepdims=True
    )
    square = iota((rows, rows), 0) == iota((rows, rows), 1)
    radial_ref[n_near + n_other :, :] = jnp.sum(
        jnp.where(square, q_radial, 0.0), axis=1, keepdims=True
    )
    back = dot(near_g, shadow_ref[0:rows, :]) + dot(near_g, shadow_ref[rows:, :])
    back = back - near_radial * near_up
    back = dot(back.astype(bf16), eye(rank, lanes))
    lane = iota((n_near, lanes), 1)
    high = loss.astype(bf16).astype(f32)
    back = jnp.where(lane == rank, high, back)
    back = jnp.where(lane == rank + 1, loss - high, back)
    ret_ref[...] = back.astype(bf16)


def halves(value):
    high = value.astype(bf16)
    return high, (value - high.astype(f32)).astype(bf16)


def wide_dot(a, value):
    high, low = halves(value)
    return dot(a, high) + dot(a, low)


def local_kernel(
    place_ref, near_ref, pair_ref, shadow_hbm, o_hbm, o_ext_hbm, x_far_hbm, q_ext_hbm, q_inv_hbm,
    p_inv_hbm, x_q_hbm, positive_hbm, g_hbm, radial_hbm, near_up_hbm, other_both_hbm,
    up_keep_ref, up_send_ref, down_ref, row_ref,
    shadow_ref, o_ref, o_ext_ref, x_far_ref, q_ext_ref, q_inv_ref, p_inv_ref, x_q_ref,
    positive_ref, g_ref, radial_ref, near_up_ref, other_both_ref, sems,
):
    pairs = [
        (g_hbm, g_ref), (radial_hbm, radial_ref), (q_ext_hbm, q_ext_ref), (o_ext_hbm, o_ext_ref),
        (o_hbm, o_ref), (positive_hbm, positive_ref), (q_inv_hbm, q_inv_ref), (p_inv_hbm, p_inv_ref),
        (shadow_hbm, shadow_ref), (near_up_hbm, near_up_ref), (other_both_hbm, other_both_ref),
        (x_far_hbm, x_far_ref), (x_q_hbm, x_q_ref),
    ]
    copies = fetch(pairs, sems)
    for c in copies[:4]:
        c.wait()
    rows, width = x_q_ref.shape
    rank = pair_ref.shape[0] - rows
    part = rank // 2
    n_near = near_ref.shape[0]
    n_far = o_ref.shape[0] - rows
    n_all = n_near + n_far + rows
    even = place_ref[2] == 0
    near_gt, other_gt = g_ref[0:n_near, :], g_ref[n_near:, :]
    near_g, other_g = flip(near_gt), flip(other_gt)
    near_radial = radial_ref[0:n_near, :]
    other_radial = radial_ref[n_near:n_all, :]
    q_radial = radial_ref[n_all:, :]
    q_ext, near_ext, o_ext = q_ext_ref[...], near_ref[:, width:], o_ext_ref[...]

    def spread(value):
        high, low = halves(value)
        return jnp.concatenate([flip(high)[0:rank], flip(low)[0:rank]], axis=0)

    near_a = spread(dot(near_gt, q_ext) - near_ext.astype(f32) * near_radial)
    other_a = spread(dot(other_gt, q_ext) - o_ext.astype(f32) * other_radial)
    q_a = spread(dot(near_g, near_ext) + dot(other_g, o_ext) - q_ext.astype(f32) * q_radial)
    all_a = jnp.concatenate([near_a, other_a, q_a], axis=1)
    copies[4].wait()
    for cols in column_tiles(width):
        stack = [near_ref[:, cols], o_ref[:, cols], pair_ref[0:rows, cols]]
        grad = dot(all_a, jnp.concatenate(stack, axis=0))
        grad = adapter_scale * (grad[0:rank] + grad[rank:])
        top, low = grad[0:part], grad[part:]
        store_blocks(up_keep_ref, cols, jnp.where(even, top, low))
        store_blocks(up_send_ref, cols, jnp.where(even, low, top).astype(bf16))
    for c in copies[5:]:
        c.wait()
    other_up = other_both_ref[:, rows:]
    q_back = wide_dot(near_g, near_up_ref[...]) + wide_dot(other_g, other_up)
    q_up = shadow_ref[0:rows, :].astype(f32) + shadow_ref[rows:, :].astype(f32)
    q_back = (q_back - q_up * q_radial).astype(bf16).astype(f32)
    other_back = dot(other_gt, shadow_ref[0:rows, :]) + dot(other_gt, shadow_ref[rows:, :])
    other_back = (other_back - other_up * other_radial).astype(bf16)
    own = (iota((rows, rows), 0) == positive_ref[...]).astype(bf16)
    wide = dot(other_back[n_far:], eye(rank, lanes)).astype(bf16)
    row_sum = dot(own, wide)
    row_ref[...] = jnp.where(iota(row_sum.shape, 1) < rank, row_sum, p_inv_ref[...])
    dz_q = (adapter_scale * q_inv_ref[:, 0:1] * q_back).astype(bf16)
    far_ext = o_ext[0:n_far, :].astype(f32)
    far_inv = far_ext[:, rank : rank + 1] + far_ext[:, rank + 1 : rank + 2]
    dz_f = (adapter_scale * far_inv * other_back[0:n_far].astype(f32)).astype(bf16)
    dz_t = flip(jnp.concatenate([dz_q, dz_f], axis=0))
    for cols in column_tiles(width):
        stack = jnp.concatenate([x_q_ref[:, cols], x_far_ref[:, cols]], axis=0)
        down_ref[:, cols] = dot(dz_t, stack)


def down_kernel(
    per_near, place_ref, ret_ref, pick_ref, row_hbm, x_p_ref, down_hbm,
    keep_ref, send_ref, loss_ref, row_ref, down_ref, sems,
):
    rank = down_ref.shape[0]
    part = rank // 2
    copies = fetch([(row_hbm, row_ref), (down_hbm, down_ref)], sems)
    ret = ret_ref[...]
    row_sum = dot(flip(pick_ref[...]), ret)[:, 0:rank]
    copies[0].wait()
    row_sum = row_sum + row_ref[:, 0:rank]
    dz_t = flip((adapter_scale * row_ref[:, rank : rank + 1] * row_sum).astype(bf16))
    copies[1].wait()
    even = place_ref[2] == 0
    for cols in column_tiles(x_p_ref.shape[1]):
        grad = dot(dz_t, x_p_ref[:, cols]) + down_ref[:, cols]
        top, low = grad[0:part], grad[part:]
        store_blocks(keep_ref, cols, jnp.where(even, top, low))
        store_blocks(send_ref, cols, jnp.where(even, low, top).astype(bf16))
    first = iota(ret.shape, 0) % per_near == 0
    lane = iota(ret.shape, 1)
    chosen = first & ((lane == rank) | (lane == rank + 1))
    share = jnp.sum(jnp.where(chosen, ret.astype(f32), 0.0), axis=1, keepdims=True)
    loss_ref[...] = jnp.broadcast_to(jnp.sum(share, axis=0, keepdims=True), loss_ref.shape)


def add_kernel(down_ref, got_down_ref, up_ref, got_up_ref, out_ref):
    part = down_ref.shape[1]
    for i in range(down_ref.shape[0]):
        out_ref[i, 0:part] = (down_ref[i] + got_down_ref[i].astype(f32)).astype(bf16)
        out_ref[i, part:] = (up_ref[i] + got_up_ref[i].astype(f32)).astype(bf16)


def sum_blocks(ref, *at):
    acc = ref[(0, *at)].astype(f32)
    for i in range(1, ref.shape[0]):
        acc = acc + ref[(i, *at)].astype(f32)
    return acc


def spread_kernel(in_ref, out_ref):
    value = sum_blocks(in_ref).astype(bf16)
    for i in range(out_ref.shape[0]):
        out_ref[i] = value


def finish_kernel(in_ref, loss_ref, out_ref):
    loss = loss_ref[...]
    high = loss.astype(bf16).astype(f32)
    row = iota(loss.shape, 0)
    tail = jnp.where(row == 0, high, jnp.where(row == 1, loss - high, 0.0))
    if out_ref.shape[2] > lanes:
        tail = jnp.concatenate([tail] * (out_ref.shape[2] // lanes), axis=1)
    value = jnp.concatenate([sum_blocks(in_ref), tail], axis=0).astype(bf16)
    for i in range(out_ref.shape[0]):
        out_ref[i] = value


def write_half(half, sums_ref, down_hbm, up_hbm, stage_ref, sems):
    count, _, size = sums_ref.shape
    part = stage_ref.shape[0] // 2
    at = pl.ds(pl.multiple_of(half * part, part), part)
    step = count // 4
    copies = []
    for i in range(count):
        cols = slice(i * size, (i + 1) * size)
        stage_ref[:, cols] = sums_ref[i, 0 : 2 * part].astype(f32)
        if (i + 1) % step == 0:
            k = i // step
            cols = slice(k * step * size, (k + 1) * step * size)
            for j, out in enumerate((down_hbm, up_hbm)):
                rows = slice(j * part, (j + 1) * part)
                copy = pltpu.make_async_copy(
                    stage_ref.at[rows, cols], out.at[at, cols], sems.at[2 * k + j]
                )
                copy.start()
                copies.append(copy)
    return copies


def own_half_kernel(queries, place_ref, mine_ref, down_hbm, up_hbm, loss_ref, stage_ref, sems):
    copies = write_half(place_ref[2], mine_ref, down_hbm, up_hbm, stage_ref, sems)
    rank = stage_ref.shape[0]
    loss = jnp.zeros((8, lanes), f32)
    for i in range(mine_ref.shape[0]):
        loss = loss + mine_ref[i, rank:, 0:lanes].astype(f32)
    loss_ref[...] = jnp.sum(loss, axis=0, keepdims=True)[:, 0:1] / queries
    for c in copies:
        c.wait()


def other_half_kernel(place_ref, other_ref, down_in, up_in, down_hbm, up_hbm, stage_ref, sems):
    for c in write_half(1 - place_ref[2], other_ref, down_hbm, up_hbm, stage_ref, sems):
        c.wait()


def call(kernel, outs, args, scratch=(), flops=0, moved=0, hbm=(), out_hbm=(), out_raw=(), alias=None, limit=16):
    specs = []
    for i, a in enumerate(args):
        space = pltpu.SMEM if a.dtype == jnp.int32 and a.ndim == 1 else pltpu.VMEM
        specs.append(pl.BlockSpec(memory_space=pltpu.HBM if i in hbm else space))
    args = [
        pltpu.with_memory_space_constraint(a, pltpu.HBM) if i in hbm else a
        for i, a in enumerate(args)
    ]
    shapes = [
        pltpu.HBM(s, d) if i in out_hbm else jax.ShapeDtypeStruct(s, d)
        for i, (s, d) in enumerate(outs)
    ]
    return pl.pallas_call(
        kernel,
        out_shape=shapes,
        in_specs=specs,
        out_specs=[
            pl.BlockSpec(memory_space=pltpu.HBM if i in out_raw else pltpu.VMEM)
            for i in range(len(shapes))
        ],
        input_output_aliases=alias or {},
        scratch_shapes=[pltpu.VMEM(*s) if isinstance(s, tuple) else s for s in scratch],
        compiler_params=pltpu.CompilerParams(vmem_limit_bytes=limit * 1024 * 1024),
        cost_estimate=pl.CostEstimate(flops=flops, bytes_accessed=moved, transcendentals=0),
    )(*args)


def exchange(x, axis, groups=None):
    return lax.all_to_all(
        x, axis, split_axis=0, concat_axis=0, tiled=True, axis_index_groups=groups
    )


def both_ways(size):
    ahead = [1] + list(range(size // 2, 1, -1))
    behind = [size - 1] + list(range(size // 2 + 1, size - 1))
    order = []
    for i in range(len(ahead)):
        order += ahead[i : i + 1] + behind[i : i + 1]
    return [d for i, d in enumerate(order) if d not in order[:i]]


def far_exchange(pieces, grid_x, grid_y):
    group = [(x, y) for x in range(grid_x) for y in range(grid_y)]
    order = [0, *both_ways(grid_y)]
    got = [pieces[0]]
    for dy in order[1:]:
        pairs = [(x * grid_y + y, x * grid_y + (y + dy) % grid_y) for x, y in group]
        got.append(lax.ppermute(pieces[dy], "group", pairs))
    lines = call(
        lambda *refs: regroup_kernel(order, *refs),
        [((grid_y * 8, got[0].shape[1]), bf16)] * grid_x,
        got,
        moved=1000,
    )
    ended = [lines[0]]
    for dx in far_order(grid_x)[1:]:
        pairs = [(x * grid_y + y, (x + dx) % grid_x * grid_y + y) for x, y in group]
        ended.append(lax.ppermute(lines[dx], "group", pairs))
    return ended


def far_order(size):
    return [0, *sorted(range(1, size), key=lambda d: -min(d, size - d))]


def make_body(grid_x, grid_y):
    def body(
        query_layer_input,
        query_frozen_base,
        passage_layer_input,
        passage_frozen_base,
        adapter_down_weight,
        adapter_up_weight,
        positive_passage_index,
        hard_negative_slots,
        group_peer_rows,
        remote_group_rows,
    ):
        n_dp = lax.axis_size("dp")
        n_group = lax.axis_size("group")
        rows, width = query_layer_input.shape
        rank = adapter_up_weight.shape[0]
        part = rank // 2
        queries = rows * n_dp * n_group
        slope = 16.0 / math.sqrt(queries) / logit_divisor
        g = lax.axis_index("group")
        place = jnp.stack([g // grid_y, g % grid_y, lax.axis_index("dp") % 2]).astype(jnp.int32)
        down_t = adapter_down_weight.T
        near_ids, far_ids = group_peer_rows.T, remote_group_rows.T
        per_near = group_peer_rows.shape[1]
        n_near = n_dp * per_near
        n_far = n_group * 2
        n_other = n_far + rows
        half = width // 2
        block = width // n_group
        near, p_unit, p_ext, p_inv, pick = call(
            passage_kernel,
            [
                ((n_near, width + lanes), bf16),
                ((rows, width), bf16),
                ((rows, lanes), bf16),
                ((rows, lanes), f32),
                ((n_near, rows), bf16),
            ],
            (passage_layer_input, passage_frozen_base, down_t, adapter_up_weight, near_ids),
            [
                ((rows, width), bf16),
                ((rows, width), bf16),
                (down_t.shape, bf16),
                (adapter_up_weight.shape, bf16),
                (near_ids.shape, jnp.int32),
                ((rows, width), f32),
                ((n_near, width + lanes), bf16),
                pltpu.SemaphoreType.DMA((5,)),
                pltpu.SemaphoreType.DMA((1 + len(column_tiles(width)),)),
            ],
            flops=300_000_000, moved=5_000_000, hbm=range(5), out_hbm=(0, 3), out_raw=(0,),
        )
        far = call(
            lambda *refs: far_pick_kernel(grid_x, grid_y, *refs),
            [((grid_x * 8, half + lanes), bf16)] * grid_y,
            (place, passage_layer_input, p_unit, p_ext, far_ids),
            flops=1000, moved=1000,
        )
        ring = [ring_spot(i, n_dp) for i in range(n_dp)]
        step = stride_of(grid_y)
        plane = [x * grid_y + y * step % grid_y for x in range(grid_x) for y in range(grid_y)]
        near = exchange(near.reshape(n_dp, per_near, width + lanes), "dp", [ring])
        near = near.reshape(n_near, width + lanes)
        far = far_exchange(far, grid_x, grid_y)
        q_pair, q_ext, q_inv, near_count, other_count, shadow = call(
            lambda *refs: query_kernel(grid_x, grid_y, per_near, *refs),
            [
                ((rows + rank, width), bf16),
                ((rows, lanes), bf16),
                ((rows, lanes), f32),
                ((n_near, rows), f32),
                ((n_other, rows), f32),
                ((2 * rows, rank), bf16),
            ],
            (
                place, query_layer_input, query_frozen_base, down_t, adapter_up_weight,
                hard_negative_slots.T,
            ),
            [
                ((rows, width), bf16),
                ((rows, width), bf16),
                (down_t.shape, bf16),
                (adapter_up_weight.shape, bf16),
                (hard_negative_slots.T.shape, jnp.int32),
                ((rows, width), f32),
                pltpu.SemaphoreType.DMA((5,)),
            ],
            flops=1000, moved=1000, hbm=range(1, 6), out_hbm=(1, 2, 5),
        )
        positive = positive_passage_index.reshape(1, rows)
        other, other_ext, x_far, other_both = call(
            lambda *refs: far_kernel(grid_x, *refs),
            [
                ((n_other, width), bf16),
                ((n_other, lanes), bf16),
                ((n_far, width), bf16),
                ((n_other, rows + rank), f32),
            ],
            (*far, q_pair, p_unit, p_ext, positive),
            flops=1000, moved=1000, out_hbm=range(4),
        )
        ret, weights, radial, near_up = call(
            lambda *refs: score_kernel(slope, rank, *refs),
            [
                ((n_near, lanes), bf16),
                ((n_near + n_other, rows), bf16),
                ((n_near + n_other + rows, 1), f32),
                ((n_near, rank), f32),
            ],
            (near, q_pair, other_both, near_count, other_count, shadow),
            [
                ((n_other, rows + rank), f32),
                (shadow.shape, bf16),
                pltpu.SemaphoreType.DMA((2,)),
            ],
            flops=200_000_000, moved=3_000_000, hbm=(2, 5), out_hbm=(1, 2, 3),
        )
        ret = exchange(ret.reshape(n_dp, per_near, lanes), "dp", [ring]).reshape(n_near, lanes)
        up_keep, up_send, down_part, row_part = call(
            local_kernel,
            [
                ((n_group, part, block), f32),
                ((n_group, part, block), bf16),
                ((rank, width), f32),
                ((rows, lanes), f32),
            ],
            (
                place, near, q_pair, shadow, other, other_ext, x_far, q_ext, q_inv, p_inv,
                query_layer_input, positive, weights, radial, near_up, other_both,
            ),
            [
                (shadow.shape, bf16),
                ((n_other, width), bf16),
                ((n_other, lanes), bf16),
                ((n_far, width), bf16),
                ((rows, lanes), bf16),
                ((rows, lanes), f32),
                ((rows, lanes), f32),
                ((rows, width), bf16),
                ((1, rows), jnp.int32),
                (weights.shape, bf16),
                (radial.shape, f32),
                (near_up.shape, f32),
                (other_both.shape, f32),
                pltpu.SemaphoreType.DMA((13,)),
            ],
            flops=900_000_000, moved=9_000_000, hbm=range(3, 16), out_hbm=(2, 3),
        )
        swap = [(i, i ^ 1) for i in range(n_dp)]
        up_got = lax.ppermute(up_send, "dp", swap)
        keep, send, loss = call(
            lambda *refs: down_kernel(per_near, *refs),
            [
                ((n_group, part, block), f32),
                ((n_group, part, block), bf16),
                ((8, lanes), f32),
            ],
            (place, ret, pick, row_part, passage_layer_input, down_part),
            [((rows, lanes), f32), ((rank, width), f32), pltpu.SemaphoreType.DMA((2,))],
            flops=100_000_000, moved=3_000_000, hbm=(3, 5),
        )
        got = lax.ppermute(send, "dp", swap)
        (sums,) = call(
            add_kernel,
            [((n_group, rank, block), bf16)],
            (keep, got, up_keep, up_got),
            moved=2_500_000,
        )
        cores = [ring[c::2] for c in range(2)]
        sums = exchange(sums, "group", [plane])
        (sums,) = call(
            spread_kernel, [((n_dp // 2, rank, block), bf16)], (sums,), moved=1_000_000
        )
        sums = exchange(sums, "dp", cores)
        (sums,) = call(
            finish_kernel, [((n_group, rank + 8, block), bf16)], (sums, loss), moved=1_000_000
        )
        sums = exchange(sums, "group", [plane])
        other_sums = lax.ppermute(sums, "dp", swap)
        halves_out = [((rank, width), f32), ((rank, width), f32)]
        stage = [((rank, width), f32), pltpu.SemaphoreType.DMA((8,))]
        down, up, loss = call(
            lambda *refs: own_half_kernel(queries, *refs),
            [*halves_out, ((1, 1), f32)],
            (place, sums),
            stage, moved=1_500_000, out_hbm=(0, 1), out_raw=(0, 1),
        )
        down, up = call(
            other_half_kernel,
            halves_out,
            (place, other_sums, down, up),
            stage, moved=1_500_000, hbm=(2, 3), out_hbm=(0, 1), out_raw=(0, 1), alias={2: 0, 3: 1},
        )
        return (down.T, up, loss.reshape(()))

    return body


def solution(mesh):
    n_group = mesh.shape["group"]
    grid_x = {32: 4, 4: 2}[n_group]
    both = P(("dp", "group"), None)
    placed = (both, both, both, both, P(), P(), P(("dp", "group")), both, both, both)
    return jax.shard_map(
        make_body(grid_x, n_group // grid_x),
        mesh=mesh,
        in_specs=placed,
        out_specs=(P(), P(), P()),
        check_vma=False,
    )
```

```python
import math

import jax
import jax.numpy as jnp
from jax import lax
from jax.experimental import pallas as pl
from jax.experimental.pallas import tpu as pltpu
from jax.sharding import PartitionSpec as P

f32 = jnp.float32
bf16 = jnp.bfloat16
adapter_scale = 2.0
logit_divisor = 0.05
epsilon = 1e-06
offset = 1.0 / logit_divisor
tile = 512
lanes = 128


def dot(a, b, ca=1, cb=0):
    return lax.dot_general(a, b, (((ca,), (cb,)), ((), ())), preferred_element_type=f32)


def iota(shape, dim):
    return lax.broadcasted_iota(jnp.int32, shape, dim)


def eye(n, m):
    return (iota((n, m), 0) == iota((n, m), 1)).astype(bf16)


def flip(a):
    return dot(eye(a.shape[1], a.shape[1]), a, 1, 1).astype(bf16)


def column_tiles(width):
    step = min(tile, width)
    return [slice(c, c + step) for c in range(0, width, step)]


def embed(x_ref, base_ref, down_ref, up_ref, unit_ref, ext_ref, inv_ref, raw_ref, ready=None):
    rows, width = x_ref.shape
    rank = up_ref.shape[0]
    latent = dot(x_ref[...], down_ref[...], 1, 1).astype(bf16)
    if ready is not None:
        ready()
    squares = jnp.zeros((rows, 1), f32)
    for cols in column_tiles(width):
        raw = base_ref[:, cols].astype(f32) + adapter_scale * dot(latent, up_ref[:, cols])
        raw_ref[:, cols] = raw
        squares = squares + jnp.sum(raw * raw, axis=1, keepdims=True)
    inverse = lax.rsqrt(squares + epsilon)
    for cols in column_tiles(width):
        unit_ref[0:rows, cols] = (raw_ref[:, cols] * inverse).astype(bf16)
    scaled = (latent.astype(f32) * inverse).astype(bf16)
    high = inverse.astype(bf16).astype(f32)
    lane = iota((rows, lanes), 1)
    ext = dot(scaled, eye(rank, lanes))
    ext = jnp.where(lane == rank, high, ext)
    ext = jnp.where(lane == rank + 1, inverse - high, ext)
    ext_ref[...] = ext.astype(bf16)
    inv_ref[...] = jnp.broadcast_to(inverse, inv_ref.shape)


def fetch(pairs, sems):
    copies = [pltpu.make_async_copy(a, b, sems.at[i]) for i, (a, b) in enumerate(pairs)]
    for c in copies:
        c.start()
    return copies


def stride_of(chips):
    return {12: 5, 8: 3, 3: 2}.get(chips, 1)


def ring_spot(position, n_dp):
    chips = n_dp // 2
    return (position // 2 * stride_of(chips)) % chips * 2 + position % 2


def passage_kernel(
    x_hbm, base_hbm, down_hbm, up_hbm, near_ids_hbm,
    near_hbm, unit_ref, ext_ref, inv_ref, pick_ref,
    x_ref, base_ref, down_ref, up_ref, near_ids_ref, raw_ref, near_ref, sems, out_sems,
):
    pairs = [
        (near_ids_hbm, near_ids_ref), (x_hbm, x_ref), (down_hbm, down_ref), (base_hbm, base_ref),
        (up_hbm, up_ref),
    ]
    copies = fetch(pairs, sems)
    copies[0].wait()
    rows, width = x_ref.shape
    per_near, n_near = near_ids_ref.shape
    count = per_near * n_near
    ids = near_ids_ref[...].astype(f32).astype(bf16)
    spot = ring_spot(iota((count, n_near), 0) // per_near, n_near)
    spread = (spot == iota((count, n_near), 1)).astype(bf16)
    table = dot(spread, ids, 1, 1)
    mine = iota((count, per_near), 0) % per_near == iota((count, per_near), 1)
    wanted = jnp.sum(jnp.where(mine, table, 0.0), axis=1, keepdims=True).astype(jnp.int32)
    pick = (iota((count, rows), 1) == wanted).astype(bf16)
    pick_ref[...] = pick
    copies[1].wait()
    copies[2].wait()

    def ready():
        copies[3].wait()
        copies[4].wait()

    embed(x_ref, base_ref, down_ref, up_ref, unit_ref, ext_ref, inv_ref, raw_ref, ready)
    near_ref[:, width:] = dot(pick, ext_ref[...]).astype(bf16)
    sent = []
    for i, cols in enumerate([slice(width, width + lanes), *column_tiles(width)]):
        if i:
            near_ref[:, cols] = dot(pick, unit_ref[:, cols]).astype(bf16)
        copy = pltpu.make_async_copy(near_ref.at[:, cols], near_hbm.at[:, cols], out_sems.at[i])
        copy.start()
        sent.append(copy)
    for copy in sent:
        copy.wait()


def far_pick_kernel(grid_x, grid_y, place_ref, x_ref, unit_ref, ext_ref, far_ids_ref, *far_refs):
    rows, width = x_ref.shape
    half = width // 2
    n_far = far_ids_ref.shape[1]
    total = n_far * 8
    size = grid_x * 8
    where_x, where_y = place_ref[0], place_ref[1]
    ids = far_ids_ref[...].astype(f32).astype(bf16)
    block = iota((total, n_far), 0) // 8
    to_x = (where_x + block % grid_x) % grid_x
    to_y = (where_y + block // grid_x) % grid_y
    spread = (to_x * grid_y + to_y == iota((total, n_far), 1)).astype(bf16)
    table = dot(spread, ids, 1, 1)
    mine = iota((total, 2), 0) % 2 == iota((total, 2), 1)
    wanted = jnp.sum(jnp.where(mine, table, 0.0), axis=1, keepdims=True).astype(jnp.int32)
    kind = (iota((total, 4 * rows), 0) // 2) % 4
    source = iota((total, 4 * rows), 1)
    choose = ((source // rows == kind) & (source % rows == wanted)).astype(bf16)
    for cols in column_tiles(half):
        later = slice(half + cols.start, half + cols.stop)
        stack = jnp.concatenate(
            [unit_ref[:, cols], unit_ref[:, later], x_ref[:, cols], x_ref[:, later]], axis=0
        )
        got = dot(choose, stack).astype(bf16)
        for dy in range(grid_y):
            far_refs[dy][:, cols] = got[dy * size : (dy + 1) * size]
    first = jnp.where(iota((total, rows), 0) // 2 % 4 == 0, wanted, -1)
    got = dot((iota((total, rows), 1) == first).astype(bf16), ext_ref[...]).astype(bf16)
    for dy in range(grid_y):
        far_refs[dy][:, half:] = got[dy * size : (dy + 1) * size]


def query_kernel(
    grid_x, grid_y, per_near, place_ref, x_hbm, base_hbm, down_hbm, up_hbm, slots_hbm,
    pair_ref, ext_ref, inv_ref, near_count_ref, other_count_ref, shadow_ref,
    x_ref, base_ref, down_ref, up_ref, slots_ref, raw_ref, sems,
):
    pairs = [
        (x_hbm, x_ref), (down_hbm, down_ref), (base_hbm, base_ref), (up_hbm, up_ref),
        (slots_hbm, slots_ref),
    ]
    for c in fetch(pairs, sems):
        c.wait()
    hard, rows = slots_ref.shape
    embed(x_ref, base_ref, down_ref, up_ref, pair_ref, ext_ref, inv_ref, raw_ref)
    pair_ref[rows:, :] = up_ref[...]
    product = dot(pair_ref[0:rows, :], up_ref[...], 1, 1)
    high = product.astype(bf16)
    shadow_ref[0:rows, :] = high
    shadow_ref[rows:, :] = (product - high.astype(f32)).astype(bf16)
    n_near = near_count_ref.shape[0]
    n_other = other_count_ref.shape[0]
    n_far = n_other - rows
    where_x, where_y = place_ref[0], place_ref[1]
    near_slot = iota((n_near, rows), 0)
    near_slot = ring_spot(near_slot // per_near, n_near // per_near) * per_near + near_slot % per_near
    spot = iota((n_other, rows), 0)
    block = spot // 2
    from_x = (where_x + grid_x - (block // grid_y) % grid_x) % grid_x
    from_y = (where_y + grid_y - block % grid_y) % grid_y
    far_slot = n_near + (from_x * grid_y + from_y) * 2 + spot % 2
    far_slot = jnp.where(spot < n_far, far_slot, -1)
    near_count = jnp.zeros((n_near, rows), f32)
    other_count = jnp.zeros((n_other, rows), f32)
    for k in range(hard):
        slot = slots_ref[k : k + 1, :]
        near_count = near_count + (near_slot == slot).astype(f32)
        other_count = other_count + (far_slot == slot).astype(f32)
    near_count_ref[...] = near_count
    other_count_ref[...] = jnp.where(spot < n_far, other_count, 1.0)


def store_blocks(ref, cols, value):
    size = ref.shape[2]
    step = min(size, cols.stop - cols.start)
    for c in range(cols.start, cols.stop, step):
        at = c % size
        block = value[:, c - cols.start : c - cols.start + step]
        ref[c // size, 0 : value.shape[0], at : at + step] = block


def regroup_kernel(order, *refs):
    size = 8
    count = refs[0].shape[0] // size
    n_in = len(order)
    refs = [refs[order.index(dy)] for dy in range(n_in)] + list(refs[n_in:])
    for dx in range(0, count, 2):
        for dy in range(0, n_in, 2):
            a, b = [refs[dy + i][dx * size : (dx + 2) * size, :] for i in range(2)]
            at = slice(dy * size, (dy + 2) * size)
            refs[n_in + dx][at, :] = jnp.concatenate([a[:size], b[:size]], axis=0)
            refs[n_in + dx + 1][at, :] = jnp.concatenate([a[size:], b[size:]], axis=0)


def far_kernel(count, *refs):
    order = far_order(count)
    far_refs = [refs[order.index(dx)] for dx in range(count)]
    pair_ref, unit_ref, p_ext_ref, positive_ref = refs[count : count + 4]
    o_ref, ext_ref, x_far_ref, both_ref = refs[count + 4 :]
    rows, width = unit_ref.shape
    half = width // 2
    total = far_refs[0].shape[0]
    each = total // 4
    n_far = each * count
    out_row = iota((total, total), 0)
    in_row = iota((total, total), 1)
    spot = out_row % each
    undo = (
        (in_row // 8 == spot // 2)
        & (in_row % 2 == spot % 2)
        & ((in_row // 2) % 4 == out_row // each)
    ).astype(bf16)
    for i, far_ref in enumerate(far_refs):
        at = slice(i * each, (i + 1) * each)
        for cols in column_tiles(half):
            later = slice(half + cols.start, half + cols.stop)
            got = dot(undo, far_ref[:, cols]).astype(bf16)
            o_ref[at, cols] = got[0:each]
            o_ref[at, later] = got[each : 2 * each]
            x_far_ref[at, cols] = got[2 * each : 3 * each]
            x_far_ref[at, later] = got[3 * each :]
        ext_ref[at, :] = dot(undo[0:each], far_ref[:, half:]).astype(bf16)
    own = (iota((rows, rows), 0) == positive_ref[...]).astype(bf16)
    own_t = flip(own)
    for cols in column_tiles(width):
        o_ref[n_far:, cols] = dot(own_t, unit_ref[:, cols]).astype(bf16)
    ext_ref[n_far:, :] = dot(own_t, p_ext_ref[...]).astype(bf16)
    both_ref[...] = dot(o_ref[...], pair_ref[...], 1, 1)


def score_kernel(
    slope, rank, near_ref, pair_ref, other_both_hbm, near_count_ref, other_count_ref, shadow_hbm,
    ret_ref, g_ref, radial_ref, near_up_ref, other_both_ref, shadow_ref, sems,
):
    copies = fetch([(other_both_hbm, other_both_ref), (shadow_hbm, shadow_ref)], sems)
    width = pair_ref.shape[1]
    n_near, rows = near_count_ref.shape
    both = dot(near_ref[:, :width], pair_ref[...], 1, 1)
    near_raw, near_up = both[:, 0:rows], both[:, rows:]
    near_up_ref[...] = near_up
    for c in copies:
        c.wait()
    other_raw = other_both_ref[:, 0:rows]
    n_other = other_raw.shape[0]
    n_far = n_other - rows
    near_exp = jnp.exp(near_raw / logit_divisor - offset) * near_count_ref[...]
    other_exp = jnp.exp(other_raw / logit_divisor - offset) * other_count_ref[...]
    partition = jnp.sum(near_exp, axis=0, keepdims=True) + jnp.sum(
        other_exp, axis=0, keepdims=True
    )
    same = iota(other_raw.shape, 0) == iota(other_raw.shape, 1) + n_far
    matched = jnp.sum(jnp.where(same, other_raw, 0.0), axis=0, keepdims=True) / logit_divisor
    loss = jnp.sum(jnp.log(partition) + offset - matched, axis=1, keepdims=True)
    near_g = (near_exp / partition * slope).astype(bf16)
    other_g = ((other_exp / partition - same.astype(f32)) * slope).astype(bf16)
    g_ref[0:n_near, :] = near_g
    g_ref[n_near:, :] = other_g
    near_part = near_g.astype(f32) * near_raw
    other_part = other_g.astype(f32) * other_raw
    near_radial = jnp.sum(near_part, axis=1, keepdims=True)
    radial_ref[0:n_near, :] = near_radial
    radial_ref[n_near : n_near + n_other, :] = jnp.sum(other_part, axis=1, keepdims=True)
    q_radial = jnp.sum(near_part, axis=0, keepdims=True) + jnp.sum(
        other_part, axis=0, keepdims=True
    )
    square = iota((rows, rows), 0) == iota((rows, rows), 1)
    radial_ref[n_near + n_other :, :] = jnp.sum(
        jnp.where(square, q_radial, 0.0), axis=1, keepdims=True
    )
    back = dot(near_g, shadow_ref[0:rows, :]) + dot(near_g, shadow_ref[rows:, :])
    back = back - near_radial * near_up
    back = dot(back.astype(bf16), eye(rank, lanes))
    lane = iota((n_near, lanes), 1)
    high = loss.astype(bf16).astype(f32)
    back = jnp.where(lane == rank, high, back)
    back = jnp.where(lane == rank + 1, loss - high, back)
    ret_ref[...] = back.astype(bf16)


def halves(value):
    high = value.astype(bf16)
    return high, (value - high.astype(f32)).astype(bf16)


def wide_dot(a, value):
    high, low = halves(value)
    return dot(a, high) + dot(a, low)


def local_kernel(
    place_ref, near_ref, pair_ref, shadow_hbm, o_hbm, o_ext_hbm, x_far_hbm, q_ext_hbm, q_inv_hbm,
    p_inv_hbm, x_q_hbm, positive_hbm, g_hbm, radial_hbm, near_up_hbm, other_both_hbm,
    up_keep_ref, up_send_ref, down_ref, row_ref,
    shadow_ref, o_ref, o_ext_ref, x_far_ref, q_ext_ref, q_inv_ref, p_inv_ref, x_q_ref,
    positive_ref, g_ref, radial_ref, near_up_ref, other_both_ref, sems,
):
    pairs = [
        (g_hbm, g_ref), (radial_hbm, radial_ref), (q_ext_hbm, q_ext_ref), (o_ext_hbm, o_ext_ref),
        (o_hbm, o_ref), (positive_hbm, positive_ref), (q_inv_hbm, q_inv_ref), (p_inv_hbm, p_inv_ref),
        (shadow_hbm, shadow_ref), (near_up_hbm, near_up_ref), (other_both_hbm, other_both_ref),
        (x_far_hbm, x_far_ref), (x_q_hbm, x_q_ref),
    ]
    copies = fetch(pairs, sems)
    for c in copies[:4]:
        c.wait()
    rows, width = x_q_ref.shape
    rank = pair_ref.shape[0] - rows
    part = rank // 2
    n_near = near_ref.shape[0]
    n_far = o_ref.shape[0] - rows
    n_all = n_near + n_far + rows
    even = place_ref[2] == 0
    near_gt, other_gt = g_ref[0:n_near, :], g_ref[n_near:, :]
    near_g, other_g = flip(near_gt), flip(other_gt)
    near_radial = radial_ref[0:n_near, :]
    other_radial = radial_ref[n_near:n_all, :]
    q_radial = radial_ref[n_all:, :]
    q_ext, near_ext, o_ext = q_ext_ref[...], near_ref[:, width:], o_ext_ref[...]

    def spread(value):
        high, low = halves(value)
        return jnp.concatenate([flip(high)[0:rank], flip(low)[0:rank]], axis=0)

    near_a = spread(dot(near_gt, q_ext) - near_ext.astype(f32) * near_radial)
    other_a = spread(dot(other_gt, q_ext) - o_ext.astype(f32) * other_radial)
    q_a = spread(dot(near_g, near_ext) + dot(other_g, o_ext) - q_ext.astype(f32) * q_radial)
    all_a = jnp.concatenate([near_a, other_a, q_a], axis=1)
    copies[4].wait()
    for cols in column_tiles(width):
        stack = [near_ref[:, cols], o_ref[:, cols], pair_ref[0:rows, cols]]
        grad = dot(all_a, jnp.concatenate(stack, axis=0))
        grad = adapter_scale * (grad[0:rank] + grad[rank:])
        top, low = grad[0:part], grad[part:]
        store_blocks(up_keep_ref, cols, jnp.where(even, top, low))
        store_blocks(up_send_ref, cols, jnp.where(even, low, top).astype(bf16))
    for c in copies[5:]:
        c.wait()
    other_up = other_both_ref[:, rows:]
    q_back = wide_dot(near_g, near_up_ref[...]) + wide_dot(other_g, other_up)
    q_up = shadow_ref[0:rows, :].astype(f32) + shadow_ref[rows:, :].astype(f32)
    q_back = (q_back - q_up * q_radial).astype(bf16).astype(f32)
    other_back = dot(other_gt, shadow_ref[0:rows, :]) + dot(other_gt, shadow_ref[rows:, :])
    other_back = (other_back - other_up * other_radial).astype(bf16)
    own = (iota((rows, rows), 0) == positive_ref[...]).astype(bf16)
    wide = dot(other_back[n_far:], eye(rank, lanes)).astype(bf16)
    row_sum = dot(own, wide)
    row_ref[...] = jnp.where(iota(row_sum.shape, 1) < rank, row_sum, p_inv_ref[...])
    dz_q = (adapter_scale * q_inv_ref[:, 0:1] * q_back).astype(bf16)
    far_ext = o_ext[0:n_far, :].astype(f32)
    far_inv = far_ext[:, rank : rank + 1] + far_ext[:, rank + 1 : rank + 2]
    dz_f = (adapter_scale * far_inv * other_back[0:n_far].astype(f32)).astype(bf16)
    dz_t = flip(jnp.concatenate([dz_q, dz_f], axis=0))
    for cols in column_tiles(width):
        stack = jnp.concatenate([x_q_ref[:, cols], x_far_ref[:, cols]], axis=0)
        down_ref[:, cols] = dot(dz_t, stack)


def down_kernel(
    per_near, place_ref, ret_ref, pick_ref, row_hbm, x_p_ref, down_hbm, up_keep_hbm, up_send_hbm,
    keep_ref, send_ref, loss_ref, row_ref, down_ref, sems,
):
    rank = down_ref.shape[0]
    part = rank // 2
    pairs = [
        (row_hbm, row_ref), (down_hbm, down_ref),
        (up_send_hbm, send_ref.at[:, part:]), (up_keep_hbm, keep_ref.at[:, part:]),
    ]
    copies = fetch(pairs, sems)
    ret = ret_ref[...]
    row_sum = dot(flip(pick_ref[...]), ret)[:, 0:rank]
    copies[0].wait()
    row_sum = row_sum + row_ref[:, 0:rank]
    dz_t = flip((adapter_scale * row_ref[:, rank : rank + 1] * row_sum).astype(bf16))
    copies[1].wait()
    even = place_ref[2] == 0
    for cols in column_tiles(x_p_ref.shape[1]):
        grad = dot(dz_t, x_p_ref[:, cols]) + down_ref[:, cols]
        top, low = grad[0:part], grad[part:]
        store_blocks(keep_ref, cols, jnp.where(even, top, low))
        store_blocks(send_ref, cols, jnp.where(even, low, top).astype(bf16))
    first = iota(ret.shape, 0) % per_near == 0
    lane = iota(ret.shape, 1)
    chosen = first & ((lane == rank) | (lane == rank + 1))
    share = jnp.sum(jnp.where(chosen, ret.astype(f32), 0.0), axis=1, keepdims=True)
    loss_ref[...] = jnp.broadcast_to(jnp.sum(share, axis=0, keepdims=True), loss_ref.shape)
    copies[2].wait()
    copies[3].wait()


def add_kernel(keep_ref, got_ref, out_ref):
    for i in range(keep_ref.shape[0]):
        out_ref[i] = (keep_ref[i] + got_ref[i].astype(f32)).astype(bf16)


def sum_blocks(ref, *at):
    acc = ref[(0, *at)].astype(f32)
    for i in range(1, ref.shape[0]):
        acc = acc + ref[(i, *at)].astype(f32)
    return acc


def spread_kernel(in_ref, out_ref):
    value = sum_blocks(in_ref).astype(bf16)
    for i in range(out_ref.shape[0]):
        out_ref[i] = value


def finish_kernel(in_ref, loss_ref, out_ref):
    loss = loss_ref[...]
    high = loss.astype(bf16).astype(f32)
    row = iota(loss.shape, 0)
    tail = jnp.where(row == 0, high, jnp.where(row == 1, loss - high, 0.0))
    if out_ref.shape[2] > lanes:
        tail = jnp.concatenate([tail] * (out_ref.shape[2] // lanes), axis=1)
    value = jnp.concatenate([sum_blocks(in_ref), tail], axis=0).astype(bf16)
    for i in range(out_ref.shape[0]):
        out_ref[i] = value


def output_kernel(queries, place_ref, mine_ref, other_ref, down_ref, up_ref, loss_ref):
    rank = down_ref.shape[0]
    part = rank // 2
    size = mine_ref.shape[2]
    even = place_ref[2] == 0
    loss = jnp.zeros((8, lanes), f32)
    for i in range(mine_ref.shape[0]):
        mine, other = mine_ref[i].astype(f32), other_ref[i].astype(f32)
        cols = slice(i * size, (i + 1) * size)
        top = jnp.where(even, mine[0:rank], other[0:rank])
        low = jnp.where(even, other[0:rank], mine[0:rank])
        down_ref[0:part, cols] = top[0:part]
        down_ref[part:, cols] = low[0:part]
        up_ref[0:part, cols] = top[part:]
        up_ref[part:, cols] = low[part:]
        loss = loss + mine[rank:, 0:lanes]
    loss_ref[...] = jnp.sum(loss, axis=0, keepdims=True)[:, 0:1] / queries


def call(kernel, outs, args, scratch=(), flops=0, moved=0, hbm=(), out_hbm=(), out_raw=(), limit=16):
    specs = []
    for i, a in enumerate(args):
        space = pltpu.SMEM if a.dtype == jnp.int32 and a.ndim == 1 else pltpu.VMEM
        specs.append(pl.BlockSpec(memory_space=pltpu.HBM if i in hbm else space))
    args = [
        pltpu.with_memory_space_constraint(a, pltpu.HBM) if i in hbm else a
        for i, a in enumerate(args)
    ]
    shapes = [
        pltpu.HBM(s, d) if i in out_hbm else jax.ShapeDtypeStruct(s, d)
        for i, (s, d) in enumerate(outs)
    ]
    return pl.pallas_call(
        kernel,
        out_shape=shapes,
        in_specs=specs,
        out_specs=[
            pl.BlockSpec(memory_space=pltpu.HBM if i in out_raw else pltpu.VMEM)
            for i in range(len(shapes))
        ],
        scratch_shapes=[pltpu.VMEM(*s) if isinstance(s, tuple) else s for s in scratch],
        compiler_params=pltpu.CompilerParams(vmem_limit_bytes=limit * 1024 * 1024),
        cost_estimate=pl.CostEstimate(flops=flops, bytes_accessed=moved, transcendentals=0),
    )(*args)


def exchange(x, axis, groups=None):
    return lax.all_to_all(
        x, axis, split_axis=0, concat_axis=0, tiled=True, axis_index_groups=groups
    )


def both_ways(size):
    ahead = [1] + list(range(size // 2, 1, -1))
    behind = [size - 1] + list(range(size // 2 + 1, size - 1))
    order = []
    for i in range(len(ahead)):
        order += ahead[i : i + 1] + behind[i : i + 1]
    return [d for i, d in enumerate(order) if d not in order[:i]]


def far_exchange(pieces, grid_x, grid_y):
    group = [(x, y) for x in range(grid_x) for y in range(grid_y)]
    order = [0, *both_ways(grid_y)]
    got = [pieces[0]]
    for dy in order[1:]:
        pairs = [(x * grid_y + y, x * grid_y + (y + dy) % grid_y) for x, y in group]
        got.append(lax.ppermute(pieces[dy], "group", pairs))
    lines = call(
        lambda *refs: regroup_kernel(order, *refs),
        [((grid_y * 8, got[0].shape[1]), bf16)] * grid_x,
        got,
        moved=1000,
    )
    ended = [lines[0]]
    for dx in far_order(grid_x)[1:]:
        pairs = [(x * grid_y + y, (x + dx) % grid_x * grid_y + y) for x, y in group]
        ended.append(lax.ppermute(lines[dx], "group", pairs))
    return ended


def far_order(size):
    return [0, *sorted(range(1, size), key=lambda d: -min(d, size - d))]


def make_body(grid_x, grid_y):
    def body(
        query_layer_input,
        query_frozen_base,
        passage_layer_input,
        passage_frozen_base,
        adapter_down_weight,
        adapter_up_weight,
        positive_passage_index,
        hard_negative_slots,
        group_peer_rows,
        remote_group_rows,
    ):
        n_dp = lax.axis_size("dp")
        n_group = lax.axis_size("group")
        rows, width = query_layer_input.shape
        rank = adapter_up_weight.shape[0]
        part = rank // 2
        queries = rows * n_dp * n_group
        slope = 16.0 / math.sqrt(queries) / logit_divisor
        g = lax.axis_index("group")
        place = jnp.stack([g // grid_y, g % grid_y, lax.axis_index("dp") % 2]).astype(jnp.int32)
        down_t = adapter_down_weight.T
        near_ids, far_ids = group_peer_rows.T, remote_group_rows.T
        per_near = group_peer_rows.shape[1]
        n_near = n_dp * per_near
        n_far = n_group * 2
        n_other = n_far + rows
        half = width // 2
        block = width // n_group
        near, p_unit, p_ext, p_inv, pick = call(
            passage_kernel,
            [
                ((n_near, width + lanes), bf16),
                ((rows, width), bf16),
                ((rows, lanes), bf16),
                ((rows, lanes), f32),
                ((n_near, rows), bf16),
            ],
            (passage_layer_input, passage_frozen_base, down_t, adapter_up_weight, near_ids),
            [
                ((rows, width), bf16),
                ((rows, width), bf16),
                (down_t.shape, bf16),
                (adapter_up_weight.shape, bf16),
                (near_ids.shape, jnp.int32),
                ((rows, width), f32),
                ((n_near, width + lanes), bf16),
                pltpu.SemaphoreType.DMA((5,)),
                pltpu.SemaphoreType.DMA((1 + len(column_tiles(width)),)),
            ],
            flops=300_000_000, moved=5_000_000, hbm=range(5), out_hbm=(0, 3), out_raw=(0,),
        )
        far = call(
            lambda *refs: far_pick_kernel(grid_x, grid_y, *refs),
            [((grid_x * 8, half + lanes), bf16)] * grid_y,
            (place, passage_layer_input, p_unit, p_ext, far_ids),
            flops=1000, moved=1000,
        )
        ring = [ring_spot(i, n_dp) for i in range(n_dp)]
        step = stride_of(grid_y)
        plane = [x * grid_y + y * step % grid_y for x in range(grid_x) for y in range(grid_y)]
        near = exchange(near.reshape(n_dp, per_near, width + lanes), "dp", [ring])
        near = near.reshape(n_near, width + lanes)
        far = far_exchange(far, grid_x, grid_y)
        q_pair, q_ext, q_inv, near_count, other_count, shadow = call(
            lambda *refs: query_kernel(grid_x, grid_y, per_near, *refs),
            [
                ((rows + rank, width), bf16),
                ((rows, lanes), bf16),
                ((rows, lanes), f32),
                ((n_near, rows), f32),
                ((n_other, rows), f32),
                ((2 * rows, rank), bf16),
            ],
            (
                place, query_layer_input, query_frozen_base, down_t, adapter_up_weight,
                hard_negative_slots.T,
            ),
            [
                ((rows, width), bf16),
                ((rows, width), bf16),
                (down_t.shape, bf16),
                (adapter_up_weight.shape, bf16),
                (hard_negative_slots.T.shape, jnp.int32),
                ((rows, width), f32),
                pltpu.SemaphoreType.DMA((5,)),
            ],
            flops=1000, moved=1000, hbm=range(1, 6), out_hbm=(1, 2, 5),
        )
        positive = positive_passage_index.reshape(1, rows)
        other, other_ext, x_far, other_both = call(
            lambda *refs: far_kernel(grid_x, *refs),
            [
                ((n_other, width), bf16),
                ((n_other, lanes), bf16),
                ((n_far, width), bf16),
                ((n_other, rows + rank), f32),
            ],
            (*far, q_pair, p_unit, p_ext, positive),
            flops=1000, moved=1000, out_hbm=range(4),
        )
        ret, weights, radial, near_up = call(
            lambda *refs: score_kernel(slope, rank, *refs),
            [
                ((n_near, lanes), bf16),
                ((n_near + n_other, rows), bf16),
                ((n_near + n_other + rows, 1), f32),
                ((n_near, rank), f32),
            ],
            (near, q_pair, other_both, near_count, other_count, shadow),
            [
                ((n_other, rows + rank), f32),
                (shadow.shape, bf16),
                pltpu.SemaphoreType.DMA((2,)),
            ],
            flops=200_000_000, moved=3_000_000, hbm=(2, 5), out_hbm=(1, 2, 3),
        )
        ret = exchange(ret.reshape(n_dp, per_near, lanes), "dp", [ring]).reshape(n_near, lanes)
        up_keep, up_send, down_part, row_part = call(
            local_kernel,
            [
                ((n_group, part, block), f32),
                ((n_group, part, block), bf16),
                ((rank, width), f32),
                ((rows, lanes), f32),
            ],
            (
                place, near, q_pair, shadow, other, other_ext, x_far, q_ext, q_inv, p_inv,
                query_layer_input, positive, weights, radial, near_up, other_both,
            ),
            [
                (shadow.shape, bf16),
                ((n_other, width), bf16),
                ((n_other, lanes), bf16),
                ((n_far, width), bf16),
                ((rows, lanes), bf16),
                ((rows, lanes), f32),
                ((rows, lanes), f32),
                ((rows, width), bf16),
                ((1, rows), jnp.int32),
                (weights.shape, bf16),
                (radial.shape, f32),
                (near_up.shape, f32),
                (other_both.shape, f32),
                pltpu.SemaphoreType.DMA((13,)),
            ],
            flops=900_000_000, moved=9_000_000, hbm=range(3, 16), out_hbm=range(4),
        )
        swap = [(i, i ^ 1) for i in range(n_dp)]
        keep, send, loss = call(
            lambda *refs: down_kernel(per_near, *refs),
            [
                ((n_group, rank, block), f32),
                ((n_group, rank, block), bf16),
                ((8, lanes), f32),
            ],
            (place, ret, pick, row_part, passage_layer_input, down_part, up_keep, up_send),
            [((rows, lanes), f32), ((rank, width), f32), pltpu.SemaphoreType.DMA((4,))],
            flops=100_000_000, moved=3_000_000, hbm=(3, 5, 6, 7),
        )
        got = lax.ppermute(send, "dp", swap)
        (sums,) = call(add_kernel, [((n_group, rank, block), bf16)], (keep, got), moved=2_500_000)
        cores = [list(range(c, n_dp, 2)) for c in range(2)]
        sums = exchange(sums, "group", [plane])
        (sums,) = call(spread_kernel, [((1, rank, block), bf16)], (sums,), moved=1_000_000)
        sums = lax.all_gather(sums, "dp", axis=0, tiled=True, axis_index_groups=cores)
        (sums,) = call(
            finish_kernel, [((n_group, rank + 8, block), bf16)], (sums, loss), moved=1_000_000
        )
        sums = exchange(sums, "group", [plane])
        other_sums = lax.ppermute(sums, "dp", swap)
        down, up, loss = call(
            lambda *refs: output_kernel(queries, *refs),
            [((rank, width), f32), ((rank, width), f32), ((1, 1), f32)],
            (place, sums, other_sums),
            moved=3_500_000,
        )
        return (down.T, up, loss.reshape(()))

    return body


def solution(mesh):
    n_group = mesh.shape["group"]
    grid_x = {32: 4, 4: 2}[n_group]
    both = P(("dp", "group"), None)
    placed = (both, both, both, both, P(), P(), P(("dp", "group")), both, both, both)
    return jax.shard_map(
        make_body(grid_x, n_group // grid_x),
        mesh=mesh,
        in_specs=placed,
        out_specs=(P(), P(), P()),
        check_vma=False,
    )
```

```python
import math

import jax
import jax.numpy as jnp
from jax import lax
from jax.experimental import pallas as pl
from jax.experimental.pallas import tpu as pltpu
from jax.sharding import PartitionSpec as P

f32 = jnp.float32
bf16 = jnp.bfloat16
adapter_scale = 2.0
logit_divisor = 0.05
epsilon = 1e-06
offset = 1.0 / logit_divisor
tile = 512
lanes = 128


def dot(a, b, ca=1, cb=0):
    return lax.dot_general(a, b, (((ca,), (cb,)), ((), ())), preferred_element_type=f32)


def iota(shape, dim):
    return lax.broadcasted_iota(jnp.int32, shape, dim)


def eye(n, m):
    return (iota((n, m), 0) == iota((n, m), 1)).astype(bf16)


def flip(a):
    return dot(eye(a.shape[1], a.shape[1]), a, 1, 1).astype(bf16)


def column_tiles(width):
    step = min(tile, width)
    return [slice(c, c + step) for c in range(0, width, step)]


def embed(x_ref, base_ref, down_ref, up_ref, unit_ref, ext_ref, inv_ref, raw_ref, ready=None):
    rows, width = x_ref.shape
    rank = up_ref.shape[0]
    latent = dot(x_ref[...], down_ref[...], 1, 1).astype(bf16)
    if ready is not None:
        ready()
    squares = jnp.zeros((rows, 1), f32)
    for cols in column_tiles(width):
        raw = base_ref[:, cols].astype(f32) + adapter_scale * dot(latent, up_ref[:, cols])
        raw_ref[:, cols] = raw
        squares = squares + jnp.sum(raw * raw, axis=1, keepdims=True)
    inverse = lax.rsqrt(squares + epsilon)
    for cols in column_tiles(width):
        unit_ref[0:rows, cols] = (raw_ref[:, cols] * inverse).astype(bf16)
    scaled = (latent.astype(f32) * inverse).astype(bf16)
    high = inverse.astype(bf16).astype(f32)
    lane = iota((rows, lanes), 1)
    ext = dot(scaled, eye(rank, lanes))
    ext = jnp.where(lane == rank, high, ext)
    ext = jnp.where(lane == rank + 1, inverse - high, ext)
    ext_ref[...] = ext.astype(bf16)
    if inv_ref is not None:
        inv_ref[...] = jnp.broadcast_to(inverse, inv_ref.shape)


def fetch(pairs, sems):
    copies = [pltpu.make_async_copy(a, b, sems.at[i]) for i, (a, b) in enumerate(pairs)]
    for c in copies:
        c.start()
    return copies


def stride_of(chips):
    return {12: 5, 8: 3, 3: 2}.get(chips, 1)


def ring_spot(position, n_dp):
    chips = n_dp // 2
    return (position // 2 * stride_of(chips)) % chips * 2 + position % 2


def passage_kernel(
    x_hbm, base_hbm, down_hbm, up_hbm, near_ids_hbm,
    near_hbm, unit_ref, ext_ref, pick_ref,
    x_ref, base_ref, down_ref, up_ref, near_ids_ref, raw_ref, near_ref, sems, out_sems,
):
    pairs = [
        (near_ids_hbm, near_ids_ref), (x_hbm, x_ref), (down_hbm, down_ref), (base_hbm, base_ref),
        (up_hbm, up_ref),
    ]
    copies = fetch(pairs, sems)
    copies[0].wait()
    rows, width = x_ref.shape
    per_near, n_near = near_ids_ref.shape
    count = per_near * n_near
    ids = near_ids_ref[...].astype(f32).astype(bf16)
    spot = ring_spot(iota((count, n_near), 0) // per_near, n_near)
    spread = (spot == iota((count, n_near), 1)).astype(bf16)
    table = dot(spread, ids, 1, 1)
    mine = iota((count, per_near), 0) % per_near == iota((count, per_near), 1)
    wanted = jnp.sum(jnp.where(mine, table, 0.0), axis=1, keepdims=True).astype(jnp.int32)
    pick = (iota((count, rows), 1) == wanted).astype(bf16)
    pick_ref[...] = pick
    copies[1].wait()
    copies[2].wait()

    def ready():
        copies[3].wait()
        copies[4].wait()

    embed(x_ref, base_ref, down_ref, up_ref, unit_ref, ext_ref, None, raw_ref, ready)
    near_ref[:, width:] = dot(pick, ext_ref[...]).astype(bf16)
    sent = []
    for i, cols in enumerate([slice(width, width + lanes), *column_tiles(width)]):
        if i:
            near_ref[:, cols] = dot(pick, unit_ref[:, cols]).astype(bf16)
        copy = pltpu.make_async_copy(near_ref.at[:, cols], near_hbm.at[:, cols], out_sems.at[i])
        copy.start()
        sent.append(copy)
    for copy in sent:
        copy.wait()


def far_pick_kernel(grid_x, grid_y, place_ref, x_ref, unit_ref, ext_ref, far_ids_ref, *far_refs):
    rows, width = x_ref.shape
    half = width // 2
    n_far = far_ids_ref.shape[1]
    total = n_far * 8
    size = grid_x * 8
    where_x, where_y = place_ref[0], place_ref[1]
    ids = far_ids_ref[...].astype(f32).astype(bf16)
    block = iota((total, n_far), 0) // 8
    to_x = (where_x + block % grid_x) % grid_x
    to_y = (where_y + block // grid_x) % grid_y
    spread = (to_x * grid_y + to_y == iota((total, n_far), 1)).astype(bf16)
    table = dot(spread, ids, 1, 1)
    mine = iota((total, 2), 0) % 2 == iota((total, 2), 1)
    wanted = jnp.sum(jnp.where(mine, table, 0.0), axis=1, keepdims=True).astype(jnp.int32)
    kind = (iota((total, 4 * rows), 0) // 2) % 4
    source = iota((total, 4 * rows), 1)
    choose = ((source // rows == kind) & (source % rows == wanted)).astype(bf16)
    for cols in column_tiles(half):
        later = slice(half + cols.start, half + cols.stop)
        stack = jnp.concatenate(
            [unit_ref[:, cols], unit_ref[:, later], x_ref[:, cols], x_ref[:, later]], axis=0
        )
        got = dot(choose, stack).astype(bf16)
        for dy in range(grid_y):
            far_refs[dy][:, cols] = got[dy * size : (dy + 1) * size]
    first = jnp.where(iota((total, rows), 0) // 2 % 4 == 0, wanted, -1)
    got = dot((iota((total, rows), 1) == first).astype(bf16), ext_ref[...]).astype(bf16)
    for dy in range(grid_y):
        far_refs[dy][:, half:] = got[dy * size : (dy + 1) * size]


def query_kernel(
    grid_x, grid_y, per_near, place_ref, x_hbm, base_hbm, down_hbm, up_hbm, slots_hbm,
    pair_ref, ext_ref, inv_ref, near_count_ref, other_count_ref, shadow_ref,
    x_ref, base_ref, down_ref, up_ref, slots_ref, raw_ref, sems,
):
    pairs = [
        (x_hbm, x_ref), (down_hbm, down_ref), (base_hbm, base_ref), (up_hbm, up_ref),
        (slots_hbm, slots_ref),
    ]
    for c in fetch(pairs, sems):
        c.wait()
    hard, rows = slots_ref.shape
    embed(x_ref, base_ref, down_ref, up_ref, pair_ref, ext_ref, inv_ref, raw_ref)
    pair_ref[rows:, :] = up_ref[...]
    product = dot(pair_ref[0:rows, :], up_ref[...], 1, 1)
    high = product.astype(bf16)
    shadow_ref[0:rows, :] = high
    shadow_ref[rows:, :] = (product - high.astype(f32)).astype(bf16)
    n_near = near_count_ref.shape[0]
    n_other = other_count_ref.shape[0]
    n_far = n_other - rows
    where_x, where_y = place_ref[0], place_ref[1]
    near_slot = iota((n_near, rows), 0)
    near_slot = ring_spot(near_slot // per_near, n_near // per_near) * per_near + near_slot % per_near
    spot = iota((n_other, rows), 0)
    block = spot // 2
    from_x = (where_x + grid_x - (block // grid_y) % grid_x) % grid_x
    from_y = (where_y + grid_y - block % grid_y) % grid_y
    far_slot = n_near + (from_x * grid_y + from_y) * 2 + spot % 2
    far_slot = jnp.where(spot < n_far, far_slot, -1)
    near_count = jnp.zeros((n_near, rows), f32)
    other_count = jnp.zeros((n_other, rows), f32)
    for k in range(hard):
        slot = slots_ref[k : k + 1, :]
        near_count = near_count + (near_slot == slot).astype(f32)
        other_count = other_count + (far_slot == slot).astype(f32)
    near_count_ref[...] = near_count
    other_count_ref[...] = jnp.where(spot < n_far, other_count, 1.0)


def store_blocks(ref, cols, value):
    size = ref.shape[2]
    step = min(size, cols.stop - cols.start)
    for c in range(cols.start, cols.stop, step):
        at = c % size
        block = value[:, c - cols.start : c - cols.start + step]
        ref[c // size, 0 : value.shape[0], at : at + step] = block


def regroup_kernel(order, *refs):
    size = 8
    count = refs[0].shape[0] // size
    n_in = len(order)
    refs = [refs[order.index(dy)] for dy in range(n_in)] + list(refs[n_in:])
    for dx in range(0, count, 2):
        for dy in range(0, n_in, 2):
            a, b = [refs[dy + i][dx * size : (dx + 2) * size, :] for i in range(2)]
            at = slice(dy * size, (dy + 2) * size)
            refs[n_in + dx][at, :] = jnp.concatenate([a[:size], b[:size]], axis=0)
            refs[n_in + dx + 1][at, :] = jnp.concatenate([a[size:], b[size:]], axis=0)


def far_kernel(count, *refs):
    order = far_order(count)
    far_refs = [refs[order.index(dx)] for dx in range(count)]
    pair_ref, unit_ref, p_ext_ref, positive_ref = refs[count : count + 4]
    o_ref, ext_ref, x_far_ref, both_ref, p_inv_ref = refs[count + 4 :]
    rows, width = unit_ref.shape
    half = width // 2
    total = far_refs[0].shape[0]
    each = total // 4
    n_far = each * count
    out_row = iota((total, total), 0)
    in_row = iota((total, total), 1)
    spot = out_row % each
    undo = (
        (in_row // 8 == spot // 2)
        & (in_row % 2 == spot % 2)
        & ((in_row // 2) % 4 == out_row // each)
    ).astype(bf16)
    for i, far_ref in enumerate(far_refs):
        at = slice(i * each, (i + 1) * each)
        for cols in column_tiles(half):
            later = slice(half + cols.start, half + cols.stop)
            got = dot(undo, far_ref[:, cols]).astype(bf16)
            o_ref[at, cols] = got[0:each]
            o_ref[at, later] = got[each : 2 * each]
            x_far_ref[at, cols] = got[2 * each : 3 * each]
            x_far_ref[at, later] = got[3 * each :]
        ext_ref[at, :] = dot(undo[0:each], far_ref[:, half:]).astype(bf16)
    own = (iota((rows, rows), 0) == positive_ref[...]).astype(bf16)
    own_t = flip(own)
    for cols in column_tiles(width):
        o_ref[n_far:, cols] = dot(own_t, unit_ref[:, cols]).astype(bf16)
    ext_ref[n_far:, :] = dot(own_t, p_ext_ref[...]).astype(bf16)
    both_ref[...] = dot(o_ref[...], pair_ref[...], 1, 1)
    rank = pair_ref.shape[0] - rows
    ext = p_ext_ref[...].astype(f32)
    inverse = ext[:, rank : rank + 1] + ext[:, rank + 1 : rank + 2]
    p_inv_ref[...] = jnp.broadcast_to(inverse, p_inv_ref.shape)


def score_kernel(
    slope, rank, near_ref, pair_ref, other_both_hbm, near_count_ref, other_count_ref, shadow_hbm,
    ret_ref, g_ref, radial_ref, near_up_ref, other_both_ref, shadow_ref, sems,
):
    copies = fetch([(other_both_hbm, other_both_ref), (shadow_hbm, shadow_ref)], sems)
    width = pair_ref.shape[1]
    n_near, rows = near_count_ref.shape
    both = dot(near_ref[:, :width], pair_ref[...], 1, 1)
    near_raw, near_up = both[:, 0:rows], both[:, rows:]
    near_up_ref[...] = near_up
    for c in copies:
        c.wait()
    other_raw = other_both_ref[:, 0:rows]
    n_other = other_raw.shape[0]
    n_far = n_other - rows
    near_exp = jnp.exp(near_raw / logit_divisor - offset) * near_count_ref[...]
    other_exp = jnp.exp(other_raw / logit_divisor - offset) * other_count_ref[...]
    partition = jnp.sum(near_exp, axis=0, keepdims=True) + jnp.sum(
        other_exp, axis=0, keepdims=True
    )
    same = iota(other_raw.shape, 0) == iota(other_raw.shape, 1) + n_far
    matched = jnp.sum(jnp.where(same, other_raw, 0.0), axis=0, keepdims=True) / logit_divisor
    loss = jnp.sum(jnp.log(partition) + offset - matched, axis=1, keepdims=True)
    near_g = (near_exp / partition * slope).astype(bf16)
    other_g = ((other_exp / partition - same.astype(f32)) * slope).astype(bf16)
    g_ref[0:n_near, :] = near_g
    g_ref[n_near:, :] = other_g
    near_part = near_g.astype(f32) * near_raw
    other_part = other_g.astype(f32) * other_raw
    near_radial = jnp.sum(near_part, axis=1, keepdims=True)
    radial_ref[0:n_near, :] = near_radial
    radial_ref[n_near : n_near + n_other, :] = jnp.sum(other_part, axis=1, keepdims=True)
    q_radial = jnp.sum(near_part, axis=0, keepdims=True) + jnp.sum(
        other_part, axis=0, keepdims=True
    )
    square = iota((rows, rows), 0) == iota((rows, rows), 1)
    radial_ref[n_near + n_other :, :] = jnp.sum(
        jnp.where(square, q_radial, 0.0), axis=1, keepdims=True
    )
    back = dot(near_g, shadow_ref[0:rows, :]) + dot(near_g, shadow_ref[rows:, :])
    back = back - near_radial * near_up
    back = dot(back.astype(bf16), eye(rank, lanes))
    lane = iota((n_near, lanes), 1)
    high = loss.astype(bf16).astype(f32)
    back = jnp.where(lane == rank, high, back)
    back = jnp.where(lane == rank + 1, loss - high, back)
    ret_ref[...] = back.astype(bf16)


def halves(value):
    high = value.astype(bf16)
    return high, (value - high.astype(f32)).astype(bf16)


def wide_dot(a, value):
    high, low = halves(value)
    return dot(a, high) + dot(a, low)


def local_kernel(
    place_ref, near_ref, pair_ref, shadow_hbm, o_hbm, o_ext_hbm, x_far_hbm, q_ext_hbm, q_inv_hbm,
    p_inv_hbm, x_q_hbm, positive_hbm, g_hbm, radial_hbm, near_up_hbm, other_both_hbm,
    up_keep_ref, up_send_ref, down_ref, row_ref,
    shadow_ref, o_ref, o_ext_ref, x_far_ref, q_ext_ref, q_inv_ref, p_inv_ref, x_q_ref,
    positive_ref, g_ref, radial_ref, near_up_ref, other_both_ref, sems,
):
    pairs = [
        (g_hbm, g_ref), (radial_hbm, radial_ref), (q_ext_hbm, q_ext_ref), (o_ext_hbm, o_ext_ref),
        (o_hbm, o_ref), (positive_hbm, positive_ref), (q_inv_hbm, q_inv_ref), (p_inv_hbm, p_inv_ref),
        (shadow_hbm, shadow_ref), (near_up_hbm, near_up_ref), (other_both_hbm, other_both_ref),
        (x_far_hbm, x_far_ref), (x_q_hbm, x_q_ref),
    ]
    copies = fetch(pairs, sems)
    for c in copies[:4]:
        c.wait()
    rows, width = x_q_ref.shape
    rank = pair_ref.shape[0] - rows
    part = rank // 2
    n_near = near_ref.shape[0]
    n_far = o_ref.shape[0] - rows
    n_all = n_near + n_far + rows
    even = place_ref[2] == 0
    near_gt, other_gt = g_ref[0:n_near, :], g_ref[n_near:, :]
    near_g, other_g = flip(near_gt), flip(other_gt)
    near_radial = radial_ref[0:n_near, :]
    other_radial = radial_ref[n_near:n_all, :]
    q_radial = radial_ref[n_all:, :]
    q_ext, near_ext, o_ext = q_ext_ref[...], near_ref[:, width:], o_ext_ref[...]

    def spread(value):
        high, low = halves(value)
        return jnp.concatenate([flip(high)[0:rank], flip(low)[0:rank]], axis=0)

    near_a = spread(dot(near_gt, q_ext) - near_ext.astype(f32) * near_radial)
    other_a = spread(dot(other_gt, q_ext) - o_ext.astype(f32) * other_radial)
    q_a = spread(dot(near_g, near_ext) + dot(other_g, o_ext) - q_ext.astype(f32) * q_radial)
    all_a = jnp.concatenate([near_a, other_a, q_a], axis=1)
    copies[4].wait()
    for cols in column_tiles(width):
        stack = [near_ref[:, cols], o_ref[:, cols], pair_ref[0:rows, cols]]
        grad = dot(all_a, jnp.concatenate(stack, axis=0))
        grad = adapter_scale * (grad[0:rank] + grad[rank:])
        top, low = grad[0:part], grad[part:]
        store_blocks(up_keep_ref, cols, jnp.where(even, top, low))
        store_blocks(up_send_ref, cols, jnp.where(even, low, top).astype(bf16))
    for c in copies[5:]:
        c.wait()
    other_up = other_both_ref[:, rows:]
    q_back = wide_dot(near_g, near_up_ref[...]) + wide_dot(other_g, other_up)
    q_up = shadow_ref[0:rows, :].astype(f32) + shadow_ref[rows:, :].astype(f32)
    q_back = (q_back - q_up * q_radial).astype(bf16).astype(f32)
    other_back = dot(other_gt, shadow_ref[0:rows, :]) + dot(other_gt, shadow_ref[rows:, :])
    other_back = (other_back - other_up * other_radial).astype(bf16)
    own = (iota((rows, rows), 0) == positive_ref[...]).astype(bf16)
    wide = dot(other_back[n_far:], eye(rank, lanes)).astype(bf16)
    row_sum = dot(own, wide)
    row_ref[...] = jnp.where(iota(row_sum.shape, 1) < rank, row_sum, p_inv_ref[...])
    dz_q = (adapter_scale * q_inv_ref[:, 0:1] * q_back).astype(bf16)
    far_ext = o_ext[0:n_far, :].astype(f32)
    far_inv = far_ext[:, rank : rank + 1] + far_ext[:, rank + 1 : rank + 2]
    dz_f = (adapter_scale * far_inv * other_back[0:n_far].astype(f32)).astype(bf16)
    dz_t = flip(jnp.concatenate([dz_q, dz_f], axis=0))
    for cols in column_tiles(width):
        stack = jnp.concatenate([x_q_ref[:, cols], x_far_ref[:, cols]], axis=0)
        down_ref[:, cols] = dot(dz_t, stack)


def down_kernel(
    per_near, place_ref, ret_ref, pick_ref, row_hbm, x_p_ref, down_hbm, up_keep_hbm, up_send_hbm,
    keep_ref, send_ref, loss_ref, row_ref, down_ref, sems,
):
    rank = down_ref.shape[0]
    part = rank // 2
    pairs = [
        (row_hbm, row_ref), (down_hbm, down_ref),
        (up_send_hbm, send_ref.at[:, part:]), (up_keep_hbm, keep_ref.at[:, part:]),
    ]
    copies = fetch(pairs, sems)
    ret = ret_ref[...]
    row_sum = dot(flip(pick_ref[...]), ret)[:, 0:rank]
    copies[0].wait()
    row_sum = row_sum + row_ref[:, 0:rank]
    dz_t = flip((adapter_scale * row_ref[:, rank : rank + 1] * row_sum).astype(bf16))
    copies[1].wait()
    even = place_ref[2] == 0
    for cols in column_tiles(x_p_ref.shape[1]):
        grad = dot(dz_t, x_p_ref[:, cols]) + down_ref[:, cols]
        top, low = grad[0:part], grad[part:]
        store_blocks(keep_ref, cols, jnp.where(even, top, low))
        store_blocks(send_ref, cols, jnp.where(even, low, top).astype(bf16))
    first = iota(ret.shape, 0) % per_near == 0
    lane = iota(ret.shape, 1)
    chosen = first & ((lane == rank) | (lane == rank + 1))
    share = jnp.sum(jnp.where(chosen, ret.astype(f32), 0.0), axis=1, keepdims=True)
    loss_ref[...] = jnp.broadcast_to(jnp.sum(share, axis=0, keepdims=True), loss_ref.shape)
    copies[2].wait()
    copies[3].wait()


def add_kernel(keep_ref, got_ref, out_ref):
    for i in range(keep_ref.shape[0]):
        out_ref[i] = (keep_ref[i] + got_ref[i].astype(f32)).astype(bf16)


def sum_blocks(ref, *at):
    acc = ref[(0, *at)].astype(f32)
    for i in range(1, ref.shape[0]):
        acc = acc + ref[(i, *at)].astype(f32)
    return acc


def spread_kernel(in_ref, out_ref):
    value = sum_blocks(in_ref).astype(bf16)
    for i in range(out_ref.shape[0]):
        out_ref[i] = value


def finish_kernel(in_ref, loss_ref, out_ref):
    loss = loss_ref[...]
    high = loss.astype(bf16).astype(f32)
    row = iota(loss.shape, 0)
    tail = jnp.where(row == 0, high, jnp.where(row == 1, loss - high, 0.0))
    if out_ref.shape[2] > lanes:
        tail = jnp.concatenate([tail] * (out_ref.shape[2] // lanes), axis=1)
    value = jnp.concatenate([sum_blocks(in_ref), tail], axis=0).astype(bf16)
    for i in range(out_ref.shape[0]):
        out_ref[i] = value


def output_kernel(queries, place_ref, mine_ref, other_ref, down_ref, up_ref, loss_ref):
    rank = down_ref.shape[0]
    part = rank // 2
    size = mine_ref.shape[2]
    even = place_ref[2] == 0
    loss = jnp.zeros((8, lanes), f32)
    for i in range(mine_ref.shape[0]):
        mine, other = mine_ref[i].astype(f32), other_ref[i].astype(f32)
        cols = slice(i * size, (i + 1) * size)
        top = jnp.where(even, mine[0:rank], other[0:rank])
        low = jnp.where(even, other[0:rank], mine[0:rank])
        down_ref[0:part, cols] = top[0:part]
        down_ref[part:, cols] = low[0:part]
        up_ref[0:part, cols] = top[part:]
        up_ref[part:, cols] = low[part:]
        loss = loss + mine[rank:, 0:lanes]
    loss_ref[...] = jnp.sum(loss, axis=0, keepdims=True)[:, 0:1] / queries


def call(kernel, outs, args, scratch=(), flops=0, moved=0, hbm=(), out_hbm=(), out_raw=(), limit=16):
    specs = []
    for i, a in enumerate(args):
        space = pltpu.SMEM if a.dtype == jnp.int32 and a.ndim == 1 else pltpu.VMEM
        specs.append(pl.BlockSpec(memory_space=pltpu.HBM if i in hbm else space))
    args = [
        pltpu.with_memory_space_constraint(a, pltpu.HBM) if i in hbm else a
        for i, a in enumerate(args)
    ]
    shapes = [
        pltpu.HBM(s, d) if i in out_hbm else jax.ShapeDtypeStruct(s, d)
        for i, (s, d) in enumerate(outs)
    ]
    return pl.pallas_call(
        kernel,
        out_shape=shapes,
        in_specs=specs,
        out_specs=[
            pl.BlockSpec(memory_space=pltpu.HBM if i in out_raw else pltpu.VMEM)
            for i in range(len(shapes))
        ],
        scratch_shapes=[pltpu.VMEM(*s) if isinstance(s, tuple) else s for s in scratch],
        compiler_params=pltpu.CompilerParams(vmem_limit_bytes=limit * 1024 * 1024),
        cost_estimate=pl.CostEstimate(flops=flops, bytes_accessed=moved, transcendentals=0),
    )(*args)


def exchange(x, axis, groups=None):
    return lax.all_to_all(
        x, axis, split_axis=0, concat_axis=0, tiled=True, axis_index_groups=groups
    )


def both_ways(size):
    ahead = [1] + list(range(size // 2, 1, -1))
    behind = [size - 1] + list(range(size // 2 + 1, size - 1))
    order = []
    for i in range(len(ahead)):
        order += ahead[i : i + 1] + behind[i : i + 1]
    return [d for i, d in enumerate(order) if d not in order[:i]]


def far_exchange(pieces, grid_x, grid_y):
    group = [(x, y) for x in range(grid_x) for y in range(grid_y)]
    order = [0, *both_ways(grid_y)]
    got = [pieces[0]]
    for dy in order[1:]:
        pairs = [(x * grid_y + y, x * grid_y + (y + dy) % grid_y) for x, y in group]
        got.append(lax.ppermute(pieces[dy], "group", pairs))
    lines = call(
        lambda *refs: regroup_kernel(order, *refs),
        [((grid_y * 8, got[0].shape[1]), bf16)] * grid_x,
        got,
        moved=1000,
    )
    ended = [lines[0]]
    for dx in far_order(grid_x)[1:]:
        pairs = [(x * grid_y + y, (x + dx) % grid_x * grid_y + y) for x, y in group]
        ended.append(lax.ppermute(lines[dx], "group", pairs))
    return ended


def far_order(size):
    return [0, *sorted(range(1, size), key=lambda d: -min(d, size - d))]


def make_body(grid_x, grid_y):
    def body(
        query_layer_input,
        query_frozen_base,
        passage_layer_input,
        passage_frozen_base,
        adapter_down_weight,
        adapter_up_weight,
        positive_passage_index,
        hard_negative_slots,
        group_peer_rows,
        remote_group_rows,
    ):
        n_dp = lax.axis_size("dp")
        n_group = lax.axis_size("group")
        rows, width = query_layer_input.shape
        rank = adapter_up_weight.shape[0]
        part = rank // 2
        queries = rows * n_dp * n_group
        slope = 16.0 / math.sqrt(queries) / logit_divisor
        g = lax.axis_index("group")
        place = jnp.stack([g // grid_y, g % grid_y, lax.axis_index("dp") % 2]).astype(jnp.int32)
        down_t = adapter_down_weight.T
        near_ids, far_ids = group_peer_rows.T, remote_group_rows.T
        per_near = group_peer_rows.shape[1]
        n_near = n_dp * per_near
        n_far = n_group * 2
        n_other = n_far + rows
        half = width // 2
        block = width // n_group
        near, p_unit, p_ext, pick = call(
            passage_kernel,
            [
                ((n_near, width + lanes), bf16),
                ((rows, width), bf16),
                ((rows, lanes), bf16),
                ((n_near, rows), bf16),
            ],
            (passage_layer_input, passage_frozen_base, down_t, adapter_up_weight, near_ids),
            [
                ((rows, width), bf16),
                ((rows, width), bf16),
                (down_t.shape, bf16),
                (adapter_up_weight.shape, bf16),
                (near_ids.shape, jnp.int32),
                ((rows, width), f32),
                ((n_near, width + lanes), bf16),
                pltpu.SemaphoreType.DMA((5,)),
                pltpu.SemaphoreType.DMA((1 + len(column_tiles(width)),)),
            ],
            flops=300_000_000, moved=5_000_000, hbm=range(5), out_hbm=(0,), out_raw=(0,),
        )
        far = call(
            lambda *refs: far_pick_kernel(grid_x, grid_y, *refs),
            [((grid_x * 8, half + lanes), bf16)] * grid_y,
            (place, passage_layer_input, p_unit, p_ext, far_ids),
            flops=1000, moved=1000,
        )
        ring = [ring_spot(i, n_dp) for i in range(n_dp)]
        step = stride_of(grid_y)
        plane = [x * grid_y + y * step % grid_y for x in range(grid_x) for y in range(grid_y)]
        near = exchange(near.reshape(n_dp, per_near, width + lanes), "dp", [ring])
        near = near.reshape(n_near, width + lanes)
        far = far_exchange(far, grid_x, grid_y)
        q_pair, q_ext, q_inv, near_count, other_count, shadow = call(
            lambda *refs: query_kernel(grid_x, grid_y, per_near, *refs),
            [
                ((rows + rank, width), bf16),
                ((rows, lanes), bf16),
                ((rows, lanes), f32),
                ((n_near, rows), f32),
                ((n_other, rows), f32),
                ((2 * rows, rank), bf16),
            ],
            (
                place, query_layer_input, query_frozen_base, down_t, adapter_up_weight,
                hard_negative_slots.T,
            ),
            [
                ((rows, width), bf16),
                ((rows, width), bf16),
                (down_t.shape, bf16),
                (adapter_up_weight.shape, bf16),
                (hard_negative_slots.T.shape, jnp.int32),
                ((rows, width), f32),
                pltpu.SemaphoreType.DMA((5,)),
            ],
            flops=1000, moved=1000, hbm=range(1, 6), out_hbm=(1, 2, 5),
        )
        positive = positive_passage_index.reshape(1, rows)
        other, other_ext, x_far, other_both, p_inv = call(
            lambda *refs: far_kernel(grid_x, *refs),
            [
                ((n_other, width), bf16),
                ((n_other, lanes), bf16),
                ((n_far, width), bf16),
                ((n_other, rows + rank), f32),
                ((rows, lanes), f32),
            ],
            (*far, q_pair, p_unit, p_ext, positive),
            flops=1000, moved=1000, out_hbm=range(5),
        )
        ret, weights, radial, near_up = call(
            lambda *refs: score_kernel(slope, rank, *refs),
            [
                ((n_near, lanes), bf16),
                ((n_near + n_other, rows), bf16),
                ((n_near + n_other + rows, 1), f32),
                ((n_near, rank), f32),
            ],
            (near, q_pair, other_both, near_count, other_count, shadow),
            [
                ((n_other, rows + rank), f32),
                (shadow.shape, bf16),
                pltpu.SemaphoreType.DMA((2,)),
            ],
            flops=200_000_000, moved=3_000_000, hbm=(2, 5), out_hbm=(1, 2, 3),
        )
        ret = exchange(ret.reshape(n_dp, per_near, lanes), "dp", [ring]).reshape(n_near, lanes)
        up_keep, up_send, down_part, row_part = call(
            local_kernel,
            [
                ((n_group, part, block), f32),
                ((n_group, part, block), bf16),
                ((rank, width), f32),
                ((rows, lanes), f32),
            ],
            (
                place, near, q_pair, shadow, other, other_ext, x_far, q_ext, q_inv, p_inv,
                query_layer_input, positive, weights, radial, near_up, other_both,
            ),
            [
                (shadow.shape, bf16),
                ((n_other, width), bf16),
                ((n_other, lanes), bf16),
                ((n_far, width), bf16),
                ((rows, lanes), bf16),
                ((rows, lanes), f32),
                ((rows, lanes), f32),
                ((rows, width), bf16),
                ((1, rows), jnp.int32),
                (weights.shape, bf16),
                (radial.shape, f32),
                (near_up.shape, f32),
                (other_both.shape, f32),
                pltpu.SemaphoreType.DMA((13,)),
            ],
            flops=900_000_000, moved=9_000_000, hbm=range(3, 16), out_hbm=range(4),
        )
        swap = [(i, i ^ 1) for i in range(n_dp)]
        keep, send, loss = call(
            lambda *refs: down_kernel(per_near, *refs),
            [
                ((n_group, rank, block), f32),
                ((n_group, rank, block), bf16),
                ((8, lanes), f32),
            ],
            (place, ret, pick, row_part, passage_layer_input, down_part, up_keep, up_send),
            [((rows, lanes), f32), ((rank, width), f32), pltpu.SemaphoreType.DMA((4,))],
            flops=100_000_000, moved=3_000_000, hbm=(3, 5, 6, 7),
        )
        got = lax.ppermute(send, "dp", swap)
        (sums,) = call(add_kernel, [((n_group, rank, block), bf16)], (keep, got), moved=2_500_000)
        cores = [ring[c::2] for c in range(2)]
        sums = exchange(sums, "group", [plane])
        (sums,) = call(
            spread_kernel, [((n_dp // 2, rank, block), bf16)], (sums,), moved=1_000_000
        )
        sums = exchange(sums, "dp", cores)
        (sums,) = call(
            finish_kernel, [((n_group, rank + 8, block), bf16)], (sums, loss), moved=1_000_000
        )
        sums = exchange(sums, "group", [plane])
        other_sums = lax.ppermute(sums, "dp", swap)
        down, up, loss = call(
            lambda *refs: output_kernel(queries, *refs),
            [((rank, width), f32), ((rank, width), f32), ((1, 1), f32)],
            (place, sums, other_sums),
            moved=3_500_000,
        )
        return (down.T, up, loss.reshape(()))

    return body


def solution(mesh):
    n_group = mesh.shape["group"]
    grid_x = {32: 4, 4: 2}[n_group]
    both = P(("dp", "group"), None)
    placed = (both, both, both, both, P(), P(), P(("dp", "group")), both, both, both)
    return jax.shard_map(
        make_body(grid_x, n_group // grid_x),
        mesh=mesh,
        in_specs=placed,
        out_specs=(P(), P(), P()),
        check_vma=False,
    )
```

```python
import math

import jax
import jax.numpy as jnp
from jax import lax
from jax.experimental import pallas as pl
from jax.experimental.pallas import tpu as pltpu
from jax.sharding import PartitionSpec as P

f32 = jnp.float32
bf16 = jnp.bfloat16
adapter_scale = 2.0
logit_divisor = 0.05
epsilon = 1e-06
offset = 1.0 / logit_divisor
tile = 512
lanes = 128


def dot(a, b, ca=1, cb=0):
    return lax.dot_general(a, b, (((ca,), (cb,)), ((), ())), preferred_element_type=f32)


def iota(shape, dim):
    return lax.broadcasted_iota(jnp.int32, shape, dim)


def eye(n, m):
    return (iota((n, m), 0) == iota((n, m), 1)).astype(bf16)


def flip(a):
    return dot(eye(a.shape[1], a.shape[1]), a, 1, 1).astype(bf16)


def column_tiles(width):
    step = min(tile, width)
    return [slice(c, c + step) for c in range(0, width, step)]


def embed(x_ref, base_ref, down_ref, up_ref, unit_ref, ext_ref, inv_ref, raw_ref, ready=None):
    rows, width = x_ref.shape
    rank = up_ref.shape[0]
    latent = dot(x_ref[...], down_ref[...], 1, 1).astype(bf16)
    if ready is not None:
        ready()
    squares = jnp.zeros((rows, 1), f32)
    for cols in column_tiles(width):
        raw = base_ref[:, cols].astype(f32) + adapter_scale * dot(latent, up_ref[:, cols])
        raw_ref[:, cols] = raw
        squares = squares + jnp.sum(raw * raw, axis=1, keepdims=True)
    inverse = lax.rsqrt(squares + epsilon)
    for cols in column_tiles(width):
        unit_ref[0:rows, cols] = (raw_ref[:, cols] * inverse).astype(bf16)
    scaled = (latent.astype(f32) * inverse).astype(bf16)
    high = inverse.astype(bf16).astype(f32)
    lane = iota((rows, lanes), 1)
    ext = dot(scaled, eye(rank, lanes))
    ext = jnp.where(lane == rank, high, ext)
    ext = jnp.where(lane == rank + 1, inverse - high, ext)
    ext_ref[...] = ext.astype(bf16)
    if inv_ref is not None:
        inv_ref[...] = jnp.broadcast_to(inverse, inv_ref.shape)


def fetch(pairs, sems):
    copies = [pltpu.make_async_copy(a, b, sems.at[i]) for i, (a, b) in enumerate(pairs)]
    for c in copies:
        c.start()
    return copies


def stride_of(chips):
    return {12: 5, 8: 3, 3: 2}.get(chips, 1)


def ring_spot(position, n_dp):
    chips = n_dp // 2
    return (position // 2 * stride_of(chips)) % chips * 2 + position % 2


def passage_kernel(
    x_hbm, base_hbm, down_hbm, up_hbm, near_ids_hbm,
    near_hbm, unit_ref, ext_ref, pick_ref,
    x_ref, base_ref, down_ref, up_ref, near_ids_ref, raw_ref, near_ref, sems, out_sems,
):
    pairs = [
        (near_ids_hbm, near_ids_ref), (x_hbm, x_ref), (down_hbm, down_ref), (base_hbm, base_ref),
        (up_hbm, up_ref),
    ]
    copies = fetch(pairs, sems)
    copies[0].wait()
    rows, width = x_ref.shape
    per_near, n_near = near_ids_ref.shape
    count = per_near * n_near
    ids = near_ids_ref[...].astype(f32).astype(bf16)
    spot = ring_spot(iota((count, n_near), 0) // per_near, n_near)
    spread = (spot == iota((count, n_near), 1)).astype(bf16)
    table = dot(spread, ids, 1, 1)
    mine = iota((count, per_near), 0) % per_near == iota((count, per_near), 1)
    wanted = jnp.sum(jnp.where(mine, table, 0.0), axis=1, keepdims=True).astype(jnp.int32)
    pick = (iota((count, rows), 1) == wanted).astype(bf16)
    pick_ref[...] = pick
    copies[1].wait()
    copies[2].wait()

    def ready():
        copies[3].wait()
        copies[4].wait()

    embed(x_ref, base_ref, down_ref, up_ref, unit_ref, ext_ref, None, raw_ref, ready)
    near_ref[:, width:] = dot(pick, ext_ref[...]).astype(bf16)
    sent = []
    for i, cols in enumerate([slice(width, width + lanes), *column_tiles(width)]):
        if i:
            near_ref[:, cols] = dot(pick, unit_ref[:, cols]).astype(bf16)
        copy = pltpu.make_async_copy(near_ref.at[:, cols], near_hbm.at[:, cols], out_sems.at[i])
        copy.start()
        sent.append(copy)
    for copy in sent:
        copy.wait()


def far_pick_kernel(grid_x, grid_y, place_ref, x_ref, unit_ref, ext_ref, far_ids_ref, *far_refs):
    rows, width = x_ref.shape
    half = width // 2
    n_far = far_ids_ref.shape[1]
    total = n_far * 8
    size = grid_x * 8
    where_x, where_y = place_ref[0], place_ref[1]
    ids = far_ids_ref[...].astype(f32).astype(bf16)
    block = iota((total, n_far), 0) // 8
    to_x = (where_x + block % grid_x) % grid_x
    to_y = (where_y + block // grid_x) % grid_y
    spread = (to_x * grid_y + to_y == iota((total, n_far), 1)).astype(bf16)
    table = dot(spread, ids, 1, 1)
    mine = iota((total, 2), 0) % 2 == iota((total, 2), 1)
    wanted = jnp.sum(jnp.where(mine, table, 0.0), axis=1, keepdims=True).astype(jnp.int32)
    kind = (iota((total, 4 * rows), 0) // 2) % 4
    source = iota((total, 4 * rows), 1)
    choose = ((source // rows == kind) & (source % rows == wanted)).astype(bf16)
    for cols in column_tiles(half):
        later = slice(half + cols.start, half + cols.stop)
        stack = jnp.concatenate(
            [unit_ref[:, cols], unit_ref[:, later], x_ref[:, cols], x_ref[:, later]], axis=0
        )
        got = dot(choose, stack).astype(bf16)
        for dy in range(grid_y):
            far_refs[dy][:, cols] = got[dy * size : (dy + 1) * size]
    first = jnp.where(iota((total, rows), 0) // 2 % 4 == 0, wanted, -1)
    got = dot((iota((total, rows), 1) == first).astype(bf16), ext_ref[...]).astype(bf16)
    for dy in range(grid_y):
        far_refs[dy][:, half:] = got[dy * size : (dy + 1) * size]


def query_kernel(
    grid_x, grid_y, per_near, place_ref, x_hbm, base_hbm, down_hbm, up_hbm, slots_hbm,
    pair_ref, ext_ref, inv_ref, near_count_ref, other_count_ref, shadow_ref,
    x_ref, base_ref, down_ref, up_ref, slots_ref, raw_ref, sems,
):
    pairs = [
        (x_hbm, x_ref), (down_hbm, down_ref), (base_hbm, base_ref), (up_hbm, up_ref),
        (slots_hbm, slots_ref),
    ]
    for c in fetch(pairs, sems):
        c.wait()
    hard, rows = slots_ref.shape
    embed(x_ref, base_ref, down_ref, up_ref, pair_ref, ext_ref, inv_ref, raw_ref)
    pair_ref[rows:, :] = up_ref[...]
    product = dot(pair_ref[0:rows, :], up_ref[...], 1, 1)
    high = product.astype(bf16)
    shadow_ref[0:rows, :] = high
    shadow_ref[rows:, :] = (product - high.astype(f32)).astype(bf16)
    n_near = near_count_ref.shape[0]
    n_other = other_count_ref.shape[0]
    n_far = n_other - rows
    where_x, where_y = place_ref[0], place_ref[1]
    near_slot = iota((n_near, rows), 0)
    near_slot = ring_spot(near_slot // per_near, n_near // per_near) * per_near + near_slot % per_near
    spot = iota((n_other, rows), 0)
    block = spot // 2
    from_x = (where_x + grid_x - (block // grid_y) % grid_x) % grid_x
    from_y = (where_y + grid_y - block % grid_y) % grid_y
    far_slot = n_near + (from_x * grid_y + from_y) * 2 + spot % 2
    far_slot = jnp.where(spot < n_far, far_slot, -1)
    near_count = jnp.zeros((n_near, rows), f32)
    other_count = jnp.zeros((n_other, rows), f32)
    for k in range(hard):
        slot = slots_ref[k : k + 1, :]
        near_count = near_count + (near_slot == slot).astype(f32)
        other_count = other_count + (far_slot == slot).astype(f32)
    near_count_ref[...] = near_count
    other_count_ref[...] = jnp.where(spot < n_far, other_count, 1.0)


def store_blocks(ref, cols, value):
    size = ref.shape[2]
    step = min(size, cols.stop - cols.start)
    for c in range(cols.start, cols.stop, step):
        at = c % size
        block = value[:, c - cols.start : c - cols.start + step]
        ref[c // size, 0 : value.shape[0], at : at + step] = block


def regroup_kernel(order, *refs):
    size = 8
    count = refs[0].shape[0] // size
    n_in = len(order)
    refs = [refs[order.index(dy)] for dy in range(n_in)] + list(refs[n_in:])
    for dx in range(0, count, 2):
        for dy in range(0, n_in, 2):
            a, b = [refs[dy + i][dx * size : (dx + 2) * size, :] for i in range(2)]
            at = slice(dy * size, (dy + 2) * size)
            refs[n_in + dx][at, :] = jnp.concatenate([a[:size], b[:size]], axis=0)
            refs[n_in + dx + 1][at, :] = jnp.concatenate([a[size:], b[size:]], axis=0)


def far_kernel(count, *refs):
    order = far_order(count)
    far_refs = [refs[order.index(dx)] for dx in range(count)]
    pair_ref, unit_ref, p_ext_ref, positive_ref = refs[count : count + 4]
    o_ref, ext_ref, x_far_ref, both_ref, p_inv_ref = refs[count + 4 :]
    rows, width = unit_ref.shape
    half = width // 2
    total = far_refs[0].shape[0]
    each = total // 4
    n_far = each * count
    out_row = iota((total, total), 0)
    in_row = iota((total, total), 1)
    spot = out_row % each
    undo = (
        (in_row // 8 == spot // 2)
        & (in_row % 2 == spot % 2)
        & ((in_row // 2) % 4 == out_row // each)
    ).astype(bf16)
    for i, far_ref in enumerate(far_refs):
        at = slice(i * each, (i + 1) * each)
        for cols in column_tiles(half):
            later = slice(half + cols.start, half + cols.stop)
            got = dot(undo, far_ref[:, cols]).astype(bf16)
            o_ref[at, cols] = got[0:each]
            o_ref[at, later] = got[each : 2 * each]
            x_far_ref[at, cols] = got[2 * each : 3 * each]
            x_far_ref[at, later] = got[3 * each :]
        ext_ref[at, :] = dot(undo[0:each], far_ref[:, half:]).astype(bf16)
    own = (iota((rows, rows), 0) == positive_ref[...]).astype(bf16)
    own_t = flip(own)
    for cols in column_tiles(width):
        o_ref[n_far:, cols] = dot(own_t, unit_ref[:, cols]).astype(bf16)
    ext_ref[n_far:, :] = dot(own_t, p_ext_ref[...]).astype(bf16)
    both_ref[...] = dot(o_ref[...], pair_ref[...], 1, 1)
    rank = pair_ref.shape[0] - rows
    ext = p_ext_ref[...].astype(f32)
    inverse = ext[:, rank : rank + 1] + ext[:, rank + 1 : rank + 2]
    p_inv_ref[...] = jnp.broadcast_to(inverse, p_inv_ref.shape)


def score_kernel(
    slope, rank, near_ref, pair_ref, other_both_hbm, near_count_ref, other_count_ref, shadow_hbm,
    ret_ref, g_hbm, radial_hbm, near_up_hbm, other_both_ref, shadow_ref, g_ref, radial_ref,
    near_up_ref, sems,
):
    outs = [(near_up_ref, near_up_hbm), (g_ref, g_hbm), (radial_ref, radial_hbm)]
    sent = [pltpu.make_async_copy(a, b, sems.at[2 + i]) for i, (a, b) in enumerate(outs)]
    copies = fetch([(other_both_hbm, other_both_ref), (shadow_hbm, shadow_ref)], sems)
    width = pair_ref.shape[1]
    n_near, rows = near_count_ref.shape
    both = dot(near_ref[:, :width], pair_ref[...], 1, 1)
    near_raw, near_up = both[:, 0:rows], both[:, rows:]
    near_up_ref[...] = near_up
    sent[0].start()
    for c in copies:
        c.wait()
    other_raw = other_both_ref[:, 0:rows]
    n_other = other_raw.shape[0]
    n_far = n_other - rows
    near_exp = jnp.exp(near_raw / logit_divisor - offset) * near_count_ref[...]
    other_exp = jnp.exp(other_raw / logit_divisor - offset) * other_count_ref[...]
    partition = jnp.sum(near_exp, axis=0, keepdims=True) + jnp.sum(
        other_exp, axis=0, keepdims=True
    )
    same = iota(other_raw.shape, 0) == iota(other_raw.shape, 1) + n_far
    matched = jnp.sum(jnp.where(same, other_raw, 0.0), axis=0, keepdims=True) / logit_divisor
    loss = jnp.sum(jnp.log(partition) + offset - matched, axis=1, keepdims=True)
    near_g = (near_exp / partition * slope).astype(bf16)
    other_g = ((other_exp / partition - same.astype(f32)) * slope).astype(bf16)
    g_ref[0:n_near, :] = near_g
    g_ref[n_near:, :] = other_g
    sent[1].start()
    near_part = near_g.astype(f32) * near_raw
    other_part = other_g.astype(f32) * other_raw
    near_radial = jnp.sum(near_part, axis=1, keepdims=True)
    radial_ref[0:n_near, :] = near_radial
    radial_ref[n_near : n_near + n_other, :] = jnp.sum(other_part, axis=1, keepdims=True)
    q_radial = jnp.sum(near_part, axis=0, keepdims=True) + jnp.sum(
        other_part, axis=0, keepdims=True
    )
    square = iota((rows, rows), 0) == iota((rows, rows), 1)
    radial_ref[n_near + n_other :, :] = jnp.sum(
        jnp.where(square, q_radial, 0.0), axis=1, keepdims=True
    )
    sent[2].start()
    back = dot(near_g, shadow_ref[0:rows, :]) + dot(near_g, shadow_ref[rows:, :])
    back = back - near_radial * near_up
    back = dot(back.astype(bf16), eye(rank, lanes))
    lane = iota((n_near, lanes), 1)
    high = loss.astype(bf16).astype(f32)
    back = jnp.where(lane == rank, high, back)
    back = jnp.where(lane == rank + 1, loss - high, back)
    ret_ref[...] = back.astype(bf16)
    for c in sent:
        c.wait()


def halves(value):
    high = value.astype(bf16)
    return high, (value - high.astype(f32)).astype(bf16)


def wide_dot(a, value):
    high, low = halves(value)
    return dot(a, high) + dot(a, low)


def local_kernel(
    place_ref, near_ref, pair_ref, shadow_hbm, o_hbm, o_ext_hbm, x_far_hbm, q_ext_hbm, q_inv_hbm,
    p_inv_hbm, x_q_hbm, positive_hbm, g_hbm, radial_hbm, near_up_hbm, other_both_hbm,
    up_keep_ref, up_send_ref, down_ref, row_ref,
    shadow_ref, o_ref, o_ext_ref, x_far_ref, q_ext_ref, q_inv_ref, p_inv_ref, x_q_ref,
    positive_ref, g_ref, radial_ref, near_up_ref, other_both_ref, sems,
):
    pairs = [
        (g_hbm, g_ref), (radial_hbm, radial_ref), (q_ext_hbm, q_ext_ref), (o_ext_hbm, o_ext_ref),
        (o_hbm, o_ref), (positive_hbm, positive_ref), (q_inv_hbm, q_inv_ref), (p_inv_hbm, p_inv_ref),
        (shadow_hbm, shadow_ref), (near_up_hbm, near_up_ref), (other_both_hbm, other_both_ref),
        (x_far_hbm, x_far_ref), (x_q_hbm, x_q_ref),
    ]
    copies = fetch(pairs, sems)
    for c in copies[:4]:
        c.wait()
    rows, width = x_q_ref.shape
    rank = pair_ref.shape[0] - rows
    part = rank // 2
    n_near = near_ref.shape[0]
    n_far = o_ref.shape[0] - rows
    n_all = n_near + n_far + rows
    even = place_ref[2] == 0
    near_gt, other_gt = g_ref[0:n_near, :], g_ref[n_near:, :]
    near_g, other_g = flip(near_gt), flip(other_gt)
    near_radial = radial_ref[0:n_near, :]
    other_radial = radial_ref[n_near:n_all, :]
    q_radial = radial_ref[n_all:, :]
    q_ext, near_ext, o_ext = q_ext_ref[...], near_ref[:, width:], o_ext_ref[...]

    def spread(value):
        high, low = halves(value)
        return jnp.concatenate([flip(high)[0:rank], flip(low)[0:rank]], axis=0)

    near_a = spread(dot(near_gt, q_ext) - near_ext.astype(f32) * near_radial)
    other_a = spread(dot(other_gt, q_ext) - o_ext.astype(f32) * other_radial)
    q_a = spread(dot(near_g, near_ext) + dot(other_g, o_ext) - q_ext.astype(f32) * q_radial)
    all_a = jnp.concatenate([near_a, other_a, q_a], axis=1)
    copies[4].wait()
    for cols in column_tiles(width):
        stack = [near_ref[:, cols], o_ref[:, cols], pair_ref[0:rows, cols]]
        grad = dot(all_a, jnp.concatenate(stack, axis=0))
        grad = adapter_scale * (grad[0:rank] + grad[rank:])
        top, low = grad[0:part], grad[part:]
        store_blocks(up_keep_ref, cols, jnp.where(even, top, low))
        store_blocks(up_send_ref, cols, jnp.where(even, low, top).astype(bf16))
    for c in copies[5:]:
        c.wait()
    other_up = other_both_ref[:, rows:]
    q_back = wide_dot(near_g, near_up_ref[...]) + wide_dot(other_g, other_up)
    q_up = shadow_ref[0:rows, :].astype(f32) + shadow_ref[rows:, :].astype(f32)
    q_back = (q_back - q_up * q_radial).astype(bf16).astype(f32)
    other_back = dot(other_gt, shadow_ref[0:rows, :]) + dot(other_gt, shadow_ref[rows:, :])
    other_back = (other_back - other_up * other_radial).astype(bf16)
    own = (iota((rows, rows), 0) == positive_ref[...]).astype(bf16)
    wide = dot(other_back[n_far:], eye(rank, lanes)).astype(bf16)
    row_sum = dot(own, wide)
    row_ref[...] = jnp.where(iota(row_sum.shape, 1) < rank, row_sum, p_inv_ref[...])
    dz_q = (adapter_scale * q_inv_ref[:, 0:1] * q_back).astype(bf16)
    far_ext = o_ext[0:n_far, :].astype(f32)
    far_inv = far_ext[:, rank : rank + 1] + far_ext[:, rank + 1 : rank + 2]
    dz_f = (adapter_scale * far_inv * other_back[0:n_far].astype(f32)).astype(bf16)
    dz_t = flip(jnp.concatenate([dz_q, dz_f], axis=0))
    for cols in column_tiles(width):
        stack = jnp.concatenate([x_q_ref[:, cols], x_far_ref[:, cols]], axis=0)
        down_ref[:, cols] = dot(dz_t, stack)


def down_kernel(
    per_near, place_ref, ret_ref, pick_ref, row_hbm, x_p_ref, down_hbm, up_keep_hbm, up_send_hbm,
    keep_ref, send_ref, loss_ref, row_ref, down_ref, sems,
):
    rank = down_ref.shape[0]
    part = rank // 2
    pairs = [
        (row_hbm, row_ref), (down_hbm, down_ref),
        (up_send_hbm, send_ref.at[:, part:]), (up_keep_hbm, keep_ref.at[:, part:]),
    ]
    copies = fetch(pairs, sems)
    ret = ret_ref[...]
    row_sum = dot(flip(pick_ref[...]), ret)[:, 0:rank]
    copies[0].wait()
    row_sum = row_sum + row_ref[:, 0:rank]
    dz_t = flip((adapter_scale * row_ref[:, rank : rank + 1] * row_sum).astype(bf16))
    copies[1].wait()
    even = place_ref[2] == 0
    for cols in column_tiles(x_p_ref.shape[1]):
        grad = dot(dz_t, x_p_ref[:, cols]) + down_ref[:, cols]
        top, low = grad[0:part], grad[part:]
        store_blocks(keep_ref, cols, jnp.where(even, top, low))
        store_blocks(send_ref, cols, jnp.where(even, low, top).astype(bf16))
    first = iota(ret.shape, 0) % per_near == 0
    lane = iota(ret.shape, 1)
    chosen = first & ((lane == rank) | (lane == rank + 1))
    share = jnp.sum(jnp.where(chosen, ret.astype(f32), 0.0), axis=1, keepdims=True)
    loss_ref[...] = jnp.broadcast_to(jnp.sum(share, axis=0, keepdims=True), loss_ref.shape)
    copies[2].wait()
    copies[3].wait()


def add_kernel(keep_ref, got_ref, out_ref):
    for i in range(keep_ref.shape[0]):
        out_ref[i] = (keep_ref[i] + got_ref[i].astype(f32)).astype(bf16)


def sum_blocks(ref, *at):
    acc = ref[(0, *at)].astype(f32)
    for i in range(1, ref.shape[0]):
        acc = acc + ref[(i, *at)].astype(f32)
    return acc


def spread_kernel(in_ref, out_ref):
    value = sum_blocks(in_ref).astype(bf16)
    for i in range(out_ref.shape[0]):
        out_ref[i] = value


def finish_kernel(in_ref, loss_ref, out_ref):
    loss = loss_ref[...]
    high = loss.astype(bf16).astype(f32)
    row = iota(loss.shape, 0)
    tail = jnp.where(row == 0, high, jnp.where(row == 1, loss - high, 0.0))
    if out_ref.shape[2] > lanes:
        tail = jnp.concatenate([tail] * (out_ref.shape[2] // lanes), axis=1)
    value = jnp.concatenate([sum_blocks(in_ref), tail], axis=0).astype(bf16)
    for i in range(out_ref.shape[0]):
        out_ref[i] = value


def output_kernel(queries, place_ref, mine_ref, other_ref, down_ref, up_ref, loss_ref):
    rank = down_ref.shape[0]
    part = rank // 2
    size = mine_ref.shape[2]
    even = place_ref[2] == 0
    loss = jnp.zeros((8, lanes), f32)
    for i in range(mine_ref.shape[0]):
        mine, other = mine_ref[i].astype(f32), other_ref[i].astype(f32)
        cols = slice(i * size, (i + 1) * size)
        top = jnp.where(even, mine[0:rank], other[0:rank])
        low = jnp.where(even, other[0:rank], mine[0:rank])
        down_ref[0:part, cols] = top[0:part]
        down_ref[part:, cols] = low[0:part]
        up_ref[0:part, cols] = top[part:]
        up_ref[part:, cols] = low[part:]
        loss = loss + mine[rank:, 0:lanes]
    loss_ref[...] = jnp.sum(loss, axis=0, keepdims=True)[:, 0:1] / queries


def call(kernel, outs, args, scratch=(), flops=0, moved=0, hbm=(), out_hbm=(), out_raw=(), limit=16):
    specs = []
    for i, a in enumerate(args):
        space = pltpu.SMEM if a.dtype == jnp.int32 and a.ndim == 1 else pltpu.VMEM
        specs.append(pl.BlockSpec(memory_space=pltpu.HBM if i in hbm else space))
    args = [
        pltpu.with_memory_space_constraint(a, pltpu.HBM) if i in hbm else a
        for i, a in enumerate(args)
    ]
    shapes = [
        pltpu.HBM(s, d) if i in out_hbm else jax.ShapeDtypeStruct(s, d)
        for i, (s, d) in enumerate(outs)
    ]
    return pl.pallas_call(
        kernel,
        out_shape=shapes,
        in_specs=specs,
        out_specs=[
            pl.BlockSpec(memory_space=pltpu.HBM if i in out_raw else pltpu.VMEM)
            for i in range(len(shapes))
        ],
        scratch_shapes=[pltpu.VMEM(*s) if isinstance(s, tuple) else s for s in scratch],
        compiler_params=pltpu.CompilerParams(vmem_limit_bytes=limit * 1024 * 1024),
        cost_estimate=pl.CostEstimate(flops=flops, bytes_accessed=moved, transcendentals=0),
    )(*args)


def exchange(x, axis, groups=None):
    return lax.all_to_all(
        x, axis, split_axis=0, concat_axis=0, tiled=True, axis_index_groups=groups
    )


def both_ways(size):
    ahead = [1] + list(range(size // 2, 1, -1))
    behind = [size - 1] + list(range(size // 2 + 1, size - 1))
    order = []
    for i in range(len(ahead)):
        order += ahead[i : i + 1] + behind[i : i + 1]
    return [d for i, d in enumerate(order) if d not in order[:i]]


def far_exchange(pieces, grid_x, grid_y):
    group = [(x, y) for x in range(grid_x) for y in range(grid_y)]
    order = [0, *both_ways(grid_y)]
    got = [pieces[0]]
    for dy in order[1:]:
        pairs = [(x * grid_y + y, x * grid_y + (y + dy) % grid_y) for x, y in group]
        got.append(lax.ppermute(pieces[dy], "group", pairs))
    lines = call(
        lambda *refs: regroup_kernel(order, *refs),
        [((grid_y * 8, got[0].shape[1]), bf16)] * grid_x,
        got,
        moved=1000,
    )
    ended = [lines[0]]
    for dx in far_order(grid_x)[1:]:
        pairs = [(x * grid_y + y, (x + dx) % grid_x * grid_y + y) for x, y in group]
        ended.append(lax.ppermute(lines[dx], "group", pairs))
    return ended


def far_order(size):
    return [0, *sorted(range(1, size), key=lambda d: -min(d, size - d))]


def make_body(grid_x, grid_y):
    def body(
        query_layer_input,
        query_frozen_base,
        passage_layer_input,
        passage_frozen_base,
        adapter_down_weight,
        adapter_up_weight,
        positive_passage_index,
        hard_negative_slots,
        group_peer_rows,
        remote_group_rows,
    ):
        n_dp = lax.axis_size("dp")
        n_group = lax.axis_size("group")
        rows, width = query_layer_input.shape
        rank = adapter_up_weight.shape[0]
        part = rank // 2
        queries = rows * n_dp * n_group
        slope = 16.0 / math.sqrt(queries) / logit_divisor
        g = lax.axis_index("group")
        place = jnp.stack([g // grid_y, g % grid_y, lax.axis_index("dp") % 2]).astype(jnp.int32)
        down_t = adapter_down_weight.T
        near_ids, far_ids = group_peer_rows.T, remote_group_rows.T
        per_near = group_peer_rows.shape[1]
        n_near = n_dp * per_near
        n_far = n_group * 2
        n_other = n_far + rows
        half = width // 2
        block = width // n_group
        near, p_unit, p_ext, pick = call(
            passage_kernel,
            [
                ((n_near, width + lanes), bf16),
                ((rows, width), bf16),
                ((rows, lanes), bf16),
                ((n_near, rows), bf16),
            ],
            (passage_layer_input, passage_frozen_base, down_t, adapter_up_weight, near_ids),
            [
                ((rows, width), bf16),
                ((rows, width), bf16),
                (down_t.shape, bf16),
                (adapter_up_weight.shape, bf16),
                (near_ids.shape, jnp.int32),
                ((rows, width), f32),
                ((n_near, width + lanes), bf16),
                pltpu.SemaphoreType.DMA((5,)),
                pltpu.SemaphoreType.DMA((1 + len(column_tiles(width)),)),
            ],
            flops=300_000_000, moved=5_000_000, hbm=range(5), out_hbm=(0,), out_raw=(0,),
        )
        far = call(
            lambda *refs: far_pick_kernel(grid_x, grid_y, *refs),
            [((grid_x * 8, half + lanes), bf16)] * grid_y,
            (place, passage_layer_input, p_unit, p_ext, far_ids),
            flops=1000, moved=1000,
        )
        ring = [ring_spot(i, n_dp) for i in range(n_dp)]
        step = stride_of(grid_y)
        plane = [x * grid_y + y * step % grid_y for x in range(grid_x) for y in range(grid_y)]
        near = exchange(near.reshape(n_dp, per_near, width + lanes), "dp", [ring])
        near = near.reshape(n_near, width + lanes)
        far = far_exchange(far, grid_x, grid_y)
        q_pair, q_ext, q_inv, near_count, other_count, shadow = call(
            lambda *refs: query_kernel(grid_x, grid_y, per_near, *refs),
            [
                ((rows + rank, width), bf16),
                ((rows, lanes), bf16),
                ((rows, lanes), f32),
                ((n_near, rows), f32),
                ((n_other, rows), f32),
                ((2 * rows, rank), bf16),
            ],
            (
                place, query_layer_input, query_frozen_base, down_t, adapter_up_weight,
                hard_negative_slots.T,
            ),
            [
                ((rows, width), bf16),
                ((rows, width), bf16),
                (down_t.shape, bf16),
                (adapter_up_weight.shape, bf16),
                (hard_negative_slots.T.shape, jnp.int32),
                ((rows, width), f32),
                pltpu.SemaphoreType.DMA((5,)),
            ],
            flops=1000, moved=1000, hbm=range(1, 6), out_hbm=(1, 2, 5),
        )
        positive = positive_passage_index.reshape(1, rows)
        other, other_ext, x_far, other_both, p_inv = call(
            lambda *refs: far_kernel(grid_x, *refs),
            [
                ((n_other, width), bf16),
                ((n_other, lanes), bf16),
                ((n_far, width), bf16),
                ((n_other, rows + rank), f32),
                ((rows, lanes), f32),
            ],
            (*far, q_pair, p_unit, p_ext, positive),
            flops=1000, moved=1000, out_hbm=range(5),
        )
        ret, weights, radial, near_up = call(
            lambda *refs: score_kernel(slope, rank, *refs),
            [
                ((n_near, lanes), bf16),
                ((n_near + n_other, rows), bf16),
                ((n_near + n_other + rows, 1), f32),
                ((n_near, rank), f32),
            ],
            (near, q_pair, other_both, near_count, other_count, shadow),
            [
                ((n_other, rows + rank), f32),
                (shadow.shape, bf16),
                ((n_near + n_other, rows), bf16),
                ((n_near + n_other + rows, 1), f32),
                ((n_near, rank), f32),
                pltpu.SemaphoreType.DMA((5,)),
            ],
            flops=200_000_000, moved=3_000_000, hbm=(2, 5), out_hbm=(1, 2, 3), out_raw=(1, 2, 3),
        )
        ret = exchange(ret.reshape(n_dp, per_near, lanes), "dp", [ring]).reshape(n_near, lanes)
        up_keep, up_send, down_part, row_part = call(
            local_kernel,
            [
                ((n_group, part, block), f32),
                ((n_group, part, block), bf16),
                ((rank, width), f32),
                ((rows, lanes), f32),
            ],
            (
                place, near, q_pair, shadow, other, other_ext, x_far, q_ext, q_inv, p_inv,
                query_layer_input, positive, weights, radial, near_up, other_both,
            ),
            [
                (shadow.shape, bf16),
                ((n_other, width), bf16),
                ((n_other, lanes), bf16),
                ((n_far, width), bf16),
                ((rows, lanes), bf16),
                ((rows, lanes), f32),
                ((rows, lanes), f32),
                ((rows, width), bf16),
                ((1, rows), jnp.int32),
                (weights.shape, bf16),
                (radial.shape, f32),
                (near_up.shape, f32),
                (other_both.shape, f32),
                pltpu.SemaphoreType.DMA((13,)),
            ],
            flops=900_000_000, moved=9_000_000, hbm=range(3, 16), out_hbm=range(4),
        )
        swap = [(i, i ^ 1) for i in range(n_dp)]
        keep, send, loss = call(
            lambda *refs: down_kernel(per_near, *refs),
            [
                ((n_group, rank, block), f32),
                ((n_group, rank, block), bf16),
                ((8, lanes), f32),
            ],
            (place, ret, pick, row_part, passage_layer_input, down_part, up_keep, up_send),
            [((rows, lanes), f32), ((rank, width), f32), pltpu.SemaphoreType.DMA((4,))],
            flops=100_000_000, moved=3_000_000, hbm=(3, 5, 6, 7),
        )
        got = lax.ppermute(send, "dp", swap)
        (sums,) = call(add_kernel, [((n_group, rank, block), bf16)], (keep, got), moved=2_500_000)
        cores = [ring[c::2] for c in range(2)]
        sums = exchange(sums, "group", [plane])
        (sums,) = call(
            spread_kernel, [((n_dp // 2, rank, block), bf16)], (sums,), moved=1_000_000
        )
        sums = exchange(sums, "dp", cores)
        (sums,) = call(
            finish_kernel, [((n_group, rank + 8, block), bf16)], (sums, loss), moved=1_000_000
        )
        sums = exchange(sums, "group", [plane])
        other_sums = lax.ppermute(sums, "dp", swap)
        down, up, loss = call(
            lambda *refs: output_kernel(queries, *refs),
            [((rank, width), f32), ((rank, width), f32), ((1, 1), f32)],
            (place, sums, other_sums),
            moved=3_500_000,
        )
        return (down.T, up, loss.reshape(()))

    return body


def solution(mesh):
    n_group = mesh.shape["group"]
    grid_x = {32: 4, 4: 2}[n_group]
    both = P(("dp", "group"), None)
    placed = (both, both, both, both, P(), P(), P(("dp", "group")), both, both, both)
    return jax.shard_map(
        make_body(grid_x, n_group // grid_x),
        mesh=mesh,
        in_specs=placed,
        out_specs=(P(), P(), P()),
        check_vma=False,
    )
```
